128 devices in a mesh: frame: 4 (over z_lo, core), space: 32 (over x, z_hi, y).
Axes of the slice: x: 4, y: 4, z: 4 (z_hi: 2, z_lo: 2; z = z_hi * 2 + z_lo), core: 2. Of those that a mesh axis runs over, the one named last changes fastest.
Arguments:
- frames: bfloat16 [4, 128, 640, 512], P('frame', 'space'), may hold values from -24 to 24
- cotangent: bfloat16 [4, 128, 640, 512], P('frame', 'space'), may hold values from -20 to 20
- layer_norm_gain: float32 [512], replicated, may hold values from 0.1 to 1.9
- w_in: bfloat16 [512, 1024], replicated, may hold values from -0.25 to 0.25
- kernel: bfloat16 [9, 1024], replicated, may hold values from -2 to 2
- w_att: float32 [512, 512], replicated, may hold values from -0.25 to 0.25
- w_out: bfloat16 [512, 512], replicated, may hold values from -0.25 to 0.25
Outputs:
- grad_frames: bfloat16 [4, 128, 640, 512], P('frame', 'space')
- grad_in: float32 [512, 1024], replicated
- grad_kernel: float32 [9, 1024], replicated
- grad_att: float32 [512, 512], replicated
- grad_out: float32 [512, 512], replicated
The draws below stay inside these ranges and needn't reach their ends.
All inputs are finite; a program needn't handle non-finite values.
Results may differ from the reference program's by a relative error of at most 0.014.
Values may be sent and summed in bfloat16 or wider, within the bound.
No kernel may reach another device: no remote copies, remote signals or barrier semaphores. Data moves between devices by JAX's collectives and lax.ppermute only.
A program may use at most 128 MiB of HBM per device.

```python
import math
import jax
import jax.numpy as jnp
from jax import lax

C = 512
HID = 1024
COLS = 640
FRAMES = 4
ROWS = 128


def draw_frames(key, part):
    key = jax.random.fold_in(key, 11)
    first, second, third = jax.random.split(key, 3)
    shape = (FRAMES, ROWS, COLS, C)
    rows = lax.broadcasted_iota(jnp.float32, (FRAMES, ROWS, COLS, 1), 1)
    rise = 0.5 + rows / ROWS
    direction = jnp.clip(jax.random.normal(second, (C,), jnp.float32), -4.0, 4.0)
    noise = jnp.clip(jax.random.normal(first, shape, jnp.float32), -4.0, 4.0)
    rough = jax.random.uniform(third, (FRAMES, ROWS, COLS, 1), jnp.float32, 0.5, 1.5)
    base = rise
    return (noise * rough + base * direction).astype(jnp.bfloat16)


def draw_cotangent(key, part):
    key = jax.random.fold_in(key, 23)
    first = jax.random.fold_in(key, 0)
    third = jax.random.fold_in(key, 2)
    shape = (FRAMES, ROWS, COLS, C)
    rows = lax.broadcasted_iota(jnp.float32, (FRAMES, ROWS, COLS, 1), 1)
    rise = 1.0 + 2.0 * rows / ROWS
    noise = jnp.clip(jax.random.normal(first, shape, jnp.float32), -4.0, 4.0)
    rough = jax.random.uniform(third, (FRAMES, ROWS, COLS, 1), jnp.float32, 0.5, 1.5)
    return (noise * rise * rough).astype(jnp.bfloat16)


def bell_draw(own_key, extent, scale, most, dtype=jnp.bfloat16):
    result = jax.random.normal(own_key, extent, jnp.float32) * scale
    return jnp.minimum(jnp.maximum(result, -most), most).astype(dtype)


def setup_inputs(seed: int = 0) -> dict:
    key_of = jax.random.split(jax.random.key(seed), 8)
    return {
        "frames": draw_frames(jax.random.fold_in(key_of[7], 71), 0),
        "cotangent": draw_cotangent(jax.random.fold_in(key_of[7], 71), 0),
        "layer_norm_gain": jnp.clip(1.0 + 0.18 * jax.random.normal(key_of[2], (C,), jnp.float32), 0.1, 1.9),
        "w_in": bell_draw(key_of[3], (C, HID), C ** -0.5, 0.25),
        "kernel": bell_draw(key_of[4], (9, HID), 9 ** -0.5, 2.0),
        "w_att": bell_draw(key_of[5], (C, C), C ** -0.5, 0.25, jnp.float32),
        "w_out": bell_draw(key_of[6], (C, C), C ** -0.5, 0.25),
    }


EPS = 1e-06

def conv_taps(padded, kernel, rows, cols, flip):
    taps = kernel.astype(jnp.float32)
    total = jnp.zeros((rows, cols, taps.shape[1]), jnp.float32)
    for i in range(3):
        for j in range(3):
            if flip:
                window = padded[2 - i:2 - i + rows, 2 - j:2 - j + cols]
            else:
                window = padded[i:i + rows, j:j + cols]
            total = total + window.astype(jnp.float32) * taps[3 * i + j]
    return total

def one_frame(image_frame, upstream_gradient, layer_norm_gain, w_in, kernel, w_att, w_out):
    width = image_frame.shape[-1]
    xf = image_frame.astype(jnp.float32)
    centered_values = xf - lax.optimization_barrier(jnp.mean(xf, -1, keepdims=True))
    inverse_deviation = lax.rsqrt(lax.optimization_barrier(jnp.mean(centered_values * centered_values, -1, keepdims=True)) + EPS)
    normalized_input = centered_values * inverse_deviation
    normalized_output = (normalized_input * layer_norm_gain).astype(jnp.bfloat16)
    flat_n = normalized_output.reshape(-1, width)
    expanded = jnp.dot(flat_n, w_in, preferred_element_type=jnp.float32).astype(jnp.bfloat16)
    expanded = expanded.reshape(ROWS, COLS, HID)
    padded = jnp.pad(expanded, ((1, 1), (1, 1), (0, 0)))
    conv = conv_taps(padded, kernel, ROWS, COLS, False)
    gated = conv[..., :width] * conv[..., width:]
    pooled = lax.optimization_barrier(jnp.sum(gated, (0, 1))) / (ROWS * COLS)
    scale = jnp.dot(pooled, w_att, precision=lax.Precision.HIGHEST)
    attended = (gated * scale).astype(jnp.bfloat16)
    flat_d = upstream_gradient.reshape(-1, width)
    d_att = jnp.dot(flat_d, w_out.T, preferred_element_type=jnp.float32).reshape(ROWS, COLS, width)
    out_sum = jnp.dot(attended.reshape(-1, width).T, flat_d, preferred_element_type=jnp.float32)
    d_scale = lax.optimization_barrier(jnp.sum(d_att * gated, (0, 1)))
    att_term = jnp.outer(pooled, d_scale)
    back = jnp.dot(d_scale, w_att.T, precision=lax.Precision.HIGHEST)
    d_gated = d_att * scale + back / (ROWS * COLS)
    d_conv = jnp.concatenate([d_gated * conv[..., width:], d_gated * conv[..., :width]], -1).astype(jnp.bfloat16)
    d_pad = jnp.pad(d_conv, ((1, 1), (1, 1), (0, 0)))
    d_exp = conv_taps(d_pad, kernel, ROWS, COLS, True).astype(jnp.bfloat16)
    dcf = d_conv.astype(jnp.float32)
    kernel_sum = jnp.stack([lax.optimization_barrier(jnp.sum(padded[i:i + ROWS, j:j + COLS].astype(jnp.float32) * dcf, (0, 1))) for i in range(3) for j in range(3)])
    flat_e = d_exp.reshape(-1, HID)
    in_sum = jnp.dot(flat_n.T, flat_e, preferred_element_type=jnp.float32)
    d_norm = jnp.dot(flat_e, w_in.T, preferred_element_type=jnp.float32).reshape(ROWS, COLS, width)
    normalized_gradient = d_norm * layer_norm_gain
    input_gradient = upstream_gradient.astype(jnp.float32) + inverse_deviation * (normalized_gradient - lax.optimization_barrier(jnp.mean(normalized_gradient, -1, keepdims=True)) - normalized_input * lax.optimization_barrier(jnp.mean(normalized_gradient * normalized_input, -1, keepdims=True)))
    return (input_gradient.astype(jnp.bfloat16), in_sum, kernel_sum, att_term, out_sum)

def reference(frames, cotangent, layer_norm_gain, w_in, kernel, w_att, w_out):

    def step(pair):
        return one_frame(pair[0], pair[1], layer_norm_gain, w_in, kernel, w_att, w_out)
    grad_frames, in_s, ker_s, att_s, out_s = lax.map(step, (frames, cotangent))
    factor = 1.0 / math.sqrt(FRAMES * ROWS * COLS)
    return (grad_frames, lax.optimization_barrier(jnp.sum(in_s, 0)) * factor, lax.optimization_barrier(jnp.sum(ker_s, 0)) * factor, lax.optimization_barrier(jnp.sum(att_s, 0)) * factor, lax.optimization_barrier(jnp.sum(out_s, 0)) * factor)
```

```python
import math

import jax
import jax.numpy as jnp
from jax import lax
from jax.sharding import Mesh, PartitionSpec as P

EPS = 1e-06
BF = jnp.bfloat16
F32 = jnp.float32


def layer_norm(x, gain):
    xf = x.astype(F32)
    centered = xf - jnp.mean(xf, -1, keepdims=True)
    rstd = lax.rsqrt(jnp.mean(centered * centered, -1, keepdims=True) + EPS)
    xhat = centered * rstd
    return (xhat * gain).astype(BF), xhat, rstd


def space_neighbours(down, up):
    count = lax.axis_size("x") * lax.axis_size("zh") * lax.axis_size("y")
    forward = [(i, i + 1) for i in range(count - 1)]
    backward = [(t, s) for s, t in forward]
    axes = ("x", "zh", "y")
    return lax.ppermute(down, axes, forward), lax.ppermute(up, axes, backward)


def ring(shift, count=4):
    return [(i, (i + shift) % count) for i in range(count)]


def z_ring(shift):
    place = lambda z: (z % 2) * 2 + z // 2
    return [(place(z), place((z + shift) % 4)) for z in range(4)]


def exchange_sum(v, axis, perms):
    parts = [lax.ppermute(v, axis, p) for p in perms]
    total = v.astype(F32)
    for part in parts:
        total = total + part.astype(F32)
    return total


def sum_over_space(v):
    v = exchange_sum(v, "y", [ring(s) for s in (1, 2, 3)])
    v = exchange_sum(v, "x", [ring(s) for s in (1, 2, 3)])
    return exchange_sum(v, "zh", [ring(1, 2)])


def scatter_sum(v, axis):
    n = lax.axis_size(axis)
    me = lax.axis_index(axis)
    rows = v.shape[0] // n
    sent = v.astype(BF)
    block = lambda a, i: lax.dynamic_slice_in_dim(a, i * rows, rows, 0)
    parts = [
        lax.ppermute(block(sent, (me + s) % n), axis, ring(s, n)) for s in range(1, n)
    ]
    total = block(v, me)
    for part in parts:
        total = total + part.astype(F32)
    return total


def gather(v, axis):
    n = lax.axis_size(axis)
    me = lax.axis_index(axis)
    rows = v.shape[0]
    out = jnp.zeros((n * rows,) + v.shape[1:], v.dtype)
    for s in range(n):
        part = v if s == 0 else lax.ppermute(v, axis, ring(s, n))
        out = lax.dynamic_update_slice_in_dim(out, part, ((me - s) % n) * rows, 0)
    return out


def sum_over_all(v):
    v = scatter_sum(v, "co")
    v = scatter_sum(v, "y")
    v = scatter_sum(v, "x")
    v = exchange_sum(v.astype(BF), ("zl", "zh"), [z_ring(s) for s in (1, 2, 3)])
    v = gather(v.astype(BF), "x")
    v = gather(v, "y")
    return gather(v, "co")


def local(frames, cotangent, gain, w_in, kernel, w_att, w_out):
    x = frames[0]
    cot = cotangent[0]
    rows, cols, width = x.shape
    hidden = w_in.shape[1]
    space = lax.axis_size("x") * lax.axis_size("zh") * lax.axis_size("y")
    place = (lax.axis_index("x") * lax.axis_size("zh") + lax.axis_index("zh")) * lax.axis_size(
        "y"
    ) + lax.axis_index("y")
    frame_count = lax.axis_size("zl") * lax.axis_size("co")
    frame = lax.axis_index("zl") * lax.axis_size("co") + lax.axis_index("co")
    pixels = rows * space * cols
    factor = 1.0 / math.sqrt(frame_count * pixels)
    taps = kernel.astype(F32)

    above, below = space_neighbours(x[-1:], x[:1])
    normed, xhat, rstd = layer_norm(x, gain)
    normed_above, _, _ = layer_norm(above, gain)
    normed_below, _, _ = layer_norm(below, gain)
    normed6 = jnp.concatenate([normed_above, normed, normed_below], 0)
    expanded = (
        jnp.dot(normed6.reshape(-1, width), w_in, preferred_element_type=F32)
        .astype(BF)
        .reshape(rows + 2, cols, hidden)
    )
    padded = jnp.pad(expanded, ((0, 0), (1, 1), (0, 0)))
    conv = jnp.zeros((rows, cols, hidden), F32)
    for i in range(3):
        for j in range(3):
            conv = conv + padded[i : i + rows, j : j + cols].astype(F32) * taps[3 * i + j]
    gated = conv[..., :width] * conv[..., width:]
    flat_cot = cot.reshape(-1, width)
    d_att = lax.dot_general(
        flat_cot, w_out, (((1,), (1,)), ((), ())), preferred_element_type=F32
    ).reshape(rows, cols, width)
    sums = jnp.concatenate([jnp.sum(gated, (0, 1)), jnp.sum(d_att * gated, (0, 1))])
    sums = sum_over_space(sums.reshape(8, 128)).reshape(-1)
    out_term = lax.dot_general(
        gated.astype(BF).reshape(-1, width),
        flat_cot,
        (((0,), (0,)), ((), ())),
        preferred_element_type=F32,
    )
    pooled = sums[:width] / pixels
    d_scale = sums[width:]
    scale = jnp.dot(pooled, w_att, precision=lax.Precision.HIGHEST)
    back = jnp.dot(d_scale, w_att.T, precision=lax.Precision.HIGHEST)
    out_term = out_term * scale[:, None]
    d_gated = d_att * scale + back / pixels
    d_conv = jnp.concatenate(
        [d_gated * conv[..., width:], d_gated * conv[..., :width]], -1
    ).astype(BF)
    dcf = d_conv.astype(F32)
    kernel_term = jnp.stack(
        [
            jnp.sum(padded[i : i + rows, j : j + cols].astype(F32) * dcf, (0, 1))
            for i in range(3)
            for j in range(3)
        ]
    )
    d_pad = jnp.pad(d_conv, ((2, 2), (1, 1), (0, 0)))
    d_exp = jnp.zeros((rows + 2, cols, hidden), F32)
    for i in range(3):
        for j in range(3):
            d_exp = (
                d_exp
                + d_pad[2 - i : 4 - i + rows, 2 - j : 2 - j + cols].astype(F32) * taps[3 * i + j]
            )
    d_exp = d_exp.astype(BF)
    in_term = lax.dot_general(
        normed6.reshape(-1, width),
        d_exp.reshape(-1, hidden),
        (((0,), (0,)), ((), ())),
        preferred_element_type=F32,
    )
    vectors = jnp.concatenate([pooled, d_scale])[None] * jnp.where(
        (jnp.arange(frame_count)[:, None] == frame) & (place == 0), 1.0, 0.0
    )
    small = jnp.concatenate([kernel_term, vectors], 0).reshape(-1, 128)
    small = jnp.pad(small, ((0, width - small.shape[0]), (0, 0)))
    total = sum_over_all(jnp.concatenate([in_term, out_term, small], 1)).astype(F32)

    d_norm = lax.dot_general(
        d_exp.reshape(-1, hidden), w_in, (((1,), (1,)), ((), ())), preferred_element_type=F32
    ).reshape(rows + 2, cols, width)
    from_above, from_below = space_neighbours(d_norm[-1].astype(BF), d_norm[0].astype(BF))
    d_norm = jnp.concatenate(
        [
            (d_norm[1] + from_above.astype(F32))[None],
            d_norm[2:rows],
            (d_norm[rows] + from_below.astype(F32))[None],
        ],
        0,
    )
    dxhat = d_norm * gain
    grad = cot.astype(F32) + rstd * (
        dxhat - jnp.mean(dxhat, -1, keepdims=True) - xhat * jnp.mean(dxhat * xhat, -1, keepdims=True)
    )

    in_sum = total[:, :hidden]
    out_sum = total[:, hidden : hidden + width]
    small = total[:, hidden + width :].reshape(-1, hidden)
    vectors = small[9 : 9 + frame_count]
    att_sum = lax.dot_general(
        vectors[:, :width],
        vectors[:, width:],
        (((0,), (0,)), ((), ())),
        precision=lax.Precision.HIGHEST,
    )
    return (
        grad.astype(BF)[None],
        in_sum * factor,
        small[:9] * factor,
        att_sum * factor,
        out_sum * factor,
    )


def solution(mesh):
    fine = Mesh(mesh.devices.reshape(2, 2, 4, 2, 4), ("zl", "co", "x", "zh", "y"))
    big = P(("zl", "co"), ("x", "zh", "y"), None, None)
    return jax.shard_map(
        local,
        mesh=fine,
        in_specs=(big, big, P(), P(), P(), P(), P()),
        out_specs=(big, P(), P(), P(), P()),
        check_vma=False,
    )
```

```python
import functools
import math

import jax
import jax.numpy as jnp
from jax import lax
from jax.experimental import pallas as pl
from jax.experimental.pallas import tpu as pltpu
from jax.sharding import Mesh, PartitionSpec as P

EPS = 1e-06
BF = jnp.bfloat16
F32 = jnp.float32
LANES = 128
PAD = 8
STEP = 16
VMEM = 56 * 1024 * 1024


def params(count=1):
    return pltpu.CompilerParams(
        dimension_semantics=("arbitrary",) * count, vmem_limit_bytes=VMEM
    )


def layer_norm(x):
    xf = x.astype(F32)
    centered = xf - jnp.mean(xf, -1, keepdims=True)
    rstd = lax.rsqrt(jnp.mean(centered * centered, -1, keepdims=True) + EPS)
    return centered * rstd, rstd


def expand_kernel(x_ref, gain_ref, w_ref, normed_t_ref, expanded_ref):
    xhat, _ = layer_norm(x_ref[0])
    normed = (xhat * gain_ref[...]).astype(BF)
    normed_t_ref[...] = normed.T
    expanded_ref[0] = jnp.dot(normed, w_ref[...], preferred_element_type=F32).astype(BF)


def expand(x, gain, w_in):
    rows, cols, width = x.shape
    hidden = w_in.shape[1]
    return pl.pallas_call(
        expand_kernel,
        grid=(rows,),
        in_specs=[
            pl.BlockSpec((1, cols, width), lambda r: (r, 0, 0)),
            pl.BlockSpec((1, width), lambda r: (0, 0)),
            pl.BlockSpec((width, hidden), lambda r: (0, 0)),
        ],
        out_specs=[
            pl.BlockSpec((width, cols), lambda r: (0, r)),
            pl.BlockSpec((1, cols, hidden), lambda r: (r, 0, 0)),
        ],
        out_shape=[
            jax.ShapeDtypeStruct((width, rows * cols), BF),
            jax.ShapeDtypeStruct((rows, cols, hidden), BF),
        ],
        compiler_params=params(),
        cost_estimate=pl.CostEstimate(
            flops=2 * rows * cols * width * hidden * 2,
            bytes_accessed=rows * cols * width * 8,
            transcendentals=0,
        ),
        name="expand",
    )(x, gain, w_in)


def attended_kernel(cot_ref, w_ref, out_ref):
    out_ref[0] = lax.dot_general(
        cot_ref[0], w_ref[...], (((1,), (1,)), ((), ())), preferred_element_type=F32
    ).astype(BF)


def attended_grad(cot, w_out):
    rows, cols, width = cot.shape
    return pl.pallas_call(
        attended_kernel,
        grid=(rows,),
        in_specs=[
            pl.BlockSpec((1, cols, width), lambda r: (r, 0, 0)),
            pl.BlockSpec((width, width), lambda r: (0, 0)),
        ],
        out_specs=pl.BlockSpec((1, cols, width), lambda r: (r, 0, 0)),
        out_shape=jax.ShapeDtypeStruct((rows, cols, width), BF),
        compiler_params=params(),
        cost_estimate=pl.CostEstimate(
            flops=2 * rows * cols * width * width * 2,
            bytes_accessed=rows * cols * width * 4,
            transcendentals=0,
        ),
        name="attended_grad",
    )(cot, w_out)


def fill(scratch, own_ref, halo_ref):
    rows, cols, _ = own_ref.shape
    zero = jnp.zeros((rows + 2, PAD, LANES), F32)
    scratch[:, 0:PAD, :] = zero
    scratch[:, PAD + cols : 2 * PAD + cols, :] = zero
    scratch[0, PAD : PAD + cols, :] = halo_ref[0].astype(F32)
    scratch[rows + 1, PAD : PAD + cols, :] = halo_ref[1].astype(F32)
    for r in range(rows):
        scratch[r + 1, PAD : PAD + cols, :] = own_ref[r].astype(F32)


def window(scratch, r, start, shift):
    return scratch[r, pl.ds(start + (PAD + shift), STEP), :]


def conv_kernel(
    ea_ref, eb_ref, ha_ref, hb_ref, ka_ref, kb_ref, d_ref, ca_ref, cb_ref, g_ref, sum_ref, sa, sb
):
    rows, cols, _ = ea_ref.shape
    fill(sa, ea_ref, ha_ref)
    fill(sb, eb_ref, hb_ref)

    def convolve(scratch, taps_ref, start):
        total = [None] * rows
        for r in range(rows + 2):
            for j in range(3):
                v = window(scratch, r, start, j - 1)
                for i in range(3):
                    if 0 <= r - i < rows:
                        term = v * taps_ref[3 * i + j, :][None, :]
                        o = r - i
                        total[o] = term if total[o] is None else total[o] + term
        return total

    def body(t, sums):
        start = pl.multiple_of(t * STEP, STEP)
        a = convolve(sa, ka_ref, start)
        b = convolve(sb, kb_ref, start)
        pooled, weighted = sums
        for r in range(rows):
            ca_ref[r, pl.ds(start, STEP), :] = a[r].astype(BF)
            cb_ref[r, pl.ds(start, STEP), :] = b[r].astype(BF)
            g = a[r] * b[r]
            g_ref[r, pl.ds(start, STEP), :] = g.astype(BF)
            dg = g * d_ref[r, pl.ds(start, STEP), :].astype(F32)
            pooled = pooled + (g[:8] + g[8:])
            weighted = weighted + (dg[:8] + dg[8:])
        return pooled, weighted

    zero = jnp.zeros((8, LANES), F32)
    pooled, weighted = lax.fori_loop(0, cols // STEP, body, (zero, zero))
    sum_ref[0:8, :] = pooled
    sum_ref[8:16, :] = weighted


def half_specs(rows, cols, chunks):
    return [
        pl.BlockSpec((rows, cols, LANES), lambda k: (0, 0, k)),
        pl.BlockSpec((rows, cols, LANES), lambda k: (0, 0, k + chunks)),
    ]


def convolution(expanded, halo, taps, d_att):
    rows, cols, hidden = expanded.shape
    width = hidden // 2
    chunks = width // LANES
    part = pl.BlockSpec((rows, cols, LANES), lambda k: (0, 0, k))
    shape = jax.ShapeDtypeStruct((rows, cols, width), BF)
    return pl.pallas_call(
        conv_kernel,
        grid=(chunks,),
        in_specs=half_specs(rows, cols, chunks)
        + half_specs(2, cols, chunks)
        + [
            pl.BlockSpec((9, LANES), lambda k: (0, k)),
            pl.BlockSpec((9, LANES), lambda k: (0, k + chunks)),
            part,
        ],
        out_specs=[part, part, part, pl.BlockSpec((16, LANES), lambda k: (0, k))],
        out_shape=[shape, shape, shape, jax.ShapeDtypeStruct((16, width), F32)],
        scratch_shapes=[pltpu.VMEM((rows + 2, cols + 2 * PAD, LANES), F32)] * 2,
        compiler_params=params(),
        cost_estimate=pl.CostEstimate(
            flops=rows * cols * hidden * 2 * 200, bytes_accessed=rows * cols * hidden * 5, transcendentals=0
        ),
        name="convolution",
    )(expanded, expanded, halo, halo, taps, taps, d_att)


def gradient_kernel(
    ea_ref, eb_ref, ha_ref, hb_ref, ka_ref, kb_ref, ca_ref, cb_ref, d_ref, scale_ref, back_ref,
    nt_ref, nh_ref, ta_ref, tb_ref, xa_ref, xb_ref, ia_ref, ib_ref, sa, sb, da, db,
):
    rows, cols, _ = ea_ref.shape
    fill(sa, ea_ref, ha_ref)
    fill(sb, eb_ref, hb_ref)
    zero = jnp.zeros((rows, PAD, LANES), F32)
    for d in (da, db):
        d[:, 0:PAD, :] = zero
        d[:, PAD + cols : 2 * PAD + cols, :] = zero
    scale = scale_ref[...]
    back = back_ref[...]

    def products(scratch, own, start, sums):
        part = [None] * 9
        for r in range(rows + 2):
            for j in range(3):
                v = window(scratch, r, start, j - 1)
                for i in range(3):
                    if 0 <= r - i < rows:
                        term = v * own[r - i]
                        n = 3 * i + j
                        part[n] = term if part[n] is None else part[n] + term
        return tuple(s + (p[:8] + p[8:]) for s, p in zip(sums, part))

    def first(t, sums):
        start = pl.multiple_of(t * STEP, STEP)
        own_a, own_b = [], []
        for r in range(rows):
            here = (r, pl.ds(start, STEP), slice(None))
            dg = d_ref[here].astype(F32) * scale + back
            own_a.append(dg * cb_ref[here].astype(F32))
            own_b.append(dg * ca_ref[here].astype(F32))
            da[r, pl.ds(start + PAD, STEP), :] = own_a[r]
            db[r, pl.ds(start + PAD, STEP), :] = own_b[r]
        return (
            products(sa, own_a, start, sums[0]),
            products(sb, own_b, start, sums[1]),
        )

    nought = (jnp.zeros((8, LANES), F32),) * 9
    sums = lax.fori_loop(0, cols // STEP, first, (nought, nought))
    for n in range(9):
        ta_ref[8 * n : 8 * n + 8, :] = sums[0][n]
        tb_ref[8 * n : 8 * n + 8, :] = sums[1][n]

    def spread(d, taps_ref, x_ref, start):
        total = [None] * (rows + 2)
        for r in range(rows):
            for j in range(3):
                v = window(d, r, start, 1 - j)
                for i in range(3):
                    term = v * taps_ref[3 * i + j, :][None, :]
                    o = r + i
                    total[o] = term if total[o] is None else total[o] + term
        for r in range(rows + 2):
            x_ref[r, pl.ds(start, STEP), :] = total[r].astype(BF)

    def second(t, carry):
        start = pl.multiple_of(t * STEP, STEP)
        spread(da, ka_ref, xa_ref, start)
        spread(db, kb_ref, xb_ref, start)
        return carry

    lax.fori_loop(0, cols // STEP, second, 0)

    total = None
    for r in range(rows + 2):
        if r == 0:
            left = nh_ref[:, 0:cols]
        elif r == rows + 1:
            left = nh_ref[:, cols : 2 * cols]
        else:
            left = nt_ref[:, (r - 1) * cols : r * cols]
        right = jnp.concatenate([xa_ref[r], xb_ref[r]], -1)
        term = jnp.dot(left, right, preferred_element_type=F32)
        total = term if total is None else total + term
    ia_ref[...] = total[:, :LANES].astype(BF)
    ib_ref[...] = total[:, LANES:].astype(BF)


def gradients(expanded, halo, taps, conv_a, conv_b, d_att, scale, back, normed_t, halo_t):
    rows, cols, hidden = expanded.shape
    width = hidden // 2
    chunks = width // LANES
    part = pl.BlockSpec((rows, cols, LANES), lambda k: (0, 0, k))
    wide = pl.BlockSpec((rows + 2, cols, LANES), lambda k: (0, 0, k))
    line = pl.BlockSpec((1, LANES), lambda k: (0, k))
    tap = pl.BlockSpec((72, LANES), lambda k: (0, k))
    inner = pl.BlockSpec((width, LANES), lambda k: (0, k))
    whole = lambda a: pl.BlockSpec(a.shape, lambda k: (0, 0))
    return pl.pallas_call(
        gradient_kernel,
        grid=(chunks,),
        in_specs=half_specs(rows, cols, chunks)
        + half_specs(2, cols, chunks)
        + [
            pl.BlockSpec((9, LANES), lambda k: (0, k)),
            pl.BlockSpec((9, LANES), lambda k: (0, k + chunks)),
            part,
            part,
            part,
            line,
            line,
            whole(normed_t),
            whole(halo_t),
        ],
        out_specs=[tap, tap, wide, wide, inner, inner],
        out_shape=[jax.ShapeDtypeStruct((72, width), F32)] * 2
        + [jax.ShapeDtypeStruct((rows + 2, cols, width), BF)] * 2
        + [jax.ShapeDtypeStruct((width, width), BF)] * 2,
        scratch_shapes=[pltpu.VMEM((rows + 2, cols + 2 * PAD, LANES), F32)] * 2
        + [pltpu.VMEM((rows, cols + 2 * PAD, LANES), F32)] * 2,
        compiler_params=params(),
        cost_estimate=pl.CostEstimate(
            flops=rows * cols * hidden * 2 * 1500, bytes_accessed=rows * cols * hidden * 10, transcendentals=0
        ),
        name="gradients",
    )(
        expanded, expanded, halo, halo, taps, taps, conv_a, conv_b, d_att, scale, back, normed_t, halo_t
    )


def back_project(xa, xb, w_ref):
    width = xa.shape[-1]
    dims = (((1,), (1,)), ((), ()))
    return lax.dot_general(
        xa, w_ref[:, :width], dims, preferred_element_type=F32
    ) + lax.dot_general(xb, w_ref[:, width:], dims, preferred_element_type=F32)


def edge_kernel(xa_ref, xb_ref, w_ref, out_ref):
    out_ref[0] = back_project(xa_ref[0], xb_ref[0], w_ref).astype(BF)


def edge_rows(xa, xb, w_in):
    rows, cols, width = xa.shape
    spec = pl.BlockSpec((1, cols, width), lambda r: (r * (rows - 1), 0, 0))
    return pl.pallas_call(
        edge_kernel,
        grid=(2,),
        in_specs=[spec, spec, pl.BlockSpec(w_in.shape, lambda r: (0, 0))],
        out_specs=pl.BlockSpec((1, cols, width), lambda r: (r, 0, 0)),
        out_shape=jax.ShapeDtypeStruct((2, cols, width), BF),
        compiler_params=params(),
        name="edge_rows",
    )(xa, xb, w_in)


def input_kernel(x_ref, cot_ref, xa_ref, xb_ref, above_ref, below_ref, gain_ref, w_ref, out_ref):
    row = pl.program_id(0)
    last = pl.num_programs(0) - 1
    d_norm = back_project(xa_ref[0], xb_ref[0], w_ref)
    d_norm = d_norm + jnp.where(row == 0, 1.0, 0.0) * above_ref[...].astype(F32)
    d_norm = d_norm + jnp.where(row == last, 1.0, 0.0) * below_ref[...].astype(F32)
    xhat, rstd = layer_norm(x_ref[0])
    dxhat = d_norm * gain_ref[...]
    grad = cot_ref[0].astype(F32) + rstd * (
        dxhat - jnp.mean(dxhat, -1, keepdims=True) - xhat * jnp.mean(dxhat * xhat, -1, keepdims=True)
    )
    out_ref[0, 0] = grad.astype(BF)


def input_grad(x, cot, xa, xb, above, below, gain, w_in):
    rows, cols, width = x.shape
    spec = pl.BlockSpec((1, cols, width), lambda r: (r, 0, 0))
    inner = pl.BlockSpec((1, cols, width), lambda r: (r + 1, 0, 0))
    edge = pl.BlockSpec((cols, width), lambda r: (0, 0))
    return pl.pallas_call(
        input_kernel,
        grid=(rows,),
        in_specs=[
            spec,
            spec,
            inner,
            inner,
            edge,
            edge,
            pl.BlockSpec((1, width), lambda r: (0, 0)),
            pl.BlockSpec(w_in.shape, lambda r: (0, 0)),
        ],
        out_specs=pl.BlockSpec((1, 1, cols, width), lambda r: (0, r, 0, 0)),
        out_shape=jax.ShapeDtypeStruct((1, rows, cols, width), BF),
        compiler_params=params(),
        cost_estimate=pl.CostEstimate(
            flops=2 * rows * cols * width * width * 6,
            bytes_accessed=rows * cols * width * 10,
            transcendentals=0,
        ),
        name="input_grad",
    )(x, cot, xa, xb, above, below, gain, w_in)


def space_neighbours(down, up):
    count = lax.axis_size("x") * lax.axis_size("zh") * lax.axis_size("y")
    forward = [(i, i + 1) for i in range(count - 1)]
    backward = [(t, s) for s, t in forward]
    axes = ("x", "zh", "y")
    return lax.ppermute(down, axes, forward), lax.ppermute(up, axes, backward)


def ring(shift, count=4):
    return [(i, (i + shift) % count) for i in range(count)]


def z_ring(shift):
    place = lambda z: (z % 2) * 2 + z // 2
    return [(place(z), place((z + shift) % 4)) for z in range(4)]


def exchange_sum(v, axis, perms):
    parts = [lax.ppermute(v, axis, p) for p in perms]
    total = v.astype(F32)
    for part in parts:
        total = total + part.astype(F32)
    return total


def sum_over_space(v):
    v = exchange_sum(v, "y", [ring(s) for s in (1, 2, 3)])
    v = exchange_sum(v, "x", [ring(s) for s in (1, 2, 3)])
    return exchange_sum(v, "zh", [ring(1, 2)])


def scatter_sum(v, axis):
    n = lax.axis_size(axis)
    me = lax.axis_index(axis)
    rows = v.shape[0] // n
    sent = v.astype(BF)
    block = lambda a, i: lax.dynamic_slice_in_dim(a, i * rows, rows, 0)
    parts = [
        lax.ppermute(block(sent, (me + s) % n), axis, ring(s, n)) for s in range(1, n)
    ]
    total = block(v, me)
    for part in parts:
        total = total + part.astype(F32)
    return total


def gather(v, axis):
    n = lax.axis_size(axis)
    me = lax.axis_index(axis)
    rows = v.shape[0]
    out = jnp.zeros((n * rows,) + v.shape[1:], v.dtype)
    for s in range(n):
        part = v if s == 0 else lax.ppermute(v, axis, ring(s, n))
        out = lax.dynamic_update_slice_in_dim(out, part, ((me - s) % n) * rows, 0)
    return out


def sum_over_all(v):
    v = scatter_sum(v, "co")
    v = scatter_sum(v, "y")
    v = scatter_sum(v, "x")
    v = exchange_sum(v.astype(BF), ("zl", "zh"), [z_ring(s) for s in (1, 2, 3)])
    v = gather(v.astype(BF), "x")
    v = gather(v, "y")
    return gather(v, "co")


def local(frames, cotangent, gain, w_in, kernel, w_att, w_out):
    x = frames[0]
    cot = cotangent[0]
    rows, cols, width = x.shape
    hidden = w_in.shape[1]
    space = lax.axis_size("x") * lax.axis_size("zh") * lax.axis_size("y")
    place = (lax.axis_index("x") * lax.axis_size("zh") + lax.axis_index("zh")) * lax.axis_size(
        "y"
    ) + lax.axis_index("y")
    frame_count = lax.axis_size("zl") * lax.axis_size("co")
    frame = lax.axis_index("zl") * lax.axis_size("co") + lax.axis_index("co")
    pixels = rows * space * cols
    factor = 1.0 / math.sqrt(frame_count * pixels)
    taps = kernel.astype(F32)
    gain = gain[None]

    above, below = space_neighbours(x[-1:], x[:1])
    normed_t, expanded = expand(x, gain, w_in)
    d_att = attended_grad(cot, w_out)
    halo_t, halo = expand(jnp.concatenate([above, below], 0), gain, w_in)
    conv_a, conv_b, gated, sums = convolution(expanded, halo, taps, d_att)
    sums = jnp.sum(sums.reshape(2, 8, width), 1)
    sums = sum_over_space(sums.reshape(8, 128)).reshape(-1)
    out_term = lax.dot_general(
        gated.reshape(-1, width),
        cot.reshape(-1, width),
        (((0,), (0,)), ((), ())),
        preferred_element_type=F32,
    )
    pooled = sums[:width] / pixels
    d_scale = sums[width:]
    scale = jnp.dot(pooled, w_att, precision=lax.Precision.HIGHEST)
    back = jnp.dot(d_scale, w_att.T, precision=lax.Precision.HIGHEST) / pixels
    taps_a, taps_b, d_exp_a, d_exp_b, in_a, in_b = gradients(
        expanded, halo, taps, conv_a, conv_b, d_att, scale[None], back[None], normed_t, halo_t
    )
    kernel_term = jnp.sum(jnp.concatenate([taps_a, taps_b], -1).reshape(9, 8, hidden), 1)
    vectors = jnp.concatenate([pooled, d_scale])[None] * jnp.where(
        (jnp.arange(frame_count)[:, None] == frame) & (place == 0), 1.0, 0.0
    )
    small = jnp.concatenate([kernel_term, vectors], 0).reshape(-1, 128)
    small = jnp.pad(small, ((0, width - small.shape[0]), (0, 0)))
    payload = jnp.concatenate(
        [in_a, in_b, (out_term * scale[:, None]).astype(BF), small.astype(BF)], 1
    )
    total = sum_over_all(payload).astype(F32)

    edges = edge_rows(d_exp_a, d_exp_b, w_in)
    from_above, from_below = space_neighbours(edges[1], edges[0])
    grad = input_grad(x, cot, d_exp_a, d_exp_b, from_above, from_below, gain, w_in)

    in_sum = total[:, :hidden]
    out_sum = total[:, hidden : hidden + width]
    small = total[:, hidden + width :].reshape(-1, hidden)
    vectors = small[9 : 9 + frame_count]
    att_sum = lax.dot_general(
        vectors[:, :width],
        vectors[:, width:],
        (((0,), (0,)), ((), ())),
        precision=lax.Precision.HIGHEST,
    )
    return (
        grad,
        in_sum * factor,
        small[:9] * factor,
        att_sum * factor,
        out_sum * factor,
    )


def solution(mesh):
    fine = Mesh(mesh.devices.reshape(2, 2, 4, 2, 4), ("zl", "co", "x", "zh", "y"))
    big = P(("zl", "co"), ("x", "zh", "y"), None, None)
    return jax.shard_map(
        local,
        mesh=fine,
        in_specs=(big, big, P(), P(), P(), P(), P()),
        out_specs=(big, P(), P(), P(), P()),
        check_vma=False,
    )
```

```python
import functools
import math

import jax
import jax.numpy as jnp
from jax import lax
from jax.experimental import pallas as pl
from jax.experimental.pallas import tpu as pltpu
from jax.sharding import Mesh, PartitionSpec as P

EPS = 1e-06
BF = jnp.bfloat16
F32 = jnp.float32
LANES = 128
PAD = 8
STEP = 16
VMEM = 56 * 1024 * 1024


def params(count=1):
    return pltpu.CompilerParams(
        dimension_semantics=("arbitrary",) * count, vmem_limit_bytes=VMEM
    )


def layer_norm(x):
    xf = x.astype(F32)
    centered = xf - jnp.mean(xf, -1, keepdims=True)
    rstd = lax.rsqrt(jnp.mean(centered * centered, -1, keepdims=True) + EPS)
    return centered * rstd, rstd


def expand_kernel(x_ref, gain_ref, w_ref, normed_t_ref, expanded_ref):
    xhat, _ = layer_norm(x_ref[0])
    normed = (xhat * gain_ref[...]).astype(BF)
    normed_t_ref[...] = normed.T
    expanded_ref[0] = jnp.dot(normed, w_ref[...], preferred_element_type=F32).astype(BF)


def expand(x, gain, w_in):
    rows, cols, width = x.shape
    hidden = w_in.shape[1]
    return pl.pallas_call(
        expand_kernel,
        grid=(rows,),
        in_specs=[
            pl.BlockSpec((1, cols, width), lambda r: (r, 0, 0)),
            pl.BlockSpec((1, width), lambda r: (0, 0)),
            pl.BlockSpec((width, hidden), lambda r: (0, 0)),
        ],
        out_specs=[
            pl.BlockSpec((width, cols), lambda r: (0, r)),
            pl.BlockSpec((1, cols, hidden), lambda r: (r, 0, 0)),
        ],
        out_shape=[
            jax.ShapeDtypeStruct((width, rows * cols), BF),
            jax.ShapeDtypeStruct((rows, cols, hidden), BF),
        ],
        compiler_params=params(),
        cost_estimate=pl.CostEstimate(
            flops=2 * rows * cols * width * hidden * 2,
            bytes_accessed=rows * cols * width * 8,
            transcendentals=0,
        ),
        name="expand",
    )(x, gain, w_in)


def attended_kernel(cot_ref, w_ref, out_ref):
    out_ref[0] = lax.dot_general(
        cot_ref[0], w_ref[...], (((1,), (1,)), ((), ())), preferred_element_type=F32
    ).astype(BF)


def attended_grad(cot, w_out):
    rows, cols, width = cot.shape
    return pl.pallas_call(
        attended_kernel,
        grid=(rows,),
        in_specs=[
            pl.BlockSpec((1, cols, width), lambda r: (r, 0, 0)),
            pl.BlockSpec((width, width), lambda r: (0, 0)),
        ],
        out_specs=pl.BlockSpec((1, cols, width), lambda r: (r, 0, 0)),
        out_shape=jax.ShapeDtypeStruct((rows, cols, width), BF),
        compiler_params=params(),
        cost_estimate=pl.CostEstimate(
            flops=2 * rows * cols * width * width * 2,
            bytes_accessed=rows * cols * width * 4,
            transcendentals=0,
        ),
        name="attended_grad",
    )(cot, w_out)


def fill(scratch, own_ref, halo_ref):
    rows, cols, _ = own_ref.shape
    zero = jnp.zeros((rows + 2, PAD, LANES), F32)
    scratch[:, 0:PAD, :] = zero
    scratch[:, PAD + cols : 2 * PAD + cols, :] = zero
    scratch[0, PAD : PAD + cols, :] = halo_ref[0].astype(F32)
    scratch[rows + 1, PAD : PAD + cols, :] = halo_ref[1].astype(F32)
    for r in range(rows):
        scratch[r + 1, PAD : PAD + cols, :] = own_ref[r].astype(F32)


def window(scratch, r, start, shift):
    return scratch[r, pl.ds(start + (PAD + shift), STEP), :]


def conv_kernel(
    ea_ref, eb_ref, ha_ref, hb_ref, ka_ref, kb_ref, d_ref, ca_ref, cb_ref, g_ref, sum_ref, sa, sb
):
    rows, cols, _ = ea_ref.shape
    fill(sa, ea_ref, ha_ref)
    fill(sb, eb_ref, hb_ref)

    def convolve(scratch, taps_ref, start):
        total = [None] * rows
        for r in range(rows + 2):
            for j in range(3):
                v = window(scratch, r, start, j - 1)
                for i in range(3):
                    if 0 <= r - i < rows:
                        term = v * taps_ref[3 * i + j, :][None, :]
                        o = r - i
                        total[o] = term if total[o] is None else total[o] + term
        return total

    def body(t, sums):
        start = pl.multiple_of(t * STEP, STEP)
        a = convolve(sa, ka_ref, start)
        b = convolve(sb, kb_ref, start)
        pooled, weighted = sums
        for r in range(rows):
            ca_ref[r, pl.ds(start, STEP), :] = a[r].astype(BF)
            cb_ref[r, pl.ds(start, STEP), :] = b[r].astype(BF)
            g = a[r] * b[r]
            g_ref[r, pl.ds(start, STEP), :] = g.astype(BF)
            dg = g * d_ref[r, pl.ds(start, STEP), :].astype(F32)
            pooled = pooled + (g[:8] + g[8:])
            weighted = weighted + (dg[:8] + dg[8:])
        return pooled, weighted

    zero = jnp.zeros((8, LANES), F32)
    pooled, weighted = lax.fori_loop(0, cols // STEP, body, (zero, zero))
    sum_ref[0:8, :] = pooled
    sum_ref[8:16, :] = weighted


def half_specs(rows, cols, chunks):
    return [
        pl.BlockSpec((rows, cols, LANES), lambda k: (0, 0, k)),
        pl.BlockSpec((rows, cols, LANES), lambda k: (0, 0, k + chunks)),
    ]


def convolution(expanded, halo, taps, d_att):
    rows, cols, hidden = expanded.shape
    width = hidden // 2
    chunks = width // LANES
    part = pl.BlockSpec((rows, cols, LANES), lambda k: (0, 0, k))
    shape = jax.ShapeDtypeStruct((rows, cols, width), BF)
    return pl.pallas_call(
        conv_kernel,
        grid=(chunks,),
        in_specs=half_specs(rows, cols, chunks)
        + half_specs(2, cols, chunks)
        + [
            pl.BlockSpec((9, LANES), lambda k: (0, k)),
            pl.BlockSpec((9, LANES), lambda k: (0, k + chunks)),
            part,
        ],
        out_specs=[part, part, part, pl.BlockSpec((16, LANES), lambda k: (0, k))],
        out_shape=[shape, shape, shape, jax.ShapeDtypeStruct((16, width), F32)],
        scratch_shapes=[pltpu.VMEM((rows + 2, cols + 2 * PAD, LANES), F32)] * 2,
        compiler_params=params(),
        cost_estimate=pl.CostEstimate(
            flops=rows * cols * hidden * 2 * 200, bytes_accessed=rows * cols * hidden * 5, transcendentals=0
        ),
        name="convolution",
    )(expanded, expanded, halo, halo, taps, taps, d_att)


def gradient_kernel(
    ea_ref, eb_ref, ha_ref, hb_ref, ka_ref, kb_ref, ca_ref, cb_ref, d_ref, scale_ref, back_ref,
    nt_ref, nh_ref, ta_ref, tb_ref, xa_ref, xb_ref, ia_ref, ib_ref, sa, sb, da, db,
):
    rows, cols, _ = ea_ref.shape
    fill(sa, ea_ref, ha_ref)
    fill(sb, eb_ref, hb_ref)
    zero = jnp.zeros((rows, PAD, LANES), F32)
    for d in (da, db):
        d[:, 0:PAD, :] = zero
        d[:, PAD + cols : 2 * PAD + cols, :] = zero
    scale = scale_ref[...]
    back = back_ref[...]

    def products(scratch, own, start, sums):
        part = [None] * 9
        for r in range(rows + 2):
            for j in range(3):
                v = window(scratch, r, start, j - 1)
                for i in range(3):
                    if 0 <= r - i < rows:
                        term = v * own[r - i]
                        n = 3 * i + j
                        part[n] = term if part[n] is None else part[n] + term
        return tuple(s + (p[:8] + p[8:]) for s, p in zip(sums, part))

    def first(t, sums):
        start = pl.multiple_of(t * STEP, STEP)
        own_a, own_b = [], []
        for r in range(rows):
            here = (r, pl.ds(start, STEP), slice(None))
            dg = d_ref[here].astype(F32) * scale + back
            own_a.append(dg * cb_ref[here].astype(F32))
            own_b.append(dg * ca_ref[here].astype(F32))
            da[r, pl.ds(start + PAD, STEP), :] = own_a[r]
            db[r, pl.ds(start + PAD, STEP), :] = own_b[r]
        return (
            products(sa, own_a, start, sums[0]),
            products(sb, own_b, start, sums[1]),
        )

    nought = (jnp.zeros((8, LANES), F32),) * 9
    sums = lax.fori_loop(0, cols // STEP, first, (nought, nought))
    for n in range(9):
        ta_ref[8 * n : 8 * n + 8, :] = sums[0][n]
        tb_ref[8 * n : 8 * n + 8, :] = sums[1][n]

    def spread(d, taps_ref, x_ref, start):
        total = [None] * (rows + 2)
        for r in range(rows):
            for j in range(3):
                v = window(d, r, start, 1 - j)
                for i in range(3):
                    term = v * taps_ref[3 * i + j, :][None, :]
                    o = r + i
                    total[o] = term if total[o] is None else total[o] + term
        for r in range(rows + 2):
            x_ref[r, pl.ds(start, STEP), :] = total[r].astype(BF)

    def second(t, carry):
        start = pl.multiple_of(t * STEP, STEP)
        spread(da, ka_ref, xa_ref, start)
        spread(db, kb_ref, xb_ref, start)
        return carry

    lax.fori_loop(0, cols // STEP, second, 0)

    total = None
    for r in range(rows + 2):
        if r == 0:
            left = nh_ref[:, 0:cols]
        elif r == rows + 1:
            left = nh_ref[:, cols : 2 * cols]
        else:
            left = nt_ref[:, (r - 1) * cols : r * cols]
        right = jnp.concatenate([xa_ref[r], xb_ref[r]], -1)
        term = jnp.dot(left, right, preferred_element_type=F32)
        total = term if total is None else total + term
    ia_ref[0] = total[:, :LANES].astype(BF)
    ib_ref[0] = total[:, LANES:].astype(BF)


def gradients(expanded, halo, taps, conv_a, conv_b, d_att, scale, back, normed_t, halo_t):
    rows, cols, hidden = expanded.shape
    width = hidden // 2
    chunks = width // LANES
    part = pl.BlockSpec((rows, cols, LANES), lambda k: (0, 0, k))
    wide = pl.BlockSpec((rows + 2, cols, LANES), lambda k: (0, 0, k))
    line = pl.BlockSpec((1, LANES), lambda k: (0, k))
    tap = pl.BlockSpec((72, LANES), lambda k: (0, k))
    inner = pl.BlockSpec((1, width, LANES), lambda k: (k, 0, 0))
    whole = lambda a: pl.BlockSpec(a.shape, lambda k: (0, 0))
    return pl.pallas_call(
        gradient_kernel,
        grid=(chunks,),
        in_specs=half_specs(rows, cols, chunks)
        + half_specs(2, cols, chunks)
        + [
            pl.BlockSpec((9, LANES), lambda k: (0, k)),
            pl.BlockSpec((9, LANES), lambda k: (0, k + chunks)),
            part,
            part,
            part,
            line,
            line,
            whole(normed_t),
            whole(halo_t),
        ],
        out_specs=[tap, tap, wide, wide, inner, inner],
        out_shape=[jax.ShapeDtypeStruct((72, width), F32)] * 2
        + [jax.ShapeDtypeStruct((rows + 2, cols, width), BF)] * 2
        + [jax.ShapeDtypeStruct((chunks, width, LANES), BF)] * 2,
        scratch_shapes=[pltpu.VMEM((rows + 2, cols + 2 * PAD, LANES), F32)] * 2
        + [pltpu.VMEM((rows, cols + 2 * PAD, LANES), F32)] * 2,
        compiler_params=params(),
        cost_estimate=pl.CostEstimate(
            flops=rows * cols * hidden * 2 * 1500, bytes_accessed=rows * cols * hidden * 10, transcendentals=0
        ),
        name="gradients",
    )(
        expanded, expanded, halo, halo, taps, taps, conv_a, conv_b, d_att, scale, back, normed_t, halo_t
    )


def back_project(xa, xb, w_ref):
    width = xa.shape[-1]
    dims = (((1,), (1,)), ((), ()))
    return lax.dot_general(
        xa, w_ref[:, :width], dims, preferred_element_type=F32
    ) + lax.dot_general(xb, w_ref[:, width:], dims, preferred_element_type=F32)


def edge_kernel(xa_ref, xb_ref, w_ref, out_ref):
    out_ref[0] = back_project(xa_ref[0], xb_ref[0], w_ref).astype(BF)


def edge_rows(xa, xb, w_in):
    rows, cols, width = xa.shape
    spec = pl.BlockSpec((1, cols, width), lambda r: (r * (rows - 1), 0, 0))
    return pl.pallas_call(
        edge_kernel,
        grid=(2,),
        in_specs=[spec, spec, pl.BlockSpec(w_in.shape, lambda r: (0, 0))],
        out_specs=pl.BlockSpec((1, cols, width), lambda r: (r, 0, 0)),
        out_shape=jax.ShapeDtypeStruct((2, cols, width), BF),
        compiler_params=params(),
        name="edge_rows",
    )(xa, xb, w_in)


def input_kernel(x_ref, cot_ref, xa_ref, xb_ref, above_ref, below_ref, gain_ref, w_ref, out_ref):
    row = pl.program_id(0)
    last = pl.num_programs(0) - 1
    d_norm = back_project(xa_ref[0], xb_ref[0], w_ref)
    d_norm = d_norm + jnp.where(row == 0, 1.0, 0.0) * above_ref[...].astype(F32)
    d_norm = d_norm + jnp.where(row == last, 1.0, 0.0) * below_ref[...].astype(F32)
    xhat, rstd = layer_norm(x_ref[0])
    dxhat = d_norm * gain_ref[...]
    grad = cot_ref[0].astype(F32) + rstd * (
        dxhat - jnp.mean(dxhat, -1, keepdims=True) - xhat * jnp.mean(dxhat * xhat, -1, keepdims=True)
    )
    out_ref[0, 0] = grad.astype(BF)


def input_grad(x, cot, xa, xb, above, below, gain, w_in):
    rows, cols, width = x.shape
    spec = pl.BlockSpec((1, cols, width), lambda r: (r, 0, 0))
    inner = pl.BlockSpec((1, cols, width), lambda r: (r + 1, 0, 0))
    edge = pl.BlockSpec((cols, width), lambda r: (0, 0))
    return pl.pallas_call(
        input_kernel,
        grid=(rows,),
        in_specs=[
            spec,
            spec,
            inner,
            inner,
            edge,
            edge,
            pl.BlockSpec((1, width), lambda r: (0, 0)),
            pl.BlockSpec(w_in.shape, lambda r: (0, 0)),
        ],
        out_specs=pl.BlockSpec((1, 1, cols, width), lambda r: (0, r, 0, 0)),
        out_shape=jax.ShapeDtypeStruct((1, rows, cols, width), BF),
        compiler_params=params(),
        cost_estimate=pl.CostEstimate(
            flops=2 * rows * cols * width * width * 6,
            bytes_accessed=rows * cols * width * 10,
            transcendentals=0,
        ),
        name="input_grad",
    )(x, cot, xa, xb, above, below, gain, w_in)


def space_neighbours(down, up):
    count = lax.axis_size("x") * lax.axis_size("zh") * lax.axis_size("y")
    forward = [(i, i + 1) for i in range(count - 1)]
    backward = [(t, s) for s, t in forward]
    axes = ("x", "zh", "y")
    return lax.ppermute(down, axes, forward), lax.ppermute(up, axes, backward)


SPACE = ("x", "zh", "y")
CHIPS = ("zl", "x", "zh", "y")


def sum_over_space(v):
    n = lax.axis_size(SPACE)
    copies = lax.optimization_barrier(jnp.broadcast_to(v[None], (n,) + v.shape))
    return jnp.sum(lax.all_to_all(copies, SPACE, 0, 0, tiled=True), 0)


def sum_over_all(v):
    half = v.shape[0] // 2
    n = lax.axis_size(CHIPS)
    me = lax.axis_index("co")
    swap = [(0, 1), (1, 0)]
    other = lax.ppermute(lax.dynamic_slice_in_dim(v, (1 - me) * half, half, 0), "co", swap)
    own = lax.dynamic_slice_in_dim(v, me * half, half, 0)
    own = (own.astype(F32) + other.astype(F32)).astype(BF)
    own = lax.optimization_barrier(own.reshape(n, half // n, v.shape[1]))
    parts = lax.all_to_all(own, CHIPS, 0, 0, tiled=True)
    part = jnp.sum(parts.astype(F32), 0).astype(BF)
    copies = lax.optimization_barrier(jnp.broadcast_to(part[None], parts.shape))
    own = lax.all_to_all(copies, CHIPS, 0, 0, tiled=True).reshape(half, v.shape[1])
    other = lax.ppermute(own, "co", swap)
    return jnp.where(me == 0, own, other), jnp.where(me == 0, other, own)


def local(frames, cotangent, gain, w_in, kernel, w_att, w_out):
    x = frames[0]
    cot = cotangent[0]
    rows, cols, width = x.shape
    hidden = w_in.shape[1]
    space = lax.axis_size("x") * lax.axis_size("zh") * lax.axis_size("y")
    place = (lax.axis_index("x") * lax.axis_size("zh") + lax.axis_index("zh")) * lax.axis_size(
        "y"
    ) + lax.axis_index("y")
    frame_count = lax.axis_size("zl") * lax.axis_size("co")
    frame = lax.axis_index("zl") * lax.axis_size("co") + lax.axis_index("co")
    pixels = rows * space * cols
    factor = 1.0 / math.sqrt(frame_count * pixels)
    taps = kernel.astype(F32)
    gain = gain[None]

    above, below = space_neighbours(x[-1:], x[:1])
    normed_t, expanded = expand(x, gain, w_in)
    d_att = attended_grad(cot, w_out)
    halo_t, halo = expand(jnp.concatenate([above, below], 0), gain, w_in)
    conv_a, conv_b, gated, sums = convolution(expanded, halo, taps, d_att)
    sums = jnp.sum(sums.reshape(2, 8, width), 1)
    sums = sum_over_space(sums.reshape(8, 128)).reshape(-1)
    out_term = lax.dot_general(
        gated.reshape(-1, width),
        cot.reshape(-1, width),
        (((0,), (0,)), ((), ())),
        preferred_element_type=F32,
    )
    pooled = sums[:width] / pixels
    d_scale = sums[width:]
    scale = jnp.dot(pooled, w_att, precision=lax.Precision.HIGHEST)
    back = jnp.dot(d_scale, w_att.T, precision=lax.Precision.HIGHEST) / pixels
    taps_a, taps_b, d_exp_a, d_exp_b, in_a, in_b = gradients(
        expanded, halo, taps, conv_a, conv_b, d_att, scale[None], back[None], normed_t, halo_t
    )
    kernel_term = jnp.sum(jnp.concatenate([taps_a, taps_b], -1).reshape(9, 8, hidden), 1)
    vectors = jnp.concatenate([pooled, d_scale])[None] * jnp.where(
        (jnp.arange(frame_count)[:, None] == frame) & (place == 0), 1.0, 0.0
    )
    small = jnp.concatenate([kernel_term, vectors], 0).reshape(-1, LANES)
    small = jnp.pad(small, ((0, 2 * width - small.shape[0]), (0, 0)))
    out_term = (out_term * scale[:, None]).reshape(width, width // LANES, LANES)
    payload = jnp.concatenate(
        [
            in_a.reshape(-1, LANES),
            in_b.reshape(-1, LANES),
            out_term.transpose(1, 0, 2).astype(BF).reshape(-1, LANES),
            small.astype(BF),
        ],
        0,
    )
    edges = edge_rows(d_exp_a, d_exp_b, w_in)
    from_above, from_below = space_neighbours(edges[1], edges[0])
    total = jnp.concatenate(sum_over_all(payload), 0).reshape(-1, width, LANES)
    grad = input_grad(x, cot, d_exp_a, d_exp_b, from_above, from_below, gain, w_in)

    total = total.astype(F32)
    groups = hidden // LANES
    lanes = lambda a: a.transpose(1, 0, 2).reshape(width, -1)
    in_sum = lanes(total[:groups])
    out_sum = lanes(total[groups : groups + width // LANES])
    small = total[groups + width // LANES :].reshape(-1, hidden)
    vectors = small[9 : 9 + frame_count]
    att_sum = lax.dot_general(
        vectors[:, :width],
        vectors[:, width:],
        (((0,), (0,)), ((), ())),
        precision=lax.Precision.HIGHEST,
    )
    return (
        grad,
        in_sum * factor,
        small[:9] * factor,
        att_sum * factor,
        out_sum * factor,
    )


def solution(mesh):
    fine = Mesh(mesh.devices.reshape(2, 2, 4, 2, 4), ("zl", "co", "x", "zh", "y"))
    big = P(("zl", "co"), ("x", "zh", "y"), None, None)
    return jax.shard_map(
        local,
        mesh=fine,
        in_specs=(big, big, P(), P(), P(), P(), P()),
        out_specs=(big, P(), P(), P(), P()),
        check_vma=False,
    )
```

```python
import functools
import math

import jax
import jax.numpy as jnp
from jax import lax
from jax.experimental import pallas as pl
from jax.experimental.pallas import tpu as pltpu
from jax.sharding import Mesh, PartitionSpec as P

EPS = 1e-06
BF = jnp.bfloat16
F32 = jnp.float32
LANES = 128
PAD = 8
STEP = 16
VMEM = 56 * 1024 * 1024


def params(count=1):
    return pltpu.CompilerParams(
        dimension_semantics=("arbitrary",) * count, vmem_limit_bytes=VMEM
    )


def layer_norm(x):
    xf = x.astype(F32)
    centered = xf - jnp.mean(xf, -1, keepdims=True)
    rstd = lax.rsqrt(jnp.mean(centered * centered, -1, keepdims=True) + EPS)
    return centered * rstd, rstd


def expand_kernel(x_ref, gain_ref, w_ref, normed_t_ref, expanded_ref):
    xhat, _ = layer_norm(x_ref[0])
    normed = (xhat * gain_ref[...]).astype(BF)
    normed_t_ref[...] = normed.T
    expanded_ref[0] = jnp.dot(normed, w_ref[...], preferred_element_type=F32).astype(BF)


def expand(x, gain, w_in):
    rows, cols, width = x.shape
    hidden = w_in.shape[1]
    return pl.pallas_call(
        expand_kernel,
        grid=(rows,),
        in_specs=[
            pl.BlockSpec((1, cols, width), lambda r: (r, 0, 0)),
            pl.BlockSpec((1, width), lambda r: (0, 0)),
            pl.BlockSpec((width, hidden), lambda r: (0, 0)),
        ],
        out_specs=[
            pl.BlockSpec((width, cols), lambda r: (0, r)),
            pl.BlockSpec((1, cols, hidden), lambda r: (r, 0, 0)),
        ],
        out_shape=[
            jax.ShapeDtypeStruct((width, rows * cols), BF),
            jax.ShapeDtypeStruct((rows, cols, hidden), BF),
        ],
        compiler_params=params(),
        cost_estimate=pl.CostEstimate(
            flops=2 * rows * cols * width * hidden * 2,
            bytes_accessed=rows * cols * width * 8,
            transcendentals=0,
        ),
        name="expand",
    )(x, gain, w_in)


def attended_kernel(cot_ref, w_ref, out_ref):
    out_ref[0] = lax.dot_general(
        cot_ref[0], w_ref[...], (((1,), (1,)), ((), ())), preferred_element_type=F32
    ).astype(BF)


def attended_grad(cot, w_out):
    rows, cols, width = cot.shape
    return pl.pallas_call(
        attended_kernel,
        grid=(rows,),
        in_specs=[
            pl.BlockSpec((1, cols, width), lambda r: (r, 0, 0)),
            pl.BlockSpec((width, width), lambda r: (0, 0)),
        ],
        out_specs=pl.BlockSpec((1, cols, width), lambda r: (r, 0, 0)),
        out_shape=jax.ShapeDtypeStruct((rows, cols, width), BF),
        compiler_params=params(),
        cost_estimate=pl.CostEstimate(
            flops=2 * rows * cols * width * width * 2,
            bytes_accessed=rows * cols * width * 4,
            transcendentals=0,
        ),
        name="attended_grad",
    )(cot, w_out)


def fill(scratch, own_ref, halo_ref):
    rows, cols, _ = own_ref.shape
    zero = jnp.zeros((rows + 2, PAD, LANES), F32)
    scratch[:, 0:PAD, :] = zero
    scratch[:, PAD + cols : 2 * PAD + cols, :] = zero
    scratch[0, PAD : PAD + cols, :] = halo_ref[0].astype(F32)
    scratch[rows + 1, PAD : PAD + cols, :] = halo_ref[1].astype(F32)
    for r in range(rows):
        scratch[r + 1, PAD : PAD + cols, :] = own_ref[r].astype(F32)


def window(scratch, r, start, shift):
    return scratch[r, pl.ds(start + (PAD + shift), STEP), :]


def conv_kernel(
    ea_ref, eb_ref, ha_ref, hb_ref, ka_ref, kb_ref, d_ref, ca_ref, cb_ref, g_ref, sum_ref, sa, sb
):
    rows, cols, _ = ea_ref.shape
    fill(sa, ea_ref, ha_ref)
    fill(sb, eb_ref, hb_ref)

    def convolve(scratch, taps_ref, start):
        total = [None] * rows
        for r in range(rows + 2):
            for j in range(3):
                v = window(scratch, r, start, j - 1)
                for i in range(3):
                    if 0 <= r - i < rows:
                        term = v * taps_ref[3 * i + j, :][None, :]
                        o = r - i
                        total[o] = term if total[o] is None else total[o] + term
        return total

    def body(t, sums):
        start = pl.multiple_of(t * STEP, STEP)
        a = convolve(sa, ka_ref, start)
        b = convolve(sb, kb_ref, start)
        pooled, weighted = sums
        for r in range(rows):
            ca_ref[r, pl.ds(start, STEP), :] = a[r].astype(BF)
            cb_ref[r, pl.ds(start, STEP), :] = b[r].astype(BF)
            g = a[r] * b[r]
            g_ref[r, pl.ds(start, STEP), :] = g.astype(BF)
            dg = g * d_ref[r, pl.ds(start, STEP), :].astype(F32)
            pooled = pooled + (g[:8] + g[8:])
            weighted = weighted + (dg[:8] + dg[8:])
        return pooled, weighted

    zero = jnp.zeros((8, LANES), F32)
    pooled, weighted = lax.fori_loop(0, cols // STEP, body, (zero, zero))
    sum_ref[0:8, :] = pooled
    sum_ref[8:16, :] = weighted


def half_specs(rows, cols, chunks):
    return [
        pl.BlockSpec((rows, cols, LANES), lambda k: (0, 0, k)),
        pl.BlockSpec((rows, cols, LANES), lambda k: (0, 0, k + chunks)),
    ]


def convolution(expanded, halo, taps, d_att):
    rows, cols, hidden = expanded.shape
    width = hidden // 2
    chunks = width // LANES
    part = pl.BlockSpec((rows, cols, LANES), lambda k: (0, 0, k))
    shape = jax.ShapeDtypeStruct((rows, cols, width), BF)
    return pl.pallas_call(
        conv_kernel,
        grid=(chunks,),
        in_specs=half_specs(rows, cols, chunks)
        + half_specs(2, cols, chunks)
        + [
            pl.BlockSpec((9, LANES), lambda k: (0, k)),
            pl.BlockSpec((9, LANES), lambda k: (0, k + chunks)),
            part,
        ],
        out_specs=[part, part, part, pl.BlockSpec((16, LANES), lambda k: (0, k))],
        out_shape=[shape, shape, shape, jax.ShapeDtypeStruct((16, width), F32)],
        scratch_shapes=[pltpu.VMEM((rows + 2, cols + 2 * PAD, LANES), F32)] * 2,
        compiler_params=params(),
        cost_estimate=pl.CostEstimate(
            flops=rows * cols * hidden * 2 * 200, bytes_accessed=rows * cols * hidden * 5, transcendentals=0
        ),
        name="convolution",
    )(expanded, expanded, halo, halo, taps, taps, d_att)


def gradient_kernel(
    ea_ref, eb_ref, ha_ref, hb_ref, ka_ref, kb_ref, ca_ref, cb_ref, d_ref, scale_ref, back_ref,
    nt_ref, nh_ref, ta_ref, tb_ref, xa_ref, xb_ref, ia_ref, ib_ref, sa, sb, da, db,
):
    rows, cols, _ = ea_ref.shape
    fill(sa, ea_ref, ha_ref)
    fill(sb, eb_ref, hb_ref)
    zero = jnp.zeros((rows, PAD, LANES), F32)
    for d in (da, db):
        d[:, 0:PAD, :] = zero
        d[:, PAD + cols : 2 * PAD + cols, :] = zero
    scale = scale_ref[...]
    back = back_ref[...]

    def products(scratch, own, start, sums):
        part = [None] * 9
        for r in range(rows + 2):
            for j in range(3):
                v = window(scratch, r, start, j - 1)
                for i in range(3):
                    if 0 <= r - i < rows:
                        term = v * own[r - i]
                        n = 3 * i + j
                        part[n] = term if part[n] is None else part[n] + term
        return tuple(s + (p[:8] + p[8:]) for s, p in zip(sums, part))

    def first(t, sums):
        start = pl.multiple_of(t * STEP, STEP)
        own_a, own_b = [], []
        for r in range(rows):
            here = (r, pl.ds(start, STEP), slice(None))
            dg = d_ref[here].astype(F32) * scale + back
            own_a.append(dg * cb_ref[here].astype(F32))
            own_b.append(dg * ca_ref[here].astype(F32))
            da[r, pl.ds(start + PAD, STEP), :] = own_a[r]
            db[r, pl.ds(start + PAD, STEP), :] = own_b[r]
        return (
            products(sa, own_a, start, sums[0]),
            products(sb, own_b, start, sums[1]),
        )

    nought = (jnp.zeros((8, LANES), F32),) * 9
    sums = lax.fori_loop(0, cols // STEP, first, (nought, nought))
    for n in range(9):
        ta_ref[8 * n : 8 * n + 8, :] = sums[0][n]
        tb_ref[8 * n : 8 * n + 8, :] = sums[1][n]

    def spread(d, taps_ref, x_ref, start):
        total = [None] * (rows + 2)
        for r in range(rows):
            for j in range(3):
                v = window(d, r, start, 1 - j)
                for i in range(3):
                    term = v * taps_ref[3 * i + j, :][None, :]
                    o = r + i
                    total[o] = term if total[o] is None else total[o] + term
        for r in range(rows + 2):
            x_ref[r, pl.ds(start, STEP), :] = total[r].astype(BF)

    def second(t, carry):
        start = pl.multiple_of(t * STEP, STEP)
        spread(da, ka_ref, xa_ref, start)
        spread(db, kb_ref, xb_ref, start)
        return carry

    lax.fori_loop(0, cols // STEP, second, 0)

    total = None
    for r in range(rows + 2):
        if r == 0:
            left = nh_ref[:, 0:cols]
        elif r == rows + 1:
            left = nh_ref[:, cols : 2 * cols]
        else:
            left = nt_ref[:, (r - 1) * cols : r * cols]
        right = jnp.concatenate([xa_ref[r], xb_ref[r]], -1)
        term = jnp.dot(left, right, preferred_element_type=F32)
        total = term if total is None else total + term
    ia_ref[0] = total[:, :LANES].astype(BF)
    ib_ref[0] = total[:, LANES:].astype(BF)


def gradients(expanded, halo, taps, conv_a, conv_b, d_att, scale, back, normed_t, halo_t):
    rows, cols, hidden = expanded.shape
    width = hidden // 2
    chunks = width // LANES
    part = pl.BlockSpec((rows, cols, LANES), lambda k: (0, 0, k))
    wide = pl.BlockSpec((rows + 2, cols, LANES), lambda k: (0, 0, k))
    line = pl.BlockSpec((1, LANES), lambda k: (0, k))
    tap = pl.BlockSpec((72, LANES), lambda k: (0, k))
    inner = pl.BlockSpec((1, width, LANES), lambda k: (k, 0, 0))
    whole = lambda a: pl.BlockSpec(a.shape, lambda k: (0, 0))
    return pl.pallas_call(
        gradient_kernel,
        grid=(chunks,),
        in_specs=half_specs(rows, cols, chunks)
        + half_specs(2, cols, chunks)
        + [
            pl.BlockSpec((9, LANES), lambda k: (0, k)),
            pl.BlockSpec((9, LANES), lambda k: (0, k + chunks)),
            part,
            part,
            part,
            line,
            line,
            whole(normed_t),
            whole(halo_t),
        ],
        out_specs=[tap, tap, wide, wide, inner, inner],
        out_shape=[jax.ShapeDtypeStruct((72, width), F32)] * 2
        + [jax.ShapeDtypeStruct((rows + 2, cols, width), BF)] * 2
        + [jax.ShapeDtypeStruct((chunks, width, LANES), BF)] * 2,
        scratch_shapes=[pltpu.VMEM((rows + 2, cols + 2 * PAD, LANES), F32)] * 2
        + [pltpu.VMEM((rows, cols + 2 * PAD, LANES), F32)] * 2,
        compiler_params=params(),
        cost_estimate=pl.CostEstimate(
            flops=rows * cols * hidden * 2 * 1500, bytes_accessed=rows * cols * hidden * 10, transcendentals=0
        ),
        name="gradients",
    )(
        expanded, expanded, halo, halo, taps, taps, conv_a, conv_b, d_att, scale, back, normed_t, halo_t
    )


def back_project(xa, xb, w_ref):
    width = xa.shape[-1]
    dims = (((1,), (1,)), ((), ()))
    return lax.dot_general(
        xa, w_ref[:, :width], dims, preferred_element_type=F32
    ) + lax.dot_general(xb, w_ref[:, width:], dims, preferred_element_type=F32)


def edge_kernel(xa_ref, xb_ref, w_ref, out_ref):
    out_ref[0] = back_project(xa_ref[0], xb_ref[0], w_ref).astype(BF)


def edge_rows(xa, xb, w_in):
    rows, cols, width = xa.shape
    spec = pl.BlockSpec((1, cols, width), lambda r: (r * (rows - 1), 0, 0))
    return pl.pallas_call(
        edge_kernel,
        grid=(2,),
        in_specs=[spec, spec, pl.BlockSpec(w_in.shape, lambda r: (0, 0))],
        out_specs=pl.BlockSpec((1, cols, width), lambda r: (r, 0, 0)),
        out_shape=jax.ShapeDtypeStruct((2, cols, width), BF),
        compiler_params=params(),
        name="edge_rows",
    )(xa, xb, w_in)


def input_kernel(x_ref, cot_ref, xa_ref, xb_ref, above_ref, below_ref, gain_ref, w_ref, out_ref):
    row = pl.program_id(0)
    last = pl.num_programs(0) - 1
    d_norm = back_project(xa_ref[0], xb_ref[0], w_ref)
    d_norm = d_norm + jnp.where(row == 0, 1.0, 0.0) * above_ref[...].astype(F32)
    d_norm = d_norm + jnp.where(row == last, 1.0, 0.0) * below_ref[...].astype(F32)
    xhat, rstd = layer_norm(x_ref[0])
    dxhat = d_norm * gain_ref[...]
    grad = cot_ref[0].astype(F32) + rstd * (
        dxhat - jnp.mean(dxhat, -1, keepdims=True) - xhat * jnp.mean(dxhat * xhat, -1, keepdims=True)
    )
    out_ref[0, 0] = grad.astype(BF)


def input_grad(x, cot, xa, xb, above, below, gain, w_in):
    rows, cols, width = x.shape
    spec = pl.BlockSpec((1, cols, width), lambda r: (r, 0, 0))
    inner = pl.BlockSpec((1, cols, width), lambda r: (r + 1, 0, 0))
    edge = pl.BlockSpec((cols, width), lambda r: (0, 0))
    return pl.pallas_call(
        input_kernel,
        grid=(rows,),
        in_specs=[
            spec,
            spec,
            inner,
            inner,
            edge,
            edge,
            pl.BlockSpec((1, width), lambda r: (0, 0)),
            pl.BlockSpec(w_in.shape, lambda r: (0, 0)),
        ],
        out_specs=pl.BlockSpec((1, 1, cols, width), lambda r: (0, r, 0, 0)),
        out_shape=jax.ShapeDtypeStruct((1, rows, cols, width), BF),
        compiler_params=params(),
        cost_estimate=pl.CostEstimate(
            flops=2 * rows * cols * width * width * 6,
            bytes_accessed=rows * cols * width * 10,
            transcendentals=0,
        ),
        name="input_grad",
    )(x, cot, xa, xb, above, below, gain, w_in)


def unpack_kernel(inner, outer, factor, me_ref, own_ref, other_ref, in_ref, out_ref, small_ref):
    g = pl.program_id(0)
    second = (g >= pl.num_programs(0) // 2).astype(jnp.int32)
    v = jnp.where(second == me_ref[0], own_ref[...].astype(F32), other_ref[...].astype(F32))

    @pl.when(g < inner)
    def _():
        in_ref[...] = v * factor

    @pl.when((g >= inner) & (g < outer))
    def _():
        out_ref[...] = v * factor

    @pl.when(g >= outer)
    def _():
        small_ref[...] = v


def unpack(own, other, me, hidden, width, factor):
    inner, outer = hidden // LANES, (hidden + width) // LANES
    groups = 2 * own.shape[0] // width
    half = pl.BlockSpec((width, LANES), lambda g: (g % (groups // 2), 0))
    clip = lambda g, low, high: jnp.minimum(jnp.maximum(g - low, 0), high - low - 1)
    return pl.pallas_call(
        functools.partial(unpack_kernel, inner, outer, factor),
        grid=(groups,),
        in_specs=[pl.BlockSpec(memory_space=pltpu.SMEM), half, half],
        out_specs=[
            pl.BlockSpec((width, LANES), lambda g: (0, clip(g, 0, inner))),
            pl.BlockSpec((width, LANES), lambda g: (0, clip(g, inner, outer))),
            pl.BlockSpec((width, LANES), lambda g: (clip(g, outer, groups), 0)),
        ],
        out_shape=[
            jax.ShapeDtypeStruct((width, hidden), F32),
            jax.ShapeDtypeStruct((width, width), F32),
            jax.ShapeDtypeStruct(((groups - outer) * width, LANES), F32),
        ],
        compiler_params=params(),
        name="unpack",
    )(me.reshape(1), own, other)


def space_neighbours(down, up):
    count = lax.axis_size("x") * lax.axis_size("zh") * lax.axis_size("y")
    forward = [(i, i + 1) for i in range(count - 1)]
    backward = [(t, s) for s, t in forward]
    axes = ("x", "zh", "y")
    return lax.ppermute(down, axes, forward), lax.ppermute(up, axes, backward)


SPACE = ("x", "zh", "y")
CHIPS = ("zl", "x", "zh", "y")


def sum_over_space(v):
    n = lax.axis_size(SPACE)
    copies = lax.optimization_barrier(jnp.broadcast_to(v[None], (n,) + v.shape))
    return jnp.sum(lax.all_to_all(copies, SPACE, 0, 0, tiled=True), 0)


def sum_over_all(v, ready):
    half = v.shape[0] // 2
    n = lax.axis_size(CHIPS)
    me = lax.axis_index("co")
    swap = [(0, 1), (1, 0)]
    other = lax.ppermute(lax.dynamic_slice_in_dim(v, (1 - me) * half, half, 0), "co", swap)
    own = lax.dynamic_slice_in_dim(v, me * half, half, 0)
    own = (own.astype(F32) + other.astype(F32)).astype(BF)
    own, ready = lax.optimization_barrier((own.reshape(n, half // n, v.shape[1]), ready))
    parts = lax.all_to_all(own, CHIPS, 0, 0, tiled=True)
    part = jnp.sum(parts.astype(F32), 0).astype(BF)
    copies = lax.optimization_barrier(jnp.broadcast_to(part[None], parts.shape))
    own = lax.all_to_all(copies, CHIPS, 0, 0, tiled=True).reshape(half, v.shape[1])
    return own, lax.ppermute(own, "co", swap), ready


def local(frames, cotangent, gain, w_in, kernel, w_att, w_out):
    x = frames[0]
    cot = cotangent[0]
    rows, cols, width = x.shape
    hidden = w_in.shape[1]
    space = lax.axis_size("x") * lax.axis_size("zh") * lax.axis_size("y")
    place = (lax.axis_index("x") * lax.axis_size("zh") + lax.axis_index("zh")) * lax.axis_size(
        "y"
    ) + lax.axis_index("y")
    frame_count = lax.axis_size("zl") * lax.axis_size("co")
    frame = lax.axis_index("zl") * lax.axis_size("co") + lax.axis_index("co")
    pixels = rows * space * cols
    factor = 1.0 / math.sqrt(frame_count * pixels)
    taps = kernel.astype(F32)
    gain = gain[None]

    above, below = space_neighbours(x[-1:], x[:1])
    normed_t, expanded = expand(x, gain, w_in)
    d_att = attended_grad(cot, w_out)
    halo_t, halo = expand(jnp.concatenate([above, below], 0), gain, w_in)
    conv_a, conv_b, gated, sums = convolution(expanded, halo, taps, d_att)
    sums = jnp.sum(sums.reshape(2, 8, width), 1)
    sums = sum_over_space(sums.reshape(8, 128)).reshape(-1)
    out_term = lax.dot_general(
        gated.reshape(-1, width),
        cot.reshape(-1, width),
        (((0,), (0,)), ((), ())),
        preferred_element_type=F32,
    )
    sums, out_term = lax.optimization_barrier((sums, out_term))
    pooled = sums[:width] / pixels
    d_scale = sums[width:]
    scale = jnp.dot(pooled, w_att, precision=lax.Precision.HIGHEST)
    back = jnp.dot(d_scale, w_att.T, precision=lax.Precision.HIGHEST) / pixels
    taps_a, taps_b, d_exp_a, d_exp_b, in_a, in_b = gradients(
        expanded, halo, taps, conv_a, conv_b, d_att, scale[None], back[None], normed_t, halo_t
    )
    kernel_term = jnp.sum(jnp.concatenate([taps_a, taps_b], -1).reshape(9, 8, hidden), 1)
    vectors = jnp.concatenate([pooled, d_scale])[None] * jnp.where(
        (jnp.arange(frame_count)[:, None] == frame) & (place == 0), 1.0, 0.0
    )
    small = jnp.concatenate([kernel_term, vectors], 0).reshape(-1, LANES)
    small = jnp.pad(small, ((0, 2 * width - small.shape[0]), (0, 0)))
    out_term = (out_term * scale[:, None]).reshape(width, width // LANES, LANES)
    payload = jnp.concatenate(
        [
            in_a.reshape(-1, LANES),
            in_b.reshape(-1, LANES),
            out_term.transpose(1, 0, 2).astype(BF).reshape(-1, LANES),
            small.astype(BF),
        ],
        0,
    )
    edges = edge_rows(d_exp_a, d_exp_b, w_in)
    own, other, edges = sum_over_all(payload, edges)
    from_above, from_below = space_neighbours(edges[1], edges[0])
    grad = input_grad(x, cot, d_exp_a, d_exp_b, from_above, from_below, gain, w_in)
    in_sum, out_sum, small = unpack(own, other, lax.axis_index("co"), hidden, width, factor)
    small = small.reshape(-1, hidden)
    vectors = small[9 : 9 + frame_count]
    att_sum = lax.dot_general(
        vectors[:, :width],
        vectors[:, width:],
        (((0,), (0,)), ((), ())),
        precision=lax.Precision.HIGHEST,
    )
    return (
        grad,
        in_sum,
        small[:9] * factor,
        att_sum * factor,
        out_sum,
    )


def solution(mesh):
    fine = Mesh(mesh.devices.reshape(2, 2, 4, 2, 4), ("zl", "co", "x", "zh", "y"))
    big = P(("zl", "co"), ("x", "zh", "y"), None, None)
    return jax.shard_map(
        local,
        mesh=fine,
        in_specs=(big, big, P(), P(), P(), P(), P()),
        out_specs=(big, P(), P(), P(), P()),
        check_vma=False,
    )
```

```python
import functools
import math

import jax
import jax.numpy as jnp
from jax import lax
from jax.experimental import pallas as pl
from jax.experimental.pallas import tpu as pltpu
from jax.sharding import Mesh, PartitionSpec as P

EPS = 1e-06
BF = jnp.bfloat16
F32 = jnp.float32
LANES = 128
STEP = 16
ACC = jnp.bfloat16
VMEM = 20 * 1024 * 1024


def params(count=1):
    return pltpu.CompilerParams(
        dimension_semantics=("arbitrary",) * count, vmem_limit_bytes=VMEM
    )


def layer_norm(x):
    xf = x.astype(F32)
    centered = xf - jnp.mean(xf, -1, keepdims=True)
    rstd = lax.rsqrt(jnp.mean(centered * centered, -1, keepdims=True) + EPS)
    return centered * rstd, rstd


def place_matrix(cols):
    place = lax.broadcasted_iota(jnp.int32, (cols, cols), 0)
    column = lax.broadcasted_iota(jnp.int32, (cols, cols), 1)
    return (column == place % STEP * (cols // STEP) + place // STEP).astype(BF)


def reorder(order, rows):
    return jnp.dot(order, rows, preferred_element_type=F32)


def neighbours(tile, first):
    zero = jnp.zeros((1, tile.shape[1]), F32)
    parts = [zero, tile[: STEP - 1]] if first else [tile[1:], zero]
    return jnp.concatenate(parts, 0).astype(BF)


def chunked(v):
    return [v[:, k * LANES : (k + 1) * LANES] for k in range(v.shape[1] // LANES)]


def expand_row(x, gain_ref, w_ref, order, normed_t_ref, expanded_ref):
    cols = x.shape[0]
    xhat, _ = layer_norm(reorder(order, x))
    normed = (xhat * gain_ref[...]).astype(BF)
    normed_t_ref[...] = normed.T
    for k, e in enumerate(chunked(jnp.dot(normed, w_ref[...], preferred_element_type=F32))):
        expanded_ref[k, 0, STEP : STEP + cols, :] = e.astype(BF)
        expanded_ref[k, 0, 0:STEP, :] = neighbours(e[cols - STEP :], True)
        expanded_ref[k, 0, STEP + cols :, :] = neighbours(e[:STEP], False)


def halo_kernel(above_ref, below_ref, gain_ref, w_ref, order_ref, normed_t_ref, expanded_ref):
    x = jnp.where(pl.program_id(0) == 0, above_ref[0].astype(F32), below_ref[0].astype(F32))
    expand_row(x.astype(BF), gain_ref, w_ref, order_ref[...], normed_t_ref, expanded_ref)


def enter_kernel(
    x_ref, gain_ref, w_ref, order_ref, cot_ref, wo_ref, normed_t_ref, expanded_ref, cot_t_ref, d_ref
):
    order = order_ref[...]
    placed = reorder(order, cot_ref[0]).astype(BF)
    cot_t_ref[...] = placed.T
    d_att = lax.dot_general(
        placed, wo_ref[...], (((1,), (1,)), ((), ())), preferred_element_type=F32
    )
    for k, d in enumerate(chunked(d_att)):
        d_ref[k, 0] = d.astype(BF)
    expand_row(x_ref[0], gain_ref, w_ref, order, normed_t_ref, expanded_ref)


def enter_specs(rows, cols, width, hidden):
    groups = hidden // LANES
    specs = [
        pl.BlockSpec((width, cols), lambda r: (0, r)),
        pl.BlockSpec((groups, 1, cols + 2 * STEP, LANES), lambda r: (0, r, 0, 0)),
    ]
    shapes = [
        jax.ShapeDtypeStruct((width, rows * cols), BF),
        jax.ShapeDtypeStruct((groups, rows, cols + 2 * STEP, LANES), BF),
    ]
    return specs, shapes


def whole(a):
    return pl.BlockSpec(a.shape, lambda r: (0,) * a.ndim)


def enter(x, gain, w_in, order, cot, w_out):
    rows, cols, width = x.shape
    chunks = width // LANES
    specs, shapes = enter_specs(rows, cols, width, w_in.shape[1])
    row = pl.BlockSpec((1, cols, width), lambda r: (r, 0, 0))
    return pl.pallas_call(
        enter_kernel,
        grid=(rows,),
        in_specs=[row, whole(gain), whole(w_in), whole(order), row, whole(w_out)],
        out_specs=specs + [specs[0], pl.BlockSpec((chunks, 1, cols, LANES), lambda r: (0, r, 0, 0))],
        out_shape=shapes + [shapes[0], jax.ShapeDtypeStruct((chunks, rows, cols, LANES), BF)],
        compiler_params=params(),
        cost_estimate=pl.CostEstimate(
            flops=2 * rows * cols * width * width * 8,
            bytes_accessed=rows * cols * width * 12,
            transcendentals=0,
        ),
        name="enter",
    )(x, gain, w_in, order, cot, w_out)


def enter_halo(above, below, gain, w_in, order):
    _, cols, width = above.shape
    specs, shapes = enter_specs(2, cols, width, w_in.shape[1])
    row = pl.BlockSpec((1, cols, width), lambda r: (0, 0, 0))
    return pl.pallas_call(
        halo_kernel,
        grid=(2,),
        in_specs=[row, row, whole(gain), whole(w_in), whole(order)],
        out_specs=specs,
        out_shape=shapes,
        compiler_params=params(),
        name="enter_halo",
    )(above, below, gain, w_in, order)


def tile(ref, r, start, shift=0):
    return ref[0, r, pl.ds(start + shift * STEP, STEP), :]


def row_tile(own_ref, halo_ref, r, start, shift):
    rows = own_ref.shape[1]
    if r == 0:
        return tile(halo_ref, 0, start, shift)
    if r == rows + 1:
        return tile(halo_ref, 1, start, shift)
    return tile(own_ref, r - 1, start, shift)


def halves(v):
    v = v.astype(F32)
    return v[: STEP // 2] + v[STEP // 2 :]


def added(total, term):
    return term if total is None else total + term


def conv_kernel(
    ea_ref, eb_ref, ha_ref, hb_ref, ka_ref, kb_ref, d_ref, ca_ref, cb_ref, g_ref, sum_ref
):
    _, rows, cols, _ = d_ref.shape

    def convolve(own_ref, halo_ref, taps_ref, start):
        total = [None] * rows
        for j in range(3):
            part = [None] * rows
            for r in range(rows + 2):
                v = row_tile(own_ref, halo_ref, r, start, j)
                for i in range(3):
                    if 0 <= r - i < rows:
                        part[r - i] = added(part[r - i], v * taps_ref[3 * i + j])
            for r in range(rows):
                total[r] = added(total[r], part[r].astype(ACC))
        return total

    def body(t, sums):
        start = pl.multiple_of(t * STEP, STEP)
        a = convolve(ea_ref, ha_ref, ka_ref, start)
        b = convolve(eb_ref, hb_ref, kb_ref, start)
        total = [None, None]
        for r in range(rows):
            here = (0, r, pl.ds(start, STEP), slice(None))
            ca_ref[here] = a[r].astype(BF)
            cb_ref[here] = b[r].astype(BF)
            g = (a[r] * b[r]).astype(BF)
            g_ref[here] = g
            total[0] = added(total[0], g)
            total[1] = added(total[1], g * d_ref[here])
        return sums[0] + halves(total[0]), sums[1] + halves(total[1])

    zero = jnp.zeros((STEP // 2, LANES), F32)
    pooled, weighted = lax.fori_loop(0, cols // STEP, body, (zero, zero), unroll=2)
    sum_ref[0:8, :] = pooled
    sum_ref[8:16, :] = weighted


def chunk_spec(shape, offset=0):
    block = (1,) + tuple(shape[1:])
    return pl.BlockSpec(block, lambda k: (k + offset,) + (0,) * (len(shape) - 1))


def half_specs(a):
    return [chunk_spec(a.shape), chunk_spec(a.shape, a.shape[0] // 2)]


def tap_specs(taps, chunks):
    block = taps.shape[:2] + (LANES,)
    return [
        pl.BlockSpec(block, lambda k: (0, 0, k)),
        pl.BlockSpec(block, lambda k: (0, 0, k + chunks)),
    ]


def convolution(expanded, halo, taps, d_att):
    chunks, rows, cols, _ = d_att.shape
    part = chunk_spec(d_att.shape)
    shape = jax.ShapeDtypeStruct(d_att.shape, BF)
    return pl.pallas_call(
        conv_kernel,
        grid=(chunks,),
        in_specs=half_specs(expanded) + half_specs(halo) + tap_specs(taps, chunks) + [part],
        out_specs=[part, part, part, pl.BlockSpec((16, LANES), lambda k: (0, k))],
        out_shape=[shape, shape, shape, jax.ShapeDtypeStruct((16, chunks * LANES), F32)],
        compiler_params=params(),
        cost_estimate=pl.CostEstimate(
            flops=d_att.size * 400, bytes_accessed=d_att.size * 14, transcendentals=0
        ),
        name="convolution",
    )(expanded, expanded, halo, halo, taps, taps, d_att)


def outer_kernel(cot_t_ref, g_ref, out_ref):
    cols = g_ref.shape[2]
    total = None
    for r in range(g_ref.shape[1]):
        left = cot_t_ref[:, r * cols : (r + 1) * cols]
        total = added(total, jnp.dot(left, g_ref[0, r], preferred_element_type=F32))
    out_ref[0] = total


def outer(cot_t, gated):
    chunks, _, _, _ = gated.shape
    shape = (chunks, cot_t.shape[0], LANES)
    return pl.pallas_call(
        outer_kernel,
        grid=(chunks,),
        in_specs=[whole(cot_t), chunk_spec(gated.shape)],
        out_specs=chunk_spec(shape),
        out_shape=jax.ShapeDtypeStruct(shape, F32),
        compiler_params=params(),
        cost_estimate=pl.CostEstimate(
            flops=2 * cot_t.shape[0] * gated.size * 2,
            bytes_accessed=gated.size * 4,
            transcendentals=0,
        ),
        name="outer",
    )(cot_t, gated)


def gradient_kernel(
    ea_ref, eb_ref, ha_ref, hb_ref, ka_ref, kb_ref, ca_ref, cb_ref, d_ref, scale_ref, back_ref,
    nt_ref, nh_ref, ta_ref, tb_ref, xa_ref, xb_ref, ia_ref, ib_ref, da, db, nt, nh, sems,
):
    _, rows, cols, _ = d_ref.shape
    scale = scale_ref[...]
    back = back_ref[...]
    copies = [
        pltpu.make_async_copy(nt_ref, nt, sems.at[0]),
        pltpu.make_async_copy(nh_ref, nh, sems.at[1]),
    ]

    @pl.when(pl.program_id(0) == 0)
    def _():
        for copy in copies:
            copy.start()

    def products(own_ref, halo_ref, own, start, sums):
        part = [None] * 9
        for r in range(rows + 2):
            for j in range(3):
                v = row_tile(own_ref, halo_ref, r, start, j)
                for i in range(3):
                    if 0 <= r - i < rows:
                        part[3 * i + j] = added(part[3 * i + j], v * own[r - i])
        return tuple(s + halves(p) for s, p in zip(sums, part))

    def first(t, sums):
        start = pl.multiple_of(t * STEP, STEP)
        own_a, own_b = [], []
        for r in range(rows):
            here = (0, r, pl.ds(start, STEP), slice(None))
            dg = (d_ref[here].astype(F32) * scale + back).astype(BF)
            own_a.append(dg * cb_ref[here])
            own_b.append(dg * ca_ref[here])
            da[0, r, pl.ds(start + STEP, STEP), :] = own_a[r]
            db[0, r, pl.ds(start + STEP, STEP), :] = own_b[r]
        return (
            products(ea_ref, ha_ref, own_a, start, sums[0]),
            products(eb_ref, hb_ref, own_b, start, sums[1]),
        )

    nought = (jnp.zeros((STEP // 2, LANES), F32),) * 9
    sums = lax.fori_loop(0, cols // STEP, first, (nought, nought))
    for n in range(9):
        ta_ref[8 * n : 8 * n + 8, :] = sums[0][n]
        tb_ref[8 * n : 8 * n + 8, :] = sums[1][n]
    for d in (da, db):
        for r in range(rows):
            d[0, r, 0:STEP, :] = neighbours(d[0, r, cols : cols + STEP, :].astype(F32), True)
            d[0, r, STEP + cols :, :] = neighbours(
                d[0, r, STEP : 2 * STEP, :].astype(F32), False
            )

    def spread(d, taps_ref, x_ref, start):
        total = [None] * (rows + 2)
        for j in range(3):
            part = [None] * (rows + 2)
            for r in range(rows):
                v = tile(d, r, start, 2 - j)
                for i in range(3):
                    part[r + i] = added(part[r + i], v * taps_ref[3 * i + j])
            for r in range(rows + 2):
                total[r] = added(total[r], part[r].astype(ACC))
        for r in range(rows + 2):
            x_ref[0, r, pl.ds(start, STEP), :] = total[r].astype(BF)

    def second(t, carry):
        start = pl.multiple_of(t * STEP, STEP)
        spread(da, ka_ref, xa_ref, start)
        spread(db, kb_ref, xb_ref, start)
        return carry

    lax.fori_loop(0, cols // STEP, second, 0, unroll=2)

    @pl.when(pl.program_id(0) == 0)
    def _():
        for copy in copies:
            copy.wait()

    total = None
    for r in range(rows + 2):
        if r == 0:
            left = nh[:, 0:cols]
        elif r == rows + 1:
            left = nh[:, cols : 2 * cols]
        else:
            left = nt[:, (r - 1) * cols : r * cols]
        right = jnp.concatenate([xa_ref[0, r], xb_ref[0, r]], -1)
        total = added(total, jnp.dot(left, right, preferred_element_type=F32))
    ia_ref[0] = total[:, :LANES].astype(BF)
    ib_ref[0] = total[:, LANES:].astype(BF)


def gradients(expanded, halo, taps, conv_a, conv_b, d_att, scale, back, normed_t, halo_t):
    chunks, rows, cols, _ = d_att.shape
    width = chunks * LANES
    part = chunk_spec(d_att.shape)
    wide = (chunks, rows + 2, cols, LANES)
    inner = (chunks, width, LANES)
    line = pl.BlockSpec((1, LANES), lambda k: (0, k))
    tap = pl.BlockSpec((72, LANES), lambda k: (0, k))
    return pl.pallas_call(
        gradient_kernel,
        grid=(chunks,),
        in_specs=half_specs(expanded)
        + half_specs(halo)
        + tap_specs(taps, chunks)
        + [part, part, part, line, line]
        + [pl.BlockSpec(memory_space=pl.ANY)] * 2,
        out_specs=[tap, tap] + [chunk_spec(wide)] * 2 + [chunk_spec(inner)] * 2,
        out_shape=[jax.ShapeDtypeStruct((72, width), F32)] * 2
        + [jax.ShapeDtypeStruct(wide, BF)] * 2
        + [jax.ShapeDtypeStruct(inner, BF)] * 2,
        scratch_shapes=[pltpu.VMEM((1, rows, cols + 2 * STEP, LANES), BF)] * 2
        + [pltpu.VMEM(normed_t.shape, BF), pltpu.VMEM(halo_t.shape, BF)]
        + [pltpu.SemaphoreType.DMA((2,))],
        compiler_params=params(),
        cost_estimate=pl.CostEstimate(
            flops=d_att.size * 3000, bytes_accessed=d_att.size * 20, transcendentals=0
        ),
        name="gradients",
    )(
        expanded, expanded, halo, halo, taps, taps, conv_a, conv_b, d_att, scale, back, normed_t, halo_t
    )


def back_project(xa_ref, xb_ref, w_ref):
    chunks = [ref[k, 0] for ref in (xa_ref, xb_ref) for k in range(ref.shape[0])]
    return lax.dot_general(
        jnp.concatenate(chunks, -1),
        w_ref[...],
        (((1,), (1,)), ((), ())),
        preferred_element_type=F32,
    )


def edge_kernel(xa_ref, xb_ref, w_ref, out_ref):
    out_ref[0] = back_project(xa_ref, xb_ref, w_ref).astype(BF)


def edge_rows(xa, xb, w_in):
    chunks, rows, cols, _ = xa.shape
    spec = pl.BlockSpec((chunks, 1, cols, LANES), lambda r: (0, r * (rows - 1), 0, 0))
    shape = (2, cols, w_in.shape[0])
    return pl.pallas_call(
        edge_kernel,
        grid=(2,),
        in_specs=[spec, spec, whole(w_in)],
        out_specs=chunk_spec(shape),
        out_shape=jax.ShapeDtypeStruct(shape, BF),
        compiler_params=params(),
        name="edge_rows",
    )(xa, xb, w_in)


def input_kernel(
    x_ref, cot_ref, xa_ref, xb_ref, above_ref, below_ref, gain_ref, w_ref, order_ref, out_ref
):
    row = pl.program_id(0)
    last = pl.num_programs(0) - 1
    d_norm = back_project(xa_ref, xb_ref, w_ref)
    d_norm = d_norm + jnp.where(row == 0, 1.0, 0.0) * above_ref[...].astype(F32)
    d_norm = d_norm + jnp.where(row == last, 1.0, 0.0) * below_ref[...].astype(F32)
    d_norm = lax.dot_general(
        order_ref[...], d_norm.astype(BF), (((0,), (0,)), ((), ())), preferred_element_type=F32
    )
    xhat, rstd = layer_norm(x_ref[0])
    dxhat = d_norm * gain_ref[...]
    grad = cot_ref[0].astype(F32) + rstd * (
        dxhat - jnp.mean(dxhat, -1, keepdims=True) - xhat * jnp.mean(dxhat * xhat, -1, keepdims=True)
    )
    out_ref[0, 0] = grad.astype(BF)


def input_grad(x, cot, xa, xb, above, below, gain, w_in, order):
    rows, cols, width = x.shape
    chunks = xa.shape[0]
    spec = pl.BlockSpec((1, cols, width), lambda r: (r, 0, 0))
    inner = pl.BlockSpec((chunks, 1, cols, LANES), lambda r: (0, r + 1, 0, 0))
    return pl.pallas_call(
        input_kernel,
        grid=(rows,),
        in_specs=[spec, spec, inner, inner]
        + [whole(a) for a in (above, below, gain, w_in, order)],
        out_specs=pl.BlockSpec((1, 1, cols, width), lambda r: (0, r, 0, 0)),
        out_shape=jax.ShapeDtypeStruct((1, rows, cols, width), BF),
        compiler_params=params(),
        cost_estimate=pl.CostEstimate(
            flops=2 * rows * cols * width * width * 6,
            bytes_accessed=rows * cols * width * 10,
            transcendentals=0,
        ),
        name="input_grad",
    )(x, cot, xa, xb, above, below, gain, w_in, order)


def unpack_kernel(factor, me_ref, own_ref, other_ref, in_ref, out_ref, att_ref, taps_ref):
    step = pl.program_id(0)
    first = me_ref[0] == 0
    own = [own_ref[g] for g in range(own_ref.shape[0])]
    other = [other_ref[g] for g in range(other_ref.shape[0])]
    group = [jnp.where(first, a.astype(F32), b.astype(F32)) for a, b in zip(own, other)]
    group += [jnp.where(first, b.astype(F32), a.astype(F32)) for a, b in zip(own, other)]
    inner = in_ref.shape[1] // LANES
    chunks = out_ref.shape[0] // LANES
    for g in range(inner):
        in_ref[:, g * LANES : (g + 1) * LANES] = group[g] * factor
    here = pl.ds(pl.multiple_of(step * LANES, LANES), LANES)
    for k in range(chunks):
        out_ref[k * LANES : (k + 1) * LANES, here] = group[inner + k].T * factor

    @pl.when(step == 0)
    def _():
        vectors = group[inner + chunks]
        taps_ref[...] = group[inner + chunks + 1][: taps_ref.shape[0]] * factor
        for k in range(chunks):
            pooled = vectors[8 * k : 8 * k + 8].astype(BF)
            for m in range(chunks):
                d_scale = vectors[8 * (chunks + m) : 8 * (chunks + m) + 8].astype(BF)
                block = lax.dot_general(
                    pooled, d_scale, (((0,), (0,)), ((), ())), preferred_element_type=F32
                )
                att_ref[k * LANES : (k + 1) * LANES, m * LANES : (m + 1) * LANES] = block * factor


def unpack(own, other, me, hidden, width, factor):
    groups = own.shape[0] // width
    own, other = (a.reshape(groups, width, LANES) for a in (own, other))
    block = pl.BlockSpec((groups, LANES, LANES), lambda s: (0, s, 0))
    full = jax.ShapeDtypeStruct((width, width), F32)
    tap_rows = 9 * hidden // LANES
    return pl.pallas_call(
        functools.partial(unpack_kernel, factor),
        grid=(width // LANES,),
        in_specs=[pl.BlockSpec(memory_space=pltpu.SMEM), block, block],
        out_specs=[
            pl.BlockSpec((LANES, hidden), lambda s: (s, 0)),
            whole(full),
            whole(full),
            pl.BlockSpec((tap_rows, LANES), lambda s: (0, 0)),
        ],
        out_shape=[
            jax.ShapeDtypeStruct((width, hidden), F32),
            full,
            full,
            jax.ShapeDtypeStruct((tap_rows, LANES), F32),
        ],
        compiler_params=params(),
        name="unpack",
    )(me.reshape(1), own, other)


def space_neighbours(down, up):
    count = lax.axis_size("x") * lax.axis_size("zh") * lax.axis_size("y")
    forward = [(i, i + 1) for i in range(count - 1)]
    backward = [(t, s) for s, t in forward]
    axes = ("x", "zh", "y")
    return lax.ppermute(down, axes, forward), lax.ppermute(up, axes, backward)


SPACE = ("x", "zh", "y")
CHIPS = ("zl", "x", "zh", "y")
SWAP = [(0, 1), (1, 0)]


def sum_over_space(v):
    n = lax.axis_size(SPACE)
    copies = lax.optimization_barrier(jnp.broadcast_to(v[None], (n,) + v.shape))
    return jnp.sum(lax.all_to_all(copies, SPACE, 0, 0, tiled=True), 0)


def sum_over_all(v, edges):
    half = v.shape[0] // 2
    n = lax.axis_size(CHIPS)
    me = lax.axis_index("co")
    other = lax.ppermute(lax.dynamic_slice_in_dim(v, (1 - me) * half, half, 0), "co", SWAP)
    own = lax.dynamic_slice_in_dim(v, me * half, half, 0)
    own = (own.astype(F32) + other.astype(F32)).astype(BF)
    own, edges = lax.optimization_barrier((own.reshape(n, half // n, v.shape[1]), edges))
    above, below = space_neighbours(edges[1], edges[0])
    parts = lax.all_to_all(own, CHIPS, 0, 0, tiled=True)
    part = jnp.sum(parts.astype(F32), 0).astype(BF)
    part, above, below = lax.optimization_barrier((part, above, below))
    copies = lax.optimization_barrier(jnp.broadcast_to(part[None], parts.shape))
    own = lax.all_to_all(copies, CHIPS, 0, 0, tiled=True).reshape(half, v.shape[1])
    return own, above, below


def local(frames, cotangent, gain, w_in, kernel, w_att, w_out):
    x = frames[0]
    cot = cotangent[0]
    rows, cols, width = x.shape
    hidden = w_in.shape[1]
    space = lax.axis_size("x") * lax.axis_size("zh") * lax.axis_size("y")
    place = (lax.axis_index("x") * lax.axis_size("zh") + lax.axis_index("zh")) * lax.axis_size(
        "y"
    ) + lax.axis_index("y")
    frame_count = lax.axis_size("zl") * lax.axis_size("co")
    frame = lax.axis_index("zl") * lax.axis_size("co") + lax.axis_index("co")
    pixels = rows * space * cols
    factor = 1.0 / math.sqrt(frame_count * pixels)
    taps = jnp.broadcast_to(kernel[:, None], (9, STEP, hidden))
    gain = gain[None]
    order = place_matrix(cols)

    above, below = space_neighbours(x[-1:], x[:1])
    normed_t, expanded, cot_t, d_att = enter(x, gain, w_in, order, cot, w_out)
    halo_t, halo = enter_halo(above, below, gain, w_in, order)
    conv_a, conv_b, gated, sums = convolution(expanded, halo, taps, d_att)
    sums = jnp.sum(sums.reshape(2, 8, width), 1)
    sums = sum_over_space(sums.reshape(8, LANES)).reshape(-1)
    out_term = outer(cot_t, gated)
    sums, out_term = lax.optimization_barrier((sums, out_term))
    pooled = sums[:width] / pixels
    d_scale = sums[width:]
    scale = jnp.dot(pooled, w_att, precision=lax.Precision.HIGHEST)
    back = jnp.dot(d_scale, w_att.T, precision=lax.Precision.HIGHEST) / pixels
    taps_a, taps_b, d_exp_a, d_exp_b, in_a, in_b = gradients(
        expanded, halo, taps, conv_a, conv_b, d_att, scale[None], back[None], normed_t, halo_t
    )
    kernel_term = jnp.sum(jnp.concatenate([taps_a, taps_b], -1).reshape(9, 8, hidden), 1)
    mine = (jnp.arange(8)[None, :, None] == frame) & (place == 0)
    vectors = jnp.where(mine, jnp.concatenate([pooled, d_scale]).reshape(-1, 1, LANES), 0.0)
    fill = lambda a: jnp.pad(a, ((0, width - a.shape[0]), (0, 0))).astype(BF)
    payload = jnp.concatenate(
        [
            in_a.reshape(-1, LANES),
            in_b.reshape(-1, LANES),
            (out_term * scale.reshape(-1, 1, LANES)).astype(BF).reshape(-1, LANES),
            fill(vectors.reshape(-1, LANES)),
            fill(kernel_term.reshape(-1, LANES)),
        ],
        0,
    )
    edges = edge_rows(d_exp_a, d_exp_b, w_in)
    own, from_above, from_below = sum_over_all(payload, edges)
    grad = input_grad(x, cot, d_exp_a, d_exp_b, from_above, from_below, gain, w_in, order)
    own, grad = lax.optimization_barrier((own, grad))
    other = lax.ppermute(own, "co", SWAP)
    in_sum, out_sum, att_sum, kernel_sum = unpack(
        own, other, lax.axis_index("co"), hidden, width, factor
    )
    return grad, in_sum, kernel_sum.reshape(9, hidden), att_sum, out_sum


def solution(mesh):
    fine = Mesh(mesh.devices.reshape(2, 2, 4, 2, 4), ("zl", "co", "x", "zh", "y"))
    big = P(("zl", "co"), ("x", "zh", "y"), None, None)
    return jax.shard_map(
        local,
        mesh=fine,
        in_specs=(big, big, P(), P(), P(), P(), P()),
        out_specs=(big, P(), P(), P(), P()),
        check_vma=False,
    )
```

```python
import functools
import math

import jax
import jax.numpy as jnp
from jax import lax
from jax.experimental import pallas as pl
from jax.experimental.pallas import tpu as pltpu
from jax.sharding import Mesh, PartitionSpec as P

EPS = 1e-06
BF = jnp.bfloat16
F32 = jnp.float32
LANES = 128
STEP = 16
VMEM = 56 * 1024 * 1024


def params(count=1):
    return pltpu.CompilerParams(
        dimension_semantics=("arbitrary",) * count, vmem_limit_bytes=VMEM
    )


def layer_norm(x):
    xf = x.astype(F32)
    centered = xf - jnp.mean(xf, -1, keepdims=True)
    rstd = lax.rsqrt(jnp.mean(centered * centered, -1, keepdims=True) + EPS)
    return centered * rstd, rstd


def place_matrix(cols):
    place = lax.broadcasted_iota(jnp.int32, (cols, cols), 0)
    column = lax.broadcasted_iota(jnp.int32, (cols, cols), 1)
    return (column == place % STEP * (cols // STEP) + place // STEP).astype(BF)


def reorder(order, rows):
    return jnp.dot(order, rows, preferred_element_type=F32)


def neighbours(tile, first):
    zero = jnp.zeros((1, tile.shape[1]), F32)
    parts = [zero, tile[: STEP - 1]] if first else [tile[1:], zero]
    return jnp.concatenate(parts, 0).astype(BF)


def chunked(v):
    return [v[:, k * LANES : (k + 1) * LANES] for k in range(v.shape[1] // LANES)]


def expand_row(x, gain_ref, w_ref, order, normed_t_ref, expanded_ref):
    cols = x.shape[0]
    xhat, _ = layer_norm(reorder(order, x))
    normed = (xhat * gain_ref[...]).astype(BF)
    normed_t_ref[...] = normed.T
    for k, e in enumerate(chunked(jnp.dot(normed, w_ref[...], preferred_element_type=F32))):
        expanded_ref[k, 0, STEP : STEP + cols, :] = e.astype(BF)
        expanded_ref[k, 0, 0:STEP, :] = neighbours(e[cols - STEP :], True)
        expanded_ref[k, 0, STEP + cols :, :] = neighbours(e[:STEP], False)


def halo_kernel(above_ref, below_ref, gain_ref, w_ref, order_ref, normed_t_ref, expanded_ref):
    x = jnp.where(pl.program_id(0) == 0, above_ref[0].astype(F32), below_ref[0].astype(F32))
    expand_row(x.astype(BF), gain_ref, w_ref, order_ref[...], normed_t_ref, expanded_ref)


def enter_kernel(
    x_ref, gain_ref, w_ref, order_ref, cot_ref, wo_ref, normed_t_ref, expanded_ref, cot_t_ref, d_ref
):
    order = order_ref[...]
    placed = reorder(order, cot_ref[0]).astype(BF)
    cot_t_ref[...] = placed.T
    d_att = lax.dot_general(
        placed, wo_ref[...], (((1,), (1,)), ((), ())), preferred_element_type=F32
    )
    for k, d in enumerate(chunked(d_att)):
        d_ref[k, 0] = d.astype(BF)
    expand_row(x_ref[0], gain_ref, w_ref, order, normed_t_ref, expanded_ref)


def enter_specs(rows, cols, width, hidden):
    groups = hidden // LANES
    specs = [
        pl.BlockSpec((width, cols), lambda r: (0, r)),
        pl.BlockSpec((groups, 1, cols + 2 * STEP, LANES), lambda r: (0, r, 0, 0)),
    ]
    shapes = [
        jax.ShapeDtypeStruct((width, rows * cols), BF),
        jax.ShapeDtypeStruct((groups, rows, cols + 2 * STEP, LANES), BF),
    ]
    return specs, shapes


def whole(a):
    return pl.BlockSpec(a.shape, lambda r: (0,) * a.ndim)


def enter(x, gain, w_in, order, cot, w_out):
    rows, cols, width = x.shape
    chunks = width // LANES
    specs, shapes = enter_specs(rows, cols, width, w_in.shape[1])
    row = pl.BlockSpec((1, cols, width), lambda r: (r, 0, 0))
    return pl.pallas_call(
        enter_kernel,
        grid=(rows,),
        in_specs=[row, whole(gain), whole(w_in), whole(order), row, whole(w_out)],
        out_specs=specs + [specs[0], pl.BlockSpec((chunks, 1, cols, LANES), lambda r: (0, r, 0, 0))],
        out_shape=shapes + [shapes[0], jax.ShapeDtypeStruct((chunks, rows, cols, LANES), BF)],
        compiler_params=params(),
        cost_estimate=pl.CostEstimate(
            flops=2 * rows * cols * width * width * 8,
            bytes_accessed=rows * cols * width * 12,
            transcendentals=0,
        ),
        name="enter",
    )(x, gain, w_in, order, cot, w_out)


def enter_halo(above, below, gain, w_in, order):
    _, cols, width = above.shape
    specs, shapes = enter_specs(2, cols, width, w_in.shape[1])
    row = pl.BlockSpec((1, cols, width), lambda r: (0, 0, 0))
    return pl.pallas_call(
        halo_kernel,
        grid=(2,),
        in_specs=[row, row, whole(gain), whole(w_in), whole(order)],
        out_specs=specs,
        out_shape=shapes,
        compiler_params=params(),
        name="enter_halo",
    )(above, below, gain, w_in, order)


def tile(ref, r, start, shift=0):
    return ref[0, r, pl.ds(start + shift * STEP, STEP), :]


def row_tile(own_ref, halo_ref, r, start, shift):
    rows = own_ref.shape[1]
    if r == 0:
        return tile(halo_ref, 0, start, shift)
    if r == rows + 1:
        return tile(halo_ref, 1, start, shift)
    return tile(own_ref, r - 1, start, shift)


def halves(v):
    v = v.astype(F32)
    return v[: STEP // 2] + v[STEP // 2 :]


def added(total, term):
    return term if total is None else total + term


def conv_kernel(
    ea_ref, eb_ref, ha_ref, hb_ref, ka_ref, kb_ref, d_ref, ca_ref, cb_ref, sum_ref
):
    _, rows, cols, _ = d_ref.shape

    def convolve(own_ref, halo_ref, taps_ref, start):
        total = [None] * rows
        for j in range(3):
            part = [None] * rows
            for r in range(rows + 2):
                v = row_tile(own_ref, halo_ref, r, start, j)
                for i in range(3):
                    if 0 <= r - i < rows:
                        part[r - i] = added(part[r - i], v * taps_ref[3 * i + j])
            for r in range(rows):
                total[r] = added(total[r], part[r].astype(F32))
        return total

    def body(t, sums):
        start = pl.multiple_of(t * STEP, STEP)
        a = convolve(ea_ref, ha_ref, ka_ref, start)
        b = convolve(eb_ref, hb_ref, kb_ref, start)
        total = [None, None]
        for r in range(rows):
            here = (0, r, pl.ds(start, STEP), slice(None))
            ca_ref[here] = a[r].astype(BF)
            cb_ref[here] = b[r].astype(BF)
            g = (a[r] * b[r]).astype(BF)
            total[0] = added(total[0], g)
            total[1] = added(total[1], g * d_ref[here])
        return sums[0] + halves(total[0]), sums[1] + halves(total[1])

    zero = jnp.zeros((STEP // 2, LANES), F32)
    pooled, weighted = lax.fori_loop(0, cols // STEP, body, (zero, zero), unroll=2)
    sum_ref[0:8, :] = pooled
    sum_ref[8:16, :] = weighted


def chunk_spec(shape, offset=0):
    block = (1,) + tuple(shape[1:])
    return pl.BlockSpec(block, lambda k: (k + offset,) + (0,) * (len(shape) - 1))


def half_specs(a):
    return [chunk_spec(a.shape), chunk_spec(a.shape, a.shape[0] // 2)]


def tap_specs(taps, chunks):
    block = taps.shape[:2] + (LANES,)
    return [
        pl.BlockSpec(block, lambda k: (0, 0, k)),
        pl.BlockSpec(block, lambda k: (0, 0, k + chunks)),
    ]


def convolution(expanded, halo, taps, d_att):
    chunks, rows, cols, _ = d_att.shape
    part = chunk_spec(d_att.shape)
    shape = jax.ShapeDtypeStruct(d_att.shape, BF)
    return pl.pallas_call(
        conv_kernel,
        grid=(chunks,),
        in_specs=half_specs(expanded) + half_specs(halo) + tap_specs(taps, chunks) + [part],
        out_specs=[part, part, pl.BlockSpec((16, LANES), lambda k: (0, k))],
        out_shape=[shape, shape, jax.ShapeDtypeStruct((16, chunks * LANES), F32)],
        compiler_params=params(),
        cost_estimate=pl.CostEstimate(
            flops=d_att.size * 400, bytes_accessed=d_att.size * 14, transcendentals=0
        ),
        name="convolution",
    )(expanded, expanded, halo, halo, taps, taps, d_att)


def outer_kernel(cot_t_ref, ca_ref, cb_ref, out_ref):
    cols = ca_ref.shape[2]
    total = None
    for r in range(ca_ref.shape[1]):
        left = cot_t_ref[:, r * cols : (r + 1) * cols]
        gated = ca_ref[0, r] * cb_ref[0, r]
        total = added(total, jnp.dot(left, gated, preferred_element_type=F32))
    out_ref[0] = total


def outer(cot_t, conv_a, conv_b):
    chunks = conv_a.shape[0]
    shape = (chunks, cot_t.shape[0], LANES)
    return pl.pallas_call(
        outer_kernel,
        grid=(chunks,),
        in_specs=[whole(cot_t), chunk_spec(conv_a.shape), chunk_spec(conv_b.shape)],
        out_specs=chunk_spec(shape),
        out_shape=jax.ShapeDtypeStruct(shape, F32),
        compiler_params=params(),
        cost_estimate=pl.CostEstimate(
            flops=2 * cot_t.shape[0] * conv_a.size * 2,
            bytes_accessed=conv_a.size * 4,
            transcendentals=0,
        ),
        name="outer",
    )(cot_t, conv_a, conv_b)


def gradient_kernel(
    ea_ref, eb_ref, ha_ref, hb_ref, ka_ref, kb_ref, ca_ref, cb_ref, d_ref, scale_ref, back_ref,
    nt_ref, nh_ref, ta_ref, tb_ref, xa_ref, xb_ref, ia_ref, ib_ref, da, db, nt, nh, sems,
):
    _, rows, cols, _ = d_ref.shape
    scale = scale_ref[...]
    back = back_ref[...]
    copies = [
        pltpu.make_async_copy(nt_ref, nt, sems.at[0]),
        pltpu.make_async_copy(nh_ref, nh, sems.at[1]),
    ]

    @pl.when(pl.program_id(0) == 0)
    def _():
        for copy in copies:
            copy.start()

    def products(own_ref, halo_ref, own, start, sums):
        part = [None] * 9
        for r in range(rows + 2):
            for j in range(3):
                v = row_tile(own_ref, halo_ref, r, start, j)
                for i in range(3):
                    if 0 <= r - i < rows:
                        part[3 * i + j] = added(part[3 * i + j], v * own[r - i])
        return tuple(s + halves(p) for s, p in zip(sums, part))

    def first(t, sums):
        start = pl.multiple_of(t * STEP, STEP)
        own_a, own_b = [], []
        for r in range(rows):
            here = (0, r, pl.ds(start, STEP), slice(None))
            dg = (d_ref[here].astype(F32) * scale + back).astype(BF)
            own_a.append(dg * cb_ref[here])
            own_b.append(dg * ca_ref[here])
            da[0, r, pl.ds(start + STEP, STEP), :] = own_a[r]
            db[0, r, pl.ds(start + STEP, STEP), :] = own_b[r]
        return (
            products(ea_ref, ha_ref, own_a, start, sums[0]),
            products(eb_ref, hb_ref, own_b, start, sums[1]),
        )

    nought = (jnp.zeros((STEP // 2, LANES), F32),) * 9
    sums = lax.fori_loop(0, cols // STEP, first, (nought, nought))
    for n in range(9):
        ta_ref[8 * n : 8 * n + 8, :] = sums[0][n]
        tb_ref[8 * n : 8 * n + 8, :] = sums[1][n]
    for d in (da, db):
        for r in range(rows):
            d[0, r, 0:STEP, :] = neighbours(d[0, r, cols : cols + STEP, :].astype(F32), True)
            d[0, r, STEP + cols :, :] = neighbours(
                d[0, r, STEP : 2 * STEP, :].astype(F32), False
            )

    def spread(d, taps_ref, x_ref, start):
        total = [None] * (rows + 2)
        for j in range(3):
            part = [None] * (rows + 2)
            for r in range(rows):
                v = tile(d, r, start, 2 - j)
                for i in range(3):
                    part[r + i] = added(part[r + i], v * taps_ref[3 * i + j])
            for r in range(rows + 2):
                total[r] = added(total[r], part[r])
        for r in range(rows + 2):
            x_ref[0, r, pl.ds(start, STEP), :] = total[r].astype(BF)

    def second(t, carry):
        start = pl.multiple_of(t * STEP, STEP)
        spread(da, ka_ref, xa_ref, start)
        spread(db, kb_ref, xb_ref, start)
        return carry

    lax.fori_loop(0, cols // STEP, second, 0, unroll=2)

    @pl.when(pl.program_id(0) == 0)
    def _():
        for copy in copies:
            copy.wait()

    total = None
    for r in range(rows + 2):
        if r == 0:
            left = nh[:, 0:cols]
        elif r == rows + 1:
            left = nh[:, cols : 2 * cols]
        else:
            left = nt[:, (r - 1) * cols : r * cols]
        right = jnp.concatenate([xa_ref[0, r], xb_ref[0, r]], -1)
        total = added(total, jnp.dot(left, right, preferred_element_type=F32))
    ia_ref[0] = total[:, :LANES].astype(BF)
    ib_ref[0] = total[:, LANES:].astype(BF)


def gradients(expanded, halo, taps, conv_a, conv_b, d_att, scale, back, normed_t, halo_t):
    chunks, rows, cols, _ = d_att.shape
    width = chunks * LANES
    part = chunk_spec(d_att.shape)
    wide = (chunks, rows + 2, cols, LANES)
    inner = (chunks, width, LANES)
    line = pl.BlockSpec((1, LANES), lambda k: (0, k))
    tap = pl.BlockSpec((72, LANES), lambda k: (0, k))
    return pl.pallas_call(
        gradient_kernel,
        grid=(chunks,),
        in_specs=half_specs(expanded)
        + half_specs(halo)
        + tap_specs(taps, chunks)
        + [part, part, part, line, line]
        + [pl.BlockSpec(memory_space=pl.ANY)] * 2,
        out_specs=[tap, tap] + [chunk_spec(wide)] * 2 + [chunk_spec(inner)] * 2,
        out_shape=[jax.ShapeDtypeStruct((72, width), F32)] * 2
        + [jax.ShapeDtypeStruct(wide, BF)] * 2
        + [jax.ShapeDtypeStruct(inner, BF)] * 2,
        scratch_shapes=[pltpu.VMEM((1, rows, cols + 2 * STEP, LANES), BF)] * 2
        + [pltpu.VMEM(normed_t.shape, BF), pltpu.VMEM(halo_t.shape, BF)]
        + [pltpu.SemaphoreType.DMA((2,))],
        compiler_params=params(),
        cost_estimate=pl.CostEstimate(
            flops=d_att.size * 3000, bytes_accessed=d_att.size * 20, transcendentals=0
        ),
        name="gradients",
    )(
        expanded, expanded, halo, halo, taps, taps, conv_a, conv_b, d_att, scale, back, normed_t, halo_t
    )


def back_project(xa_ref, xb_ref, w_ref):
    chunks = [ref[k, 0] for ref in (xa_ref, xb_ref) for k in range(ref.shape[0])]
    return lax.dot_general(
        jnp.concatenate(chunks, -1),
        w_ref[...],
        (((1,), (1,)), ((), ())),
        preferred_element_type=F32,
    )


def edge_kernel(ca_ref, cb_ref, d_ref, scale_ref, back_ref, taps_ref, w_ref, out_ref):
    side = pl.program_id(0)
    chunks, _, cols, _ = d_ref.shape
    spread = [None] * (2 * chunks)
    for k in range(chunks):
        dg = (d_ref[k, 0].astype(F32) * scale_ref[k] + back_ref[k]).astype(BF)
        for n, ref in ((k, cb_ref), (chunks + k, ca_ref)):
            d = dg * ref[k, 0]
            before = neighbours(d[cols - STEP :].astype(F32), True)
            behind = neighbours(d[:STEP].astype(F32), False)
            windows = (
                jnp.concatenate([d[STEP:], behind], 0),
                d,
                jnp.concatenate([before, d[: cols - STEP]], 0),
            )
            total = None
            for j in range(3):
                tap = taps_ref[6 * side + j, :, n * LANES : (n + 1) * LANES]
                total = added(total, windows[j].reshape(-1, STEP, LANES) * tap[None])
            spread[n] = total.reshape(cols, LANES)
    out_ref[0] = lax.dot_general(
        jnp.concatenate(spread, -1),
        w_ref[...],
        (((1,), (1,)), ((), ())),
        preferred_element_type=F32,
    ).astype(BF)


def edge_rows(conv_a, conv_b, d_att, scale, back, taps, w_in):
    chunks, rows, cols, _ = d_att.shape
    spec = pl.BlockSpec((chunks, 1, cols, LANES), lambda r: (0, r * (rows - 1), 0, 0))
    shape = (2, cols, w_in.shape[0])
    return pl.pallas_call(
        edge_kernel,
        grid=(2,),
        in_specs=[spec, spec, spec] + [whole(a) for a in (scale, back, taps, w_in)],
        out_specs=chunk_spec(shape),
        out_shape=jax.ShapeDtypeStruct(shape, BF),
        compiler_params=params(),
        name="edge_rows",
    )(conv_a, conv_b, d_att, scale, back, taps, w_in)


def input_kernel(
    x_ref, cot_ref, xa_ref, xb_ref, above_ref, below_ref, gain_ref, w_ref, order_ref, out_ref
):
    row = pl.program_id(0)
    last = pl.num_programs(0) - 1
    d_norm = back_project(xa_ref, xb_ref, w_ref)
    d_norm = d_norm + jnp.where(row == 0, 1.0, 0.0) * above_ref[...].astype(F32)
    d_norm = d_norm + jnp.where(row == last, 1.0, 0.0) * below_ref[...].astype(F32)
    d_norm = lax.dot_general(
        order_ref[...], d_norm.astype(BF), (((0,), (0,)), ((), ())), preferred_element_type=F32
    )
    xhat, rstd = layer_norm(x_ref[0])
    dxhat = d_norm * gain_ref[...]
    grad = cot_ref[0].astype(F32) + rstd * (
        dxhat - jnp.mean(dxhat, -1, keepdims=True) - xhat * jnp.mean(dxhat * xhat, -1, keepdims=True)
    )
    out_ref[0, 0] = grad.astype(BF)


def input_grad(x, cot, xa, xb, above, below, gain, w_in, order):
    rows, cols, width = x.shape
    chunks = xa.shape[0]
    spec = pl.BlockSpec((1, cols, width), lambda r: (r, 0, 0))
    inner = pl.BlockSpec((chunks, 1, cols, LANES), lambda r: (0, r + 1, 0, 0))
    return pl.pallas_call(
        input_kernel,
        grid=(rows,),
        in_specs=[spec, spec, inner, inner]
        + [whole(a) for a in (above, below, gain, w_in, order)],
        out_specs=pl.BlockSpec((1, 1, cols, width), lambda r: (0, r, 0, 0)),
        out_shape=jax.ShapeDtypeStruct((1, rows, cols, width), BF),
        compiler_params=params(),
        cost_estimate=pl.CostEstimate(
            flops=2 * rows * cols * width * width * 6,
            bytes_accessed=rows * cols * width * 10,
            transcendentals=0,
        ),
        name="input_grad",
    )(x, cot, xa, xb, above, below, gain, w_in, order)


def unpack_kernel(factor, me_ref, own_ref, other_ref, in_ref, out_ref, att_ref, taps_ref):
    step = pl.program_id(0)
    first = me_ref[0] == 0
    own = [own_ref[g] for g in range(own_ref.shape[0])]
    other = [other_ref[g] for g in range(other_ref.shape[0])]
    group = [jnp.where(first, a.astype(F32), b.astype(F32)) for a, b in zip(own, other)]
    group += [jnp.where(first, b.astype(F32), a.astype(F32)) for a, b in zip(own, other)]
    inner = in_ref.shape[1] // LANES
    chunks = out_ref.shape[0] // LANES
    for g in range(inner):
        in_ref[:, g * LANES : (g + 1) * LANES] = group[g] * factor
    here = pl.ds(pl.multiple_of(step * LANES, LANES), LANES)
    for k in range(chunks):
        out_ref[k * LANES : (k + 1) * LANES, here] = group[inner + k].T * factor

    @pl.when(step == 0)
    def _():
        vectors = group[inner + chunks]
        taps_ref[...] = group[inner + chunks + 1][: taps_ref.shape[0]] * factor
        for k in range(chunks):
            pooled = vectors[8 * k : 8 * k + 8].astype(BF)
            for m in range(chunks):
                d_scale = vectors[8 * (chunks + m) : 8 * (chunks + m) + 8].astype(BF)
                block = lax.dot_general(
                    pooled, d_scale, (((0,), (0,)), ((), ())), preferred_element_type=F32
                )
                att_ref[k * LANES : (k + 1) * LANES, m * LANES : (m + 1) * LANES] = block * factor


def unpack(own, other, me, hidden, width, factor):
    groups = own.shape[0] // width
    own, other = (a.reshape(groups, width, LANES) for a in (own, other))
    block = pl.BlockSpec((groups, LANES, LANES), lambda s: (0, s, 0))
    full = jax.ShapeDtypeStruct((width, width), F32)
    tap_rows = 9 * hidden // LANES
    return pl.pallas_call(
        functools.partial(unpack_kernel, factor),
        grid=(width // LANES,),
        in_specs=[pl.BlockSpec(memory_space=pltpu.SMEM), block, block],
        out_specs=[
            pl.BlockSpec((LANES, hidden), lambda s: (s, 0)),
            whole(full),
            whole(full),
            pl.BlockSpec((tap_rows, LANES), lambda s: (0, 0)),
        ],
        out_shape=[
            jax.ShapeDtypeStruct((width, hidden), F32),
            full,
            full,
            jax.ShapeDtypeStruct((tap_rows, LANES), F32),
        ],
        compiler_params=params(),
        name="unpack",
    )(me.reshape(1), own, other)


def space_neighbours(down, up):
    count = lax.axis_size("x") * lax.axis_size("zh") * lax.axis_size("y")
    forward = [(i, i + 1) for i in range(count - 1)]
    backward = [(t, s) for s, t in forward]
    axes = ("x", "zh", "y")
    return lax.ppermute(down, axes, forward), lax.ppermute(up, axes, backward)


SPACE = ("x", "zh", "y")
CHIPS = ("zl", "x", "zh", "y")
SWAP = [(0, 1), (1, 0)]


def sum_over_space(v):
    n = lax.axis_size(SPACE)
    copies = lax.optimization_barrier(jnp.broadcast_to(v[None], (n,) + v.shape))
    return jnp.sum(lax.all_to_all(copies, SPACE, 0, 0, tiled=True), 0)


def sum_over_all(v, later):
    half = v.shape[0] // 2
    n = lax.axis_size(CHIPS)
    me = lax.axis_index("co")
    other = lax.ppermute(lax.dynamic_slice_in_dim(v, (1 - me) * half, half, 0), "co", SWAP)
    own = lax.dynamic_slice_in_dim(v, me * half, half, 0)
    own = (own.astype(F32) + other.astype(F32)).astype(BF)
    own = lax.optimization_barrier(own.reshape(n, half // n, v.shape[1]))
    parts = lax.all_to_all(own, CHIPS, 0, 0, tiled=True)
    part = jnp.sum(parts.astype(F32), 0).astype(BF)
    part, later = lax.optimization_barrier((part, later))
    copies = lax.optimization_barrier(jnp.broadcast_to(part[None], parts.shape))
    return lax.all_to_all(copies, CHIPS, 0, 0, tiled=True).reshape(half, v.shape[1]), later


def local(frames, cotangent, gain, w_in, kernel, w_att, w_out):
    x = frames[0]
    cot = cotangent[0]
    rows, cols, width = x.shape
    hidden = w_in.shape[1]
    space = lax.axis_size("x") * lax.axis_size("zh") * lax.axis_size("y")
    place = (lax.axis_index("x") * lax.axis_size("zh") + lax.axis_index("zh")) * lax.axis_size(
        "y"
    ) + lax.axis_index("y")
    frame_count = lax.axis_size("zl") * lax.axis_size("co")
    frame = lax.axis_index("zl") * lax.axis_size("co") + lax.axis_index("co")
    pixels = rows * space * cols
    factor = 1.0 / math.sqrt(frame_count * pixels)
    taps = jnp.broadcast_to(kernel[:, None], (9, STEP, hidden))
    gain = gain[None]
    order = place_matrix(cols)

    above, below = space_neighbours(x[-1:], x[:1])
    normed_t, expanded, cot_t, d_att = enter(x, gain, w_in, order, cot, w_out)
    halo_t, halo = enter_halo(above, below, gain, w_in, order)
    conv_a, conv_b, sums = convolution(expanded, halo, taps, d_att)
    sums = jnp.sum(sums.reshape(2, 8, width), 1)
    sums = sum_over_space(sums.reshape(8, LANES)).reshape(-1)
    out_term = outer(cot_t, conv_a, conv_b)
    sums, out_term = lax.optimization_barrier((sums, out_term))
    pooled = sums[:width] / pixels
    d_scale = sums[width:]
    scale = jnp.dot(pooled, w_att, precision=lax.Precision.HIGHEST)
    back = jnp.dot(d_scale, w_att.T, precision=lax.Precision.HIGHEST) / pixels
    edges = edge_rows(
        conv_a, conv_b, d_att, scale.reshape(-1, 1, LANES), back.reshape(-1, 1, LANES), taps, w_in
    )
    from_above, from_below = space_neighbours(edges[1], edges[0])
    taps_a, taps_b, d_exp_a, d_exp_b, in_a, in_b = gradients(
        expanded, halo, taps, conv_a, conv_b, d_att, scale[None], back[None], normed_t, halo_t
    )
    in_a, in_b, from_above, from_below = lax.optimization_barrier(
        (in_a, in_b, from_above, from_below)
    )
    kernel_term = jnp.sum(jnp.concatenate([taps_a, taps_b], -1).reshape(9, 8, hidden), 1)
    mine = (jnp.arange(8)[None, :, None] == frame) & (place == 0)
    vectors = jnp.where(mine, jnp.concatenate([pooled, d_scale]).reshape(-1, 1, LANES), 0.0)
    fill = lambda a: jnp.pad(a, ((0, width - a.shape[0]), (0, 0))).astype(BF)
    payload = jnp.concatenate(
        [
            in_a.reshape(-1, LANES),
            in_b.reshape(-1, LANES),
            (out_term * scale.reshape(-1, 1, LANES)).astype(BF).reshape(-1, LANES),
            fill(vectors.reshape(-1, LANES)),
            fill(kernel_term.reshape(-1, LANES)),
        ],
        0,
    )
    own, (from_above, from_below) = sum_over_all(payload, (from_above, from_below))
    grad = input_grad(x, cot, d_exp_a, d_exp_b, from_above, from_below, gain, w_in, order)
    own, grad = lax.optimization_barrier((own, grad))
    other = lax.ppermute(own, "co", SWAP)
    in_sum, out_sum, att_sum, kernel_sum = unpack(
        own, other, lax.axis_index("co"), hidden, width, factor
    )
    return grad, in_sum, kernel_sum.reshape(9, hidden), att_sum, out_sum


def solution(mesh):
    fine = Mesh(mesh.devices.reshape(2, 2, 4, 2, 4), ("zl", "co", "x", "zh", "y"))
    big = P(("zl", "co"), ("x", "zh", "y"), None, None)
    return jax.shard_map(
        local,
        mesh=fine,
        in_specs=(big, big, P(), P(), P(), P(), P()),
        out_specs=(big, P(), P(), P(), P()),
        check_vma=False,
    )
```

```python
import functools
import math

import jax
import jax.numpy as jnp
import numpy as np
from jax import lax
from jax.experimental import pallas as pl
from jax.experimental.pallas import tpu as pltpu
from jax.sharding import Mesh, PartitionSpec as P

EPS = 1e-06
BF = jnp.bfloat16
F32 = jnp.float32
LANES = 128
STEP = 16
VMEM = 56 * 1024 * 1024


def params(count=1):
    return pltpu.CompilerParams(
        dimension_semantics=("arbitrary",) * count, vmem_limit_bytes=VMEM
    )


def layer_norm(x):
    xf = x.astype(F32)
    centered = xf - jnp.mean(xf, -1, keepdims=True)
    rstd = lax.rsqrt(jnp.mean(centered * centered, -1, keepdims=True) + EPS)
    return centered * rstd, rstd


def place_matrix(cols):
    place = np.arange(cols)[:, None]
    column = np.arange(cols)[None]
    return jnp.asarray(column == place % STEP * (cols // STEP) + place // STEP, BF)


def reorder(order, rows):
    return jnp.dot(order, rows, preferred_element_type=F32)


def neighbours(tile, first):
    zero = jnp.zeros((1, tile.shape[1]), F32)
    parts = [zero, tile[: STEP - 1]] if first else [tile[1:], zero]
    return jnp.concatenate(parts, 0)


def chunked(v):
    return [v[:, k * LANES : (k + 1) * LANES] for k in range(v.shape[1] // LANES)]


def tiled(v):
    return v.reshape(-1, STEP, LANES)


def flat(v):
    return v.reshape(-1, LANES)


def expand_row(x, gain_ref, w_ref, order, normed_t_ref, expanded_ref):
    cols = x.shape[0]
    xhat, _ = layer_norm(reorder(order, x))
    normed = (xhat * gain_ref[...]).astype(BF)
    normed_t_ref[...] = normed.T
    for k, e in enumerate(chunked(jnp.dot(normed, w_ref[...], preferred_element_type=F32))):
        expanded_ref[k, 0, 1 : 1 + cols // STEP] = tiled(e.astype(BF))
        expanded_ref[k, 0, 0] = neighbours(e[cols - STEP :], True).astype(BF)
        expanded_ref[k, 0, 1 + cols // STEP] = neighbours(e[:STEP], False).astype(BF)


def halo_kernel(above_ref, below_ref, gain_ref, w_ref, order_ref, normed_t_ref, expanded_ref):
    x = jnp.where(pl.program_id(0) == 0, above_ref[0].astype(F32), below_ref[0].astype(F32))
    expand_row(x.astype(BF), gain_ref, w_ref, order_ref[...], normed_t_ref, expanded_ref)


def enter_kernel(
    x_ref, gain_ref, w_ref, order_ref, cot_ref, wo_ref, normed_t_ref, expanded_ref, cot_t_ref, d_ref
):
    order = order_ref[...]
    placed = reorder(order, cot_ref[0]).astype(BF)
    cot_t_ref[...] = placed.T
    d_att = lax.dot_general(
        placed, wo_ref[...], (((1,), (1,)), ((), ())), preferred_element_type=F32
    )
    for k, d in enumerate(chunked(d_att)):
        d_ref[k, 0] = tiled(d.astype(BF))
    expand_row(x_ref[0], gain_ref, w_ref, order, normed_t_ref, expanded_ref)


def enter_specs(rows, cols, width, hidden):
    groups, tiles = hidden // LANES, cols // STEP
    specs = [
        pl.BlockSpec((width, cols), lambda r: (0, r)),
        pl.BlockSpec((groups, 1, tiles + 2, STEP, LANES), lambda r: (0, r, 0, 0, 0)),
    ]
    shapes = [
        jax.ShapeDtypeStruct((width, rows * cols), BF),
        jax.ShapeDtypeStruct((groups, rows, tiles + 2, STEP, LANES), BF),
    ]
    return specs, shapes


def whole(a):
    return pl.BlockSpec(a.shape, lambda r: (0,) * a.ndim)


def enter(x, gain, w_in, order, cot, w_out):
    rows, cols, width = x.shape
    chunks = width // LANES
    specs, shapes = enter_specs(rows, cols, width, w_in.shape[1])
    row = pl.BlockSpec((1, cols, width), lambda r: (r, 0, 0))
    return pl.pallas_call(
        enter_kernel,
        grid=(rows,),
        in_specs=[row, whole(gain), whole(w_in), whole(order), row, whole(w_out)],
        out_specs=specs
        + [specs[0], pl.BlockSpec((chunks, 1, cols // STEP, STEP, LANES), lambda r: (0, r, 0, 0, 0))],
        out_shape=shapes
        + [shapes[0], jax.ShapeDtypeStruct((chunks, rows, cols // STEP, STEP, LANES), BF)],
        compiler_params=params(),
        cost_estimate=pl.CostEstimate(
            flops=2 * rows * cols * width * width * 8,
            bytes_accessed=rows * cols * width * 12,
            transcendentals=0,
        ),
        name="enter",
    )(x, gain, w_in, order, cot, w_out)


def enter_halo(above, below, gain, w_in, order):
    _, cols, width = above.shape
    specs, shapes = enter_specs(2, cols, width, w_in.shape[1])
    row = pl.BlockSpec((1, cols, width), lambda r: (0, 0, 0))
    return pl.pallas_call(
        halo_kernel,
        grid=(2,),
        in_specs=[row, row, whole(gain), whole(w_in), whole(order)],
        out_specs=specs,
        out_shape=shapes,
        compiler_params=params(),
        name="enter_halo",
    )(above, below, gain, w_in, order)


def row_tile(own_ref, halo_ref, r, t):
    rows = own_ref.shape[1]
    if r == 0:
        return halo_ref[0, 0, t]
    if r == rows + 1:
        return halo_ref[0, 1, t]
    return own_ref[0, r - 1, t]


def halves(v):
    return v[: STEP // 2] + v[STEP // 2 :]


def added(total, term):
    return term if total is None else total + term


def conv_kernel(
    ea_ref, eb_ref, ha_ref, hb_ref, ka_ref, kb_ref, d_ref, ca_ref, cb_ref, sum_ref
):
    _, rows, tiles, _, _ = d_ref.shape
    taps_a = [ka_ref[n].astype(F32) for n in range(9)]
    taps_b = [kb_ref[n].astype(F32) for n in range(9)]

    def convolve(own_ref, halo_ref, taps, t):
        total = [None] * rows
        for r in range(rows + 2):
            for j in range(3):
                v = row_tile(own_ref, halo_ref, r, t + j).astype(F32)
                for i in range(3):
                    if 0 <= r - i < rows:
                        total[r - i] = added(total[r - i], v * taps[3 * i + j])
        return total

    def body(t, sums):
        a = convolve(ea_ref, ha_ref, taps_a, t)
        b = convolve(eb_ref, hb_ref, taps_b, t)
        total = [None, None]
        for r in range(rows):
            here = (0, r, t)
            ca_ref[here] = a[r].astype(BF)
            cb_ref[here] = b[r].astype(BF)
            g = a[r] * b[r]
            total[0] = added(total[0], g)
            total[1] = added(total[1], g * d_ref[here].astype(F32))
        return sums[0] + halves(total[0]), sums[1] + halves(total[1])

    zero = jnp.zeros((STEP // 2, LANES), F32)
    pooled, weighted = lax.fori_loop(0, tiles, body, (zero, zero), unroll=1)
    sum_ref[0:8, :] = pooled
    sum_ref[8:16, :] = weighted


def chunk_spec(shape, offset=0):
    block = (1,) + tuple(shape[1:])
    return pl.BlockSpec(block, lambda k: (k + offset,) + (0,) * (len(shape) - 1))


def half_specs(a):
    return [chunk_spec(a.shape), chunk_spec(a.shape, a.shape[0] // 2)]


def tap_specs(taps, chunks):
    block = taps.shape[:2] + (LANES,)
    return [
        pl.BlockSpec(block, lambda k: (0, 0, k)),
        pl.BlockSpec(block, lambda k: (0, 0, k + chunks)),
    ]


def convolution(expanded, halo, taps, d_att):
    chunks = d_att.shape[0]
    part = chunk_spec(d_att.shape)
    shape = jax.ShapeDtypeStruct(d_att.shape, BF)
    return pl.pallas_call(
        conv_kernel,
        grid=(chunks,),
        in_specs=half_specs(expanded) + half_specs(halo) + tap_specs(taps, chunks) + [part],
        out_specs=[part, part, pl.BlockSpec((16, LANES), lambda k: (0, k))],
        out_shape=[shape, shape, jax.ShapeDtypeStruct((16, chunks * LANES), F32)],
        compiler_params=params(),
        cost_estimate=pl.CostEstimate(
            flops=d_att.size * 400, bytes_accessed=d_att.size * 14, transcendentals=0
        ),
        name="convolution",
    )(expanded, expanded, halo, halo, taps, taps, d_att)


def outer_kernel(cot_t_ref, ca_ref, cb_ref, out_ref):
    cols = ca_ref.shape[2] * STEP
    total = None
    for r in range(ca_ref.shape[1]):
        left = cot_t_ref[:, r * cols : (r + 1) * cols]
        gated = flat((ca_ref[0, r].astype(F32) * cb_ref[0, r].astype(F32)).astype(BF))
        total = added(total, jnp.dot(left, gated, preferred_element_type=F32))
    out_ref[0] = total


def outer(cot_t, conv_a, conv_b):
    chunks = conv_a.shape[0]
    shape = (chunks, cot_t.shape[0], LANES)
    return pl.pallas_call(
        outer_kernel,
        grid=(chunks,),
        in_specs=[whole(cot_t), chunk_spec(conv_a.shape), chunk_spec(conv_b.shape)],
        out_specs=chunk_spec(shape),
        out_shape=jax.ShapeDtypeStruct(shape, F32),
        compiler_params=params(),
        cost_estimate=pl.CostEstimate(
            flops=2 * cot_t.shape[0] * conv_a.size * 2,
            bytes_accessed=conv_a.size * 4,
            transcendentals=0,
        ),
        name="outer",
    )(cot_t, conv_a, conv_b)


def gradient_kernel(
    ea_ref, eb_ref, ha_ref, hb_ref, ka_ref, kb_ref, ca_ref, cb_ref, d_ref, scale_ref, back_ref,
    nt_ref, nh_ref, ta_ref, tb_ref, xa_ref, xb_ref, ia_ref, ib_ref, da, db, nt, nh, sems,
):
    _, rows, tiles, _, _ = d_ref.shape
    cols = tiles * STEP
    scale = jnp.broadcast_to(scale_ref[...], (STEP, LANES))
    back = jnp.broadcast_to(back_ref[...], (STEP, LANES))
    copies = [
        pltpu.make_async_copy(nt_ref, nt, sems.at[0]),
        pltpu.make_async_copy(nh_ref, nh, sems.at[1]),
    ]

    @pl.when(pl.program_id(0) == 0)
    def _():
        for copy in copies:
            copy.start()

    def products(own_ref, halo_ref, own, t, sums):
        part = [None] * 9
        for r in range(rows + 2):
            for j in range(3):
                v = row_tile(own_ref, halo_ref, r, t + j).astype(F32)
                for i in range(3):
                    if 0 <= r - i < rows:
                        part[3 * i + j] = added(part[3 * i + j], v * own[r - i])
        return tuple(s + halves(p) for s, p in zip(sums, part))

    def first(own_ref, halo_ref, other_ref, d, t, sums):
        own = []
        for r in range(rows):
            dg = d_ref[0, r, t].astype(F32) * scale + back
            own.append(dg * other_ref[0, r, t].astype(F32))
            d[r, t + 1] = own[r].astype(BF)
        return products(own_ref, halo_ref, own, t, sums)

    nought = (jnp.zeros((STEP // 2, LANES), F32),) * 9
    sums = [
        lax.fori_loop(0, tiles, functools.partial(first, *refs), nought, unroll=2)
        for refs in ((ea_ref, ha_ref, cb_ref, da), (eb_ref, hb_ref, ca_ref, db))
    ]
    for n in range(9):
        ta_ref[8 * n : 8 * n + 8, :] = sums[0][n]
        tb_ref[8 * n : 8 * n + 8, :] = sums[1][n]
    for d in (da, db):
        for r in range(rows):
            d[r, 0] = neighbours(d[r, tiles].astype(F32), True).astype(BF)
            d[r, tiles + 1] = neighbours(d[r, 1].astype(F32), False).astype(BF)

    taps_a = [ka_ref[n].astype(F32) for n in range(9)]
    taps_b = [kb_ref[n].astype(F32) for n in range(9)]

    def spread(d, taps, x_ref, t):
        total = [None] * (rows + 2)
        for r in range(rows):
            for j in range(3):
                v = d[r, t + 2 - j].astype(F32)
                for i in range(3):
                    total[r + i] = added(total[r + i], v * taps[3 * i + j])
        for r in range(rows + 2):
            x_ref[0, r, t] = total[r].astype(BF)

    for d, taps, x_ref in ((da, taps_a, xa_ref), (db, taps_b, xb_ref)):

        def second(t, carry, d=d, taps=taps, x_ref=x_ref):
            spread(d, taps, x_ref, t)
            return carry

        lax.fori_loop(0, tiles, second, 0, unroll=1)

    @pl.when(pl.program_id(0) == 0)
    def _():
        for copy in copies:
            copy.wait()

    total = None
    for r in range(rows + 2):
        if r == 0:
            left = nh[:, 0:cols]
        elif r == rows + 1:
            left = nh[:, cols : 2 * cols]
        else:
            left = nt[:, (r - 1) * cols : r * cols]
        right = jnp.concatenate([flat(xa_ref[0, r]), flat(xb_ref[0, r])], -1)
        total = added(total, jnp.dot(left, right, preferred_element_type=F32))
    ia_ref[0] = total[:, :LANES].astype(BF)
    ib_ref[0] = total[:, LANES:].astype(BF)


def gradients(expanded, halo, taps, conv_a, conv_b, d_att, scale, back, normed_t, halo_t):
    chunks, rows, tiles, _, _ = d_att.shape
    width = chunks * LANES
    part = chunk_spec(d_att.shape)
    wide = (chunks, rows + 2, tiles, STEP, LANES)
    inner = (chunks, width, LANES)
    line = pl.BlockSpec((1, LANES), lambda k: (0, k))
    tap = pl.BlockSpec((72, LANES), lambda k: (0, k))
    return pl.pallas_call(
        gradient_kernel,
        grid=(chunks,),
        in_specs=half_specs(expanded)
        + half_specs(halo)
        + tap_specs(taps, chunks)
        + [part, part, part, line, line]
        + [pl.BlockSpec(memory_space=pl.ANY)] * 2,
        out_specs=[tap, tap] + [chunk_spec(wide)] * 2 + [chunk_spec(inner)] * 2,
        out_shape=[jax.ShapeDtypeStruct((72, width), F32)] * 2
        + [jax.ShapeDtypeStruct(wide, BF)] * 2
        + [jax.ShapeDtypeStruct(inner, BF)] * 2,
        scratch_shapes=[pltpu.VMEM((rows, tiles + 2, STEP, LANES), BF)] * 2
        + [pltpu.VMEM(normed_t.shape, BF), pltpu.VMEM(halo_t.shape, BF)]
        + [pltpu.SemaphoreType.DMA((2,))],
        compiler_params=params(),
        cost_estimate=pl.CostEstimate(
            flops=d_att.size * 3000, bytes_accessed=d_att.size * 20, transcendentals=0
        ),
        name="gradients",
    )(
        expanded, expanded, halo, halo, taps, taps, conv_a, conv_b, d_att, scale, back, normed_t, halo_t
    )


def back_project(xa_ref, xb_ref, w_ref):
    chunks = [flat(ref[k, 0]) for ref in (xa_ref, xb_ref) for k in range(ref.shape[0])]
    return lax.dot_general(
        jnp.concatenate(chunks, -1),
        w_ref[...],
        (((1,), (1,)), ((), ())),
        preferred_element_type=F32,
    )


def edge_kernel(
    ca_ref, cb_ref, d_ref, scale_ref, back_ref, taps_ref, w_ref, above_ref, below_ref
):
    side = pl.program_id(0)
    chunks = d_ref.shape[0]
    spread = [None] * (2 * chunks)
    for k in range(chunks):
        dg = d_ref[k, 0].astype(F32) * scale_ref[k] + back_ref[k]
        for n, ref in ((k, cb_ref), (chunks + k, ca_ref)):
            d = dg * ref[k, 0].astype(F32)
            before = neighbours(d[-1], True)[None]
            behind = neighbours(d[0], False)[None]
            windows = (
                jnp.concatenate([d[1:], behind], 0),
                d,
                jnp.concatenate([before, d[:-1]], 0),
            )
            total = None
            for j in range(3):
                tap = taps_ref[6 * side + j, :, n * LANES : (n + 1) * LANES].astype(F32)
                total = added(total, windows[j] * tap[None])
            spread[n] = flat(total.astype(BF))
    row = lax.dot_general(
        jnp.concatenate(spread, -1),
        w_ref[...],
        (((1,), (1,)), ((), ())),
        preferred_element_type=F32,
    ).astype(BF)

    @pl.when(side == 0)
    def _():
        above_ref[...] = row

    @pl.when(side == 1)
    def _():
        below_ref[...] = row


def edge_rows(conv_a, conv_b, d_att, scale, back, taps, w_in):
    chunks, rows, tiles, _, _ = d_att.shape
    spec = pl.BlockSpec(
        (chunks, 1, tiles, STEP, LANES), lambda r: (0, r * (rows - 1), 0, 0, 0)
    )
    out = jax.ShapeDtypeStruct((tiles * STEP, w_in.shape[0]), BF)
    return pl.pallas_call(
        edge_kernel,
        grid=(2,),
        in_specs=[spec, spec, spec] + [whole(a) for a in (scale, back, taps, w_in)],
        out_specs=[whole(out)] * 2,
        out_shape=[out] * 2,
        compiler_params=params(),
        name="edge_rows",
    )(conv_a, conv_b, d_att, scale, back, taps, w_in)


def input_kernel(
    x_ref, cot_ref, xa_ref, xb_ref, above_ref, below_ref, gain_ref, w_ref, order_ref, out_ref
):
    row = pl.program_id(0)
    last = pl.num_programs(0) - 1
    d_norm = back_project(xa_ref, xb_ref, w_ref)
    d_norm = d_norm + jnp.where(row == 0, 1.0, 0.0) * above_ref[...].astype(F32)
    d_norm = d_norm + jnp.where(row == last, 1.0, 0.0) * below_ref[...].astype(F32)
    d_norm = lax.dot_general(
        order_ref[...], d_norm.astype(BF), (((0,), (0,)), ((), ())), preferred_element_type=F32
    )
    xhat, rstd = layer_norm(x_ref[0])
    dxhat = d_norm * gain_ref[...]
    grad = cot_ref[0].astype(F32) + rstd * (
        dxhat - jnp.mean(dxhat, -1, keepdims=True) - xhat * jnp.mean(dxhat * xhat, -1, keepdims=True)
    )
    out_ref[0, 0] = grad.astype(BF)


def input_grad(x, cot, xa, xb, above, below, gain, w_in, order):
    rows, cols, width = x.shape
    chunks = xa.shape[0]
    spec = pl.BlockSpec((1, cols, width), lambda r: (r, 0, 0))
    inner = pl.BlockSpec(
        (chunks, 1, cols // STEP, STEP, LANES), lambda r: (0, r + 1, 0, 0, 0)
    )
    return pl.pallas_call(
        input_kernel,
        grid=(rows,),
        in_specs=[spec, spec, inner, inner]
        + [whole(a) for a in (above, below, gain, w_in, order)],
        out_specs=pl.BlockSpec((1, 1, cols, width), lambda r: (0, r, 0, 0)),
        out_shape=jax.ShapeDtypeStruct((1, rows, cols, width), BF),
        compiler_params=params(),
        cost_estimate=pl.CostEstimate(
            flops=2 * rows * cols * width * width * 6,
            bytes_accessed=rows * cols * width * 10,
            transcendentals=0,
        ),
        name="input_grad",
    )(x, cot, xa, xb, above, below, gain, w_in, order)


def unpack_kernel(factor, me_ref, own_ref, other_ref, in_ref, out_ref, att_ref, taps_ref):
    step = pl.program_id(0)
    first = me_ref[0] == 0
    own = [own_ref[g] for g in range(own_ref.shape[0])]
    other = [other_ref[g] for g in range(other_ref.shape[0])]
    group = [jnp.where(first, a.astype(F32), b.astype(F32)) for a, b in zip(own, other)]
    group += [jnp.where(first, b.astype(F32), a.astype(F32)) for a, b in zip(own, other)]
    inner = in_ref.shape[1] // LANES
    chunks = out_ref.shape[0] // LANES
    for g in range(inner):
        in_ref[:, g * LANES : (g + 1) * LANES] = group[g] * factor
    here = pl.ds(pl.multiple_of(step * LANES, LANES), LANES)
    for k in range(chunks):
        out_ref[k * LANES : (k + 1) * LANES, here] = group[inner + k].T * factor

    @pl.when(step == 0)
    def _():
        vectors = group[inner + chunks]
        taps = group[inner + chunks + 1][: 9 * inner] * factor
        for n in range(9):
            for g in range(inner):
                taps_ref[n : n + 1, g * LANES : (g + 1) * LANES] = taps[n * inner + g][None]
        for k in range(chunks):
            pooled = vectors[8 * k : 8 * k + 8].astype(BF)
            for m in range(chunks):
                d_scale = vectors[8 * (chunks + m) : 8 * (chunks + m) + 8].astype(BF)
                block = lax.dot_general(
                    pooled, d_scale, (((0,), (0,)), ((), ())), preferred_element_type=F32
                )
                att_ref[k * LANES : (k + 1) * LANES, m * LANES : (m + 1) * LANES] = block * factor


def unpack(own, other, me, hidden, width, factor):
    groups = own.shape[0] // width
    own, other = (a.reshape(groups, width, LANES) for a in (own, other))
    block = pl.BlockSpec((groups, LANES, LANES), lambda s: (0, s, 0))
    full = jax.ShapeDtypeStruct((width, width), F32)
    return pl.pallas_call(
        functools.partial(unpack_kernel, factor),
        grid=(width // LANES,),
        in_specs=[pl.BlockSpec(memory_space=pltpu.SMEM), block, block],
        out_specs=[
            pl.BlockSpec((LANES, hidden), lambda s: (s, 0)),
            whole(full),
            whole(full),
            pl.BlockSpec((9, hidden), lambda s: (0, 0)),
        ],
        out_shape=[
            jax.ShapeDtypeStruct((width, hidden), F32),
            full,
            full,
            jax.ShapeDtypeStruct((9, hidden), F32),
        ],
        compiler_params=params(),
        name="unpack",
    )(me.reshape(1), own, other)


def space_neighbours(down, up):
    count = lax.axis_size("x") * lax.axis_size("zh") * lax.axis_size("y")
    forward = [(i, i + 1) for i in range(count - 1)]
    backward = [(t, s) for s, t in forward]
    axes = ("x", "zh", "y")
    return lax.ppermute(down, axes, forward), lax.ppermute(up, axes, backward)


SPACE = ("x", "zh", "y")
CHIPS = ("zl", "x", "zh", "y")
SWAP = [(0, 1), (1, 0)]


def sum_over_space(v):
    n = lax.axis_size(SPACE)
    copies = lax.optimization_barrier(jnp.broadcast_to(v[None], (n,) + v.shape))
    return jnp.sum(lax.all_to_all(copies, SPACE, 0, 0, tiled=True), 0)


def sum_over_all(v, later):
    half = v.shape[0] // 2
    n = lax.axis_size(CHIPS)
    me = lax.axis_index("co")
    other = lax.ppermute(lax.dynamic_slice_in_dim(v, (1 - me) * half, half, 0), "co", SWAP)
    own = lax.dynamic_slice_in_dim(v, me * half, half, 0)
    own = (own.astype(F32) + other.astype(F32)).astype(BF)
    own = lax.optimization_barrier(own.reshape(n, half // n, v.shape[1]))
    parts = lax.all_to_all(own, CHIPS, 0, 0, tiled=True)
    part = jnp.sum(parts.astype(F32), 0).astype(BF)
    part, later = lax.optimization_barrier((part, later))
    copies = lax.optimization_barrier(jnp.broadcast_to(part[None], parts.shape))
    return lax.all_to_all(copies, CHIPS, 0, 0, tiled=True).reshape(half, v.shape[1]), later


def local(frames, cotangent, gain, w_in, kernel, w_att, w_out):
    x = frames[0]
    cot = cotangent[0]
    rows, cols, width = x.shape
    hidden = w_in.shape[1]
    space = lax.axis_size("x") * lax.axis_size("zh") * lax.axis_size("y")
    place = (lax.axis_index("x") * lax.axis_size("zh") + lax.axis_index("zh")) * lax.axis_size(
        "y"
    ) + lax.axis_index("y")
    frame_count = lax.axis_size("zl") * lax.axis_size("co")
    frame = lax.axis_index("zl") * lax.axis_size("co") + lax.axis_index("co")
    pixels = rows * space * cols
    factor = 1.0 / math.sqrt(frame_count * pixels)
    taps = jnp.broadcast_to(kernel[:, None], (9, STEP, hidden))
    gain = gain[None]
    order = place_matrix(cols)

    above, below = space_neighbours(x[-1:], x[:1])
    normed_t, expanded, cot_t, d_att = enter(x, gain, w_in, order, cot, w_out)
    halo_t, halo = enter_halo(above, below, gain, w_in, order)
    conv_a, conv_b, sums = convolution(expanded, halo, taps, d_att)
    sums = jnp.sum(sums.reshape(2, 8, width), 1)
    sums = sum_over_space(sums.reshape(8, LANES)).reshape(-1)
    out_term = outer(cot_t, conv_a, conv_b)
    sums, out_term = lax.optimization_barrier((sums, out_term))
    pooled = sums[:width] / pixels
    d_scale = sums[width:]
    scale = jnp.dot(pooled, w_att, precision=lax.Precision.HIGHEST)
    back = jnp.dot(d_scale, w_att.T, precision=lax.Precision.HIGHEST) / pixels
    to_above, to_below = edge_rows(
        conv_a, conv_b, d_att, scale.reshape(-1, 1, LANES), back.reshape(-1, 1, LANES), taps, w_in
    )
    from_above, from_below = space_neighbours(to_below, to_above)
    taps_a, taps_b, d_exp_a, d_exp_b, in_a, in_b = gradients(
        expanded, halo, taps, conv_a, conv_b, d_att, scale[None], back[None], normed_t, halo_t
    )
    in_a, in_b, from_above, from_below = lax.optimization_barrier(
        (in_a, in_b, from_above, from_below)
    )
    kernel_term = jnp.sum(jnp.concatenate([taps_a, taps_b], -1).reshape(9, 8, hidden), 1)
    mine = (jnp.arange(8)[None, :, None] == frame) & (place == 0)
    vectors = jnp.where(mine, jnp.concatenate([pooled, d_scale]).reshape(-1, 1, LANES), 0.0)
    fill = lambda a: jnp.pad(a, ((0, width - a.shape[0]), (0, 0))).astype(BF)
    payload = jnp.concatenate(
        [
            in_a.reshape(-1, LANES),
            in_b.reshape(-1, LANES),
            (out_term * scale.reshape(-1, 1, LANES)).astype(BF).reshape(-1, LANES),
            fill(vectors.reshape(-1, LANES)),
            fill(kernel_term.reshape(-1, LANES)),
        ],
        0,
    )
    own, (from_above, from_below) = sum_over_all(payload, (from_above, from_below))
    grad = input_grad(x, cot, d_exp_a, d_exp_b, from_above, from_below, gain, w_in, order)
    own, grad = lax.optimization_barrier((own, grad))
    other = lax.ppermute(own, "co", SWAP)
    in_sum, out_sum, att_sum, kernel_sum = unpack(
        own, other, lax.axis_index("co"), hidden, width, factor
    )
    return grad, in_sum, kernel_sum, att_sum, out_sum


def solution(mesh):
    fine = Mesh(mesh.devices.reshape(2, 2, 4, 2, 4), ("zl", "co", "x", "zh", "y"))
    big = P(("zl", "co"), ("x", "zh", "y"), None, None)
    return jax.shard_map(
        local,
        mesh=fine,
        in_specs=(big, big, P(), P(), P(), P(), P()),
        out_specs=(big, P(), P(), P(), P()),
        check_vma=False,
    )
```

```python
import functools
import math

import jax
import jax.numpy as jnp
import numpy as np
from jax import lax
from jax.experimental import pallas as pl
from jax.experimental.pallas import tpu as pltpu
from jax.sharding import Mesh, PartitionSpec as P

EPS = 1e-06
BF = jnp.bfloat16
F32 = jnp.float32
LANES = 128
STEP = 16
SMALL = 48
VMEM = 56 * 1024 * 1024


def params(vmem=VMEM):
    return pltpu.CompilerParams(dimension_semantics=("arbitrary",), vmem_limit_bytes=vmem)


def layer_norm(x):
    xf = x.astype(F32)
    centered = xf - jnp.mean(xf, -1, keepdims=True)
    rstd = lax.rsqrt(jnp.mean(centered * centered, -1, keepdims=True) + EPS)
    return centered * rstd, rstd


def place_matrix(cols):
    place = np.arange(cols)[:, None]
    column = np.arange(cols)[None]
    return jnp.asarray(column == place % STEP * (cols // STEP) + place // STEP, BF)


def reorder(order, rows):
    return jnp.dot(order, rows, preferred_element_type=F32)


def neighbours(tile, first):
    zero = jnp.zeros((1, tile.shape[1]), F32)
    parts = [zero, tile[: STEP - 1]] if first else [tile[1:], zero]
    return jnp.concatenate(parts, 0)


def chunked(v):
    return [v[:, k * LANES : (k + 1) * LANES] for k in range(v.shape[1] // LANES)]


def tiled(v):
    return v.reshape(-1, STEP, LANES)


def flat(v):
    return v.reshape(-1, LANES)


def expand_row(x, gain_ref, w_ref, order, normed_t_ref, expanded_ref, r=0):
    cols = x.shape[0]
    xhat, _ = layer_norm(reorder(order, x))
    normed = (xhat * gain_ref[...]).astype(BF)
    normed_t_ref[:, r * cols : (r + 1) * cols] = normed.T
    for k, e in enumerate(chunked(jnp.dot(normed, w_ref[...], preferred_element_type=F32))):
        expanded_ref[k, r, 1 : 1 + cols // STEP] = tiled(e.astype(BF))
        expanded_ref[k, r, 0] = neighbours(e[cols - STEP :], True).astype(BF)
        expanded_ref[k, r, 1 + cols // STEP] = neighbours(e[:STEP], False).astype(BF)


def halo_kernel(above_ref, below_ref, gain_ref, w_ref, order_ref, normed_t_ref, expanded_ref):
    x = jnp.where(pl.program_id(0) == 0, above_ref[0].astype(F32), below_ref[0].astype(F32))
    expand_row(x.astype(BF), gain_ref, w_ref, order_ref[...], normed_t_ref, expanded_ref)


def enter_kernel(
    x_ref, gain_ref, w_ref, order_ref, cot_ref, wo_ref, normed_t_ref, expanded_ref, cot_t_ref, d_ref
):
    order = order_ref[...]
    placed = reorder(order, cot_ref[0]).astype(BF)
    cot_t_ref[...] = placed.T
    d_att = lax.dot_general(
        placed, wo_ref[...], (((1,), (1,)), ((), ())), preferred_element_type=F32
    )
    for k, d in enumerate(chunked(d_att)):
        d_ref[k, 0] = tiled(d.astype(BF))
    expand_row(x_ref[0], gain_ref, w_ref, order, normed_t_ref, expanded_ref)


def enter_specs(rows, cols, width, hidden):
    groups, tiles = hidden // LANES, cols // STEP
    specs = [
        pl.BlockSpec((width, cols), lambda r: (0, r)),
        pl.BlockSpec((groups, 1, tiles + 2, STEP, LANES), lambda r: (0, r, 0, 0, 0)),
    ]
    shapes = [
        jax.ShapeDtypeStruct((width, rows * cols), BF),
        jax.ShapeDtypeStruct((groups, rows, tiles + 2, STEP, LANES), BF),
    ]
    return specs, shapes


def whole(a):
    return pl.BlockSpec(a.shape, lambda r: (0,) * a.ndim)


def enter(x, gain, w_in, order, cot, w_out):
    rows, cols, width = x.shape
    chunks = width // LANES
    specs, shapes = enter_specs(rows, cols, width, w_in.shape[1])
    row = pl.BlockSpec((1, cols, width), lambda r: (r, 0, 0))
    return pl.pallas_call(
        enter_kernel,
        grid=(rows,),
        in_specs=[row, whole(gain), whole(w_in), whole(order), row, whole(w_out)],
        out_specs=specs
        + [specs[0], pl.BlockSpec((chunks, 1, cols // STEP, STEP, LANES), lambda r: (0, r, 0, 0, 0))],
        out_shape=shapes
        + [shapes[0], jax.ShapeDtypeStruct((chunks, rows, cols // STEP, STEP, LANES), BF)],
        compiler_params=params(),
        cost_estimate=pl.CostEstimate(
            flops=2 * rows * cols * width * width * 8,
            bytes_accessed=rows * cols * width * 12,
            transcendentals=0,
        ),
        name="enter",
    )(x, gain, w_in, order, cot, w_out)


def enter_halo(above, below, gain, w_in, order):
    _, cols, width = above.shape
    specs, shapes = enter_specs(2, cols, width, w_in.shape[1])
    row = pl.BlockSpec((1, cols, width), lambda r: (0, 0, 0))
    return pl.pallas_call(
        halo_kernel,
        grid=(2,),
        in_specs=[row, row, whole(gain), whole(w_in), whole(order)],
        out_specs=specs,
        out_shape=shapes,
        compiler_params=params(),
        name="enter_halo",
    )(above, below, gain, w_in, order)


def row_tile(own_ref, halo_ref, r, t):
    rows = own_ref.shape[1]
    if r == 0:
        return halo_ref[0, 0, t]
    if r == rows + 1:
        return halo_ref[0, 1, t]
    return own_ref[0, r - 1, t]


def halves(v):
    return v[: STEP // 2] + v[STEP // 2 :]


def added(total, term):
    return term if total is None else total + term


def conv_kernel(
    ea_ref, eb_ref, ha_ref, hb_ref, ka_ref, kb_ref, d_ref, ca_ref, cb_ref, sum_ref
):
    _, rows, tiles, _, _ = d_ref.shape
    taps_a = [ka_ref[n].astype(F32) for n in range(9)]
    taps_b = [kb_ref[n].astype(F32) for n in range(9)]

    def convolve(own_ref, halo_ref, taps, t):
        total = [None] * rows
        for r in range(rows + 2):
            for j in range(3):
                v = row_tile(own_ref, halo_ref, r, t + j).astype(F32)
                for i in range(3):
                    if 0 <= r - i < rows:
                        total[r - i] = added(total[r - i], v * taps[3 * i + j])
        return total

    def body(t, sums):
        a = convolve(ea_ref, ha_ref, taps_a, t)
        b = convolve(eb_ref, hb_ref, taps_b, t)
        total = [None, None]
        for r in range(rows):
            here = (0, r, t)
            ca_ref[here] = a[r].astype(BF)
            cb_ref[here] = b[r].astype(BF)
            g = a[r] * b[r]
            total[0] = added(total[0], g)
            total[1] = added(total[1], g * d_ref[here].astype(F32))
        return sums[0] + halves(total[0]), sums[1] + halves(total[1])

    zero = jnp.zeros((STEP // 2, LANES), F32)
    pooled, weighted = lax.fori_loop(0, tiles, body, (zero, zero), unroll=1)
    sum_ref[0:8, :] = pooled
    sum_ref[8:16, :] = weighted


def chunk_spec(shape, offset=0):
    block = (1,) + tuple(shape[1:])
    return pl.BlockSpec(block, lambda k: (k + offset,) + (0,) * (len(shape) - 1))


def half_specs(a):
    return [chunk_spec(a.shape), chunk_spec(a.shape, a.shape[0] // 2)]


def tap_specs(taps, chunks):
    block = taps.shape[:2] + (LANES,)
    return [
        pl.BlockSpec(block, lambda k: (0, 0, k)),
        pl.BlockSpec(block, lambda k: (0, 0, k + chunks)),
    ]


def convolution(expanded, halo, taps, d_att):
    chunks = d_att.shape[0]
    part = chunk_spec(d_att.shape)
    shape = jax.ShapeDtypeStruct(d_att.shape, BF)
    return pl.pallas_call(
        conv_kernel,
        grid=(chunks,),
        in_specs=half_specs(expanded) + half_specs(halo) + tap_specs(taps, chunks) + [part],
        out_specs=[part, part, pl.BlockSpec((16, LANES), lambda k: (0, k))],
        out_shape=[shape, shape, jax.ShapeDtypeStruct((16, chunks * LANES), F32)],
        compiler_params=params(),
        cost_estimate=pl.CostEstimate(
            flops=d_att.size * 400, bytes_accessed=d_att.size * 14, transcendentals=0
        ),
        name="convolution",
    )(expanded, expanded, halo, halo, taps, taps, d_att)


def outer_kernel(cot_t_ref, ca_ref, cb_ref, out_ref):
    cols = ca_ref.shape[2] * STEP
    total = None
    for r in range(ca_ref.shape[1]):
        left = cot_t_ref[:, r * cols : (r + 1) * cols]
        gated = flat((ca_ref[0, r].astype(F32) * cb_ref[0, r].astype(F32)).astype(BF))
        total = added(total, jnp.dot(left, gated, preferred_element_type=F32))
    out_ref[0] = total


def outer(cot_t, conv_a, conv_b):
    chunks = conv_a.shape[0]
    shape = (chunks, cot_t.shape[0], LANES)
    return pl.pallas_call(
        outer_kernel,
        grid=(chunks,),
        in_specs=[whole(cot_t), chunk_spec(conv_a.shape), chunk_spec(conv_b.shape)],
        out_specs=chunk_spec(shape),
        out_shape=jax.ShapeDtypeStruct(shape, F32),
        compiler_params=params(),
        cost_estimate=pl.CostEstimate(
            flops=2 * cot_t.shape[0] * conv_a.size * 2,
            bytes_accessed=conv_a.size * 4,
            transcendentals=0,
        ),
        name="outer",
    )(cot_t, conv_a, conv_b)


def gradient_kernel(
    me_ref, ea_ref, eb_ref, ha_ref, hb_ref, ka_ref, kb_ref, ca_ref, cb_ref, d_ref, scale_ref, back_ref,
    out_ref, vec_ref, nt_ref, nh_ref, xa_ref, xb_ref, send_ref, keep_ref, da, db, nt, nh, sems,
):
    _, rows, tiles, _, _ = d_ref.shape
    cols = tiles * STEP
    scale = jnp.broadcast_to(scale_ref[...], (STEP, LANES))
    back = jnp.broadcast_to(back_ref[...], (STEP, LANES))
    copies = [
        pltpu.make_async_copy(nt_ref, nt, sems.at[0]),
        pltpu.make_async_copy(nh_ref, nh, sems.at[1]),
    ]

    @pl.when(pl.program_id(0) == 0)
    def _():
        for copy in copies:
            copy.start()

    def products(own_ref, halo_ref, own, t, sums):
        part = [None] * 9
        for r in range(rows + 2):
            for j in range(3):
                v = row_tile(own_ref, halo_ref, r, t + j).astype(F32)
                for i in range(3):
                    if 0 <= r - i < rows:
                        part[3 * i + j] = added(part[3 * i + j], v * own[r - i])
        return tuple(s + halves(p) for s, p in zip(sums, part))

    def first(own_ref, halo_ref, other_ref, d, t, sums):
        own = []
        for r in range(rows):
            dg = d_ref[0, r, t].astype(F32) * scale + back
            own.append(dg * other_ref[0, r, t].astype(F32))
            d[r, t + 1] = own[r].astype(BF)
        return products(own_ref, halo_ref, own, t, sums)

    nought = (jnp.zeros((STEP // 2, LANES), F32),) * 9
    sums = [
        lax.fori_loop(0, tiles, functools.partial(first, *refs), nought, unroll=2)
        for refs in ((ea_ref, ha_ref, cb_ref, da), (eb_ref, hb_ref, ca_ref, db))
    ]
    for d in (da, db):
        for r in range(rows):
            d[r, 0] = neighbours(d[r, tiles].astype(F32), True).astype(BF)
            d[r, tiles + 1] = neighbours(d[r, 1].astype(F32), False).astype(BF)

    taps_a = [ka_ref[n].astype(F32) for n in range(9)]
    taps_b = [kb_ref[n].astype(F32) for n in range(9)]

    def spread(d, taps, x_ref, t):
        total = [None] * (rows + 2)
        for r in range(rows):
            for j in range(3):
                v = d[r, t + 2 - j].astype(F32)
                for i in range(3):
                    total[r + i] = added(total[r + i], v * taps[3 * i + j])
        for r in range(rows + 2):
            x_ref[0, r, t] = total[r].astype(BF)

    for d, taps, x_ref in ((da, taps_a, xa_ref), (db, taps_b, xb_ref)):

        def second(t, carry, d=d, taps=taps, x_ref=x_ref):
            spread(d, taps, x_ref, t)
            return carry

        lax.fori_loop(0, tiles, second, 0, unroll=1)

    @pl.when(pl.program_id(0) == 0)
    def _():
        for copy in copies:
            copy.wait()

    total = None
    for r in range(rows + 2):
        if r == 0:
            left = nh[:, 0:cols]
        elif r == rows + 1:
            left = nh[:, cols : 2 * cols]
        else:
            left = nt[:, (r - 1) * cols : r * cols]
        right = jnp.concatenate([flat(xa_ref[0, r]), flat(xb_ref[0, r])], -1)
        total = added(total, jnp.dot(left, right, preferred_element_type=F32))
    width = total.shape[0]
    blank = jnp.zeros((7, LANES), F32)
    rows_of = lambda part: [jnp.sum(p, 0, keepdims=True) for p in part]
    small = jnp.concatenate([vec_ref[0], *rows_of(sums[0]), blank, *rows_of(sums[1]), blank], 0)

    def write(ref):
        ref[0, 0:width] = total[:, :LANES].astype(BF)
        ref[0, width : 2 * width] = total[:, LANES:].astype(BF)
        ref[0, 2 * width : 3 * width] = (out_ref[0] * scale_ref[...]).astype(BF)
        ref[0, 3 * width : 3 * width + SMALL] = small.astype(BF)
        ref[0, 3 * width + SMALL :] = jnp.zeros((width // 2 - SMALL, LANES), BF)

    early = pl.program_id(0) < pl.num_programs(0) // 2
    pl.when(early)(lambda: write(send_ref))
    pl.when(jnp.logical_not(early))(lambda: write(keep_ref))


def gradients(
    me, expanded, halo, taps, conv_a, conv_b, d_att, scale, back, out_term, vectors, normed_t, halo_t
):
    chunks, rows, tiles, _, _ = d_att.shape
    width = chunks * LANES
    half = chunks // 2
    chunk = lambda s, me: (s + half * (1 - me[0])) % chunks

    def by_chunk(a, offset=0):
        block = (1,) + tuple(a.shape[1:])
        return pl.BlockSpec(block, lambda s, me: (chunk(s, me) + offset,) + (0,) * (len(block) - 1))

    def by_half(a):
        return [by_chunk(a), by_chunk(a, chunks)]

    def lanes(a, offset=0):
        block = a.shape[:-1] + (LANES,)
        return pl.BlockSpec(
            block, lambda s, me: (0,) * (len(block) - 1) + (chunk(s, me) + offset,)
        )

    spread = jax.ShapeDtypeStruct((chunks, rows + 2, tiles, STEP, LANES), BF)
    part = jax.ShapeDtypeStruct((half, 7 * width // 2, LANES), BF)
    block = (1,) + part.shape[1:]
    return pl.pallas_call(
        gradient_kernel,
        grid_spec=pltpu.PrefetchScalarGridSpec(
            num_scalar_prefetch=1,
            grid=(chunks,),
            in_specs=by_half(expanded)
            + by_half(halo)
            + [lanes(taps), lanes(taps, chunks)]
            + [by_chunk(a) for a in (conv_a, conv_b, d_att)]
            + [lanes(scale), lanes(back), by_chunk(out_term), by_chunk(vectors)]
            + [pl.BlockSpec(memory_space=pl.ANY)] * 2,
            out_specs=[
                by_chunk(spread),
                by_chunk(spread),
                pl.BlockSpec(block, lambda s, me: (jnp.minimum(s, half - 1), 0, 0)),
                pl.BlockSpec(block, lambda s, me: (jnp.maximum(s - half, 0), 0, 0)),
            ],
            scratch_shapes=[pltpu.VMEM((rows, tiles + 2, STEP, LANES), BF)] * 2
            + [pltpu.VMEM(normed_t.shape, BF), pltpu.VMEM(halo_t.shape, BF)]
            + [pltpu.SemaphoreType.DMA((2,))],
        ),
        out_shape=[spread, spread, part, part],
        compiler_params=params(),
        cost_estimate=pl.CostEstimate(
            flops=d_att.size * 3000, bytes_accessed=d_att.size * 20, transcendentals=0
        ),
        name="gradients",
    )(
        me.reshape(1), expanded, expanded, halo, halo, taps, taps, conv_a, conv_b, d_att, scale, back,
        out_term, vectors, normed_t, halo_t,
    )


def back_project(xa_ref, xb_ref, w_ref):
    chunks = [flat(ref[k, 0]) for ref in (xa_ref, xb_ref) for k in range(ref.shape[0])]
    return lax.dot_general(
        jnp.concatenate(chunks, -1),
        w_ref[...],
        (((1,), (1,)), ((), ())),
        preferred_element_type=F32,
    )


def edge_kernel(
    ca_ref, cb_ref, d_ref, scale_ref, back_ref, taps_ref, w_ref, above_ref, below_ref
):
    side = pl.program_id(0)
    chunks = d_ref.shape[0]
    spread = [None] * (2 * chunks)
    for k in range(chunks):
        dg = d_ref[k, 0].astype(F32) * scale_ref[k] + back_ref[k]
        for n, ref in ((k, cb_ref), (chunks + k, ca_ref)):
            d = dg * ref[k, 0].astype(F32)
            before = neighbours(d[-1], True)[None]
            behind = neighbours(d[0], False)[None]
            windows = (
                jnp.concatenate([d[1:], behind], 0),
                d,
                jnp.concatenate([before, d[:-1]], 0),
            )
            total = None
            for j in range(3):
                tap = taps_ref[6 * side + j, :, n * LANES : (n + 1) * LANES].astype(F32)
                total = added(total, windows[j] * tap[None])
            spread[n] = flat(total.astype(BF))
    row = lax.dot_general(
        jnp.concatenate(spread, -1),
        w_ref[...],
        (((1,), (1,)), ((), ())),
        preferred_element_type=F32,
    ).astype(BF)

    @pl.when(side == 0)
    def _():
        above_ref[...] = row

    @pl.when(side == 1)
    def _():
        below_ref[...] = row


def edge_rows(conv_a, conv_b, d_att, scale, back, taps, w_in):
    chunks, rows, tiles, _, _ = d_att.shape
    spec = pl.BlockSpec(
        (chunks, 1, tiles, STEP, LANES), lambda r: (0, r * (rows - 1), 0, 0, 0)
    )
    out = jax.ShapeDtypeStruct((tiles * STEP, w_in.shape[0]), BF)
    return pl.pallas_call(
        edge_kernel,
        grid=(2,),
        in_specs=[spec, spec, spec] + [whole(a) for a in (scale, back, taps, w_in)],
        out_specs=[whole(out)] * 2,
        out_shape=[out] * 2,
        compiler_params=params(),
        name="edge_rows",
    )(conv_a, conv_b, d_att, scale, back, taps, w_in)


def input_kernel(
    x_ref, cot_ref, xa_ref, xb_ref, above_ref, below_ref, gain_ref, w_ref, order_ref, out_ref
):
    row = pl.program_id(0)
    last = pl.num_programs(0) - 1
    d_norm = back_project(xa_ref, xb_ref, w_ref)
    d_norm = d_norm + jnp.where(row == 0, 1.0, 0.0) * above_ref[...].astype(F32)
    d_norm = d_norm + jnp.where(row == last, 1.0, 0.0) * below_ref[...].astype(F32)
    d_norm = lax.dot_general(
        order_ref[...], d_norm.astype(BF), (((0,), (0,)), ((), ())), preferred_element_type=F32
    )
    xhat, rstd = layer_norm(x_ref[0])
    dxhat = d_norm * gain_ref[...]
    grad = cot_ref[0].astype(F32) + rstd * (
        dxhat - jnp.mean(dxhat, -1, keepdims=True) - xhat * jnp.mean(dxhat * xhat, -1, keepdims=True)
    )
    out_ref[0, 0] = grad.astype(BF)


def input_grad(x, cot, xa, xb, above, below, gain, w_in, order):
    rows, cols, width = x.shape
    chunks = xa.shape[0]
    spec = pl.BlockSpec((1, cols, width), lambda r: (r, 0, 0))
    inner = pl.BlockSpec(
        (chunks, 1, cols // STEP, STEP, LANES), lambda r: (0, r + 1, 0, 0, 0)
    )
    return pl.pallas_call(
        input_kernel,
        grid=(rows,),
        in_specs=[spec, spec, inner, inner]
        + [whole(a) for a in (above, below, gain, w_in, order)],
        out_specs=pl.BlockSpec((1, 1, cols, width), lambda r: (0, r, 0, 0)),
        out_shape=jax.ShapeDtypeStruct((1, rows, cols, width), BF),
        compiler_params=params(),
        cost_estimate=pl.CostEstimate(
            flops=2 * rows * cols * width * width * 6,
            bytes_accessed=rows * cols * width * 10,
            transcendentals=0,
        ),
        name="input_grad",
    )(x, cot, xa, xb, above, below, gain, w_in, order)


def unpack_kernel(factor, me_ref, own_ref, other_ref, in_ref, out_ref, att_ref, taps_ref):
    step = pl.program_id(0)
    first = me_ref[0] == 0
    half = own_ref.shape[0]
    chunks = 2 * half
    width = chunks * LANES

    def rows(k, start, count):
        own = own_ref[k % half, pl.ds(start, count)].astype(F32)
        other = other_ref[k % half, pl.ds(start, count)].astype(F32)
        return jnp.where(first, own, other) if k < half else jnp.where(first, other, own)

    start = pl.multiple_of(step * LANES, LANES)
    for k in range(chunks):
        here = slice(k * LANES, (k + 1) * LANES)
        in_ref[:, here] = rows(k, start, LANES) * factor
        in_ref[:, width + k * LANES : width + (k + 1) * LANES] = (
            rows(k, start + width, LANES) * factor
        )
        out_ref[here, pl.ds(start, LANES)] = rows(k, start + 2 * width, LANES).T * factor

    @pl.when(step == 0)
    def _():
        small = [rows(k, 3 * width, SMALL) for k in range(chunks)]
        for k in range(chunks):
            here = slice(k * LANES, (k + 1) * LANES)
            taps_ref[:, here] = small[k][16:25] * factor
            taps_ref[:, width + k * LANES : width + (k + 1) * LANES] = small[k][32:41] * factor
            for m in range(chunks):
                block = lax.dot_general(
                    small[k][0:8].astype(BF),
                    small[m][8:16].astype(BF),
                    (((0,), (0,)), ((), ())),
                    preferred_element_type=F32,
                )
                att_ref[here, m * LANES : (m + 1) * LANES] = block * factor


def unpack(own, other, me, hidden, width, factor):
    full = jax.ShapeDtypeStruct((width, width), F32)
    return pl.pallas_call(
        functools.partial(unpack_kernel, factor),
        grid=(width // LANES,),
        in_specs=[pl.BlockSpec(memory_space=pltpu.SMEM), whole(own), whole(other)],
        out_specs=[
            pl.BlockSpec((LANES, hidden), lambda s: (s, 0)),
            whole(full),
            whole(full),
            pl.BlockSpec((9, hidden), lambda s: (0, 0)),
        ],
        out_shape=[
            jax.ShapeDtypeStruct((width, hidden), F32),
            full,
            full,
            jax.ShapeDtypeStruct((9, hidden), F32),
        ],
        compiler_params=params(vmem=16 * 1024 * 1024),
        name="unpack",
    )(me.reshape(1), own, other)


def space_neighbours(down, up):
    count = lax.axis_size("x") * lax.axis_size("zh") * lax.axis_size("y")
    forward = [(i, i + 1) for i in range(count - 1)]
    backward = [(t, s) for s, t in forward]
    axes = ("x", "zh", "y")
    return lax.ppermute(down, axes, forward), lax.ppermute(up, axes, backward)


SPACE = ("x", "zh", "y")
CHIPS = ("zl", "x", "zh", "y")
SWAP = [(0, 1), (1, 0)]


def sum_over_space(v):
    n = lax.axis_size(SPACE)
    copies = lax.optimization_barrier(jnp.broadcast_to(v[None], (n,) + v.shape))
    return jnp.sum(lax.all_to_all(copies, SPACE, 0, 0, tiled=True), 0)


def sum_over_all(send, keep, later):
    n = lax.axis_size(CHIPS)
    other = lax.ppermute(send, "co", SWAP)
    own = (keep.astype(F32) + other.astype(F32)).astype(BF)
    own = lax.optimization_barrier(own.reshape(n, -1, LANES))
    parts = lax.all_to_all(own, CHIPS, 0, 0, tiled=True)
    part = jnp.sum(parts.astype(F32), 0).astype(BF)
    part, later = lax.optimization_barrier((part, later))
    copies = lax.optimization_barrier(jnp.broadcast_to(part[None], parts.shape))
    own = lax.all_to_all(copies, CHIPS, 0, 0, tiled=True)
    return own.reshape(keep.shape), later


def local(frames, cotangent, gain, w_in, kernel, w_att, w_out):
    x = frames[0]
    cot = cotangent[0]
    rows, cols, width = x.shape
    hidden = w_in.shape[1]
    space = lax.axis_size("x") * lax.axis_size("zh") * lax.axis_size("y")
    place = (lax.axis_index("x") * lax.axis_size("zh") + lax.axis_index("zh")) * lax.axis_size(
        "y"
    ) + lax.axis_index("y")
    frame_count = lax.axis_size("zl") * lax.axis_size("co")
    frame = lax.axis_index("zl") * lax.axis_size("co") + lax.axis_index("co")
    pixels = rows * space * cols
    factor = 1.0 / math.sqrt(frame_count * pixels)
    taps = jnp.broadcast_to(kernel[:, None], (9, STEP, hidden))
    gain = gain[None]
    order = place_matrix(cols)

    above, below = space_neighbours(x[-1:], x[:1])
    normed_t, expanded, cot_t, d_att = enter(x, gain, w_in, order, cot, w_out)
    halo_t, halo = enter_halo(above, below, gain, w_in, order)
    conv_a, conv_b, sums = convolution(expanded, halo, taps, d_att)
    sums = jnp.sum(sums.reshape(2, 8, width), 1)
    sums = sum_over_space(sums.reshape(8, LANES)).reshape(-1)
    out_term = outer(cot_t, conv_a, conv_b)
    sums, out_term = lax.optimization_barrier((sums, out_term))
    pooled = sums[:width] / pixels
    d_scale = sums[width:]
    scale = jnp.dot(pooled, w_att, precision=lax.Precision.HIGHEST)
    back = jnp.dot(d_scale, w_att.T, precision=lax.Precision.HIGHEST) / pixels
    to_above, to_below = edge_rows(
        conv_a, conv_b, d_att, scale.reshape(-1, 1, LANES), back.reshape(-1, 1, LANES), taps, w_in
    )
    from_above, from_below = space_neighbours(to_below, to_above)
    mine = (jnp.arange(8)[None, :, None] == frame) & (place == 0)
    vectors = jnp.concatenate(
        [jnp.where(mine, v.reshape(-1, 1, LANES), 0.0) for v in (pooled, d_scale)], 1
    )
    me = lax.axis_index("co")
    d_exp_a, d_exp_b, send, keep = gradients(
        me, expanded, halo, taps, conv_a, conv_b, d_att, scale[None], back[None], out_term, vectors,
        normed_t, halo_t,
    )
    send, from_above, from_below = lax.optimization_barrier((send, from_above, from_below))
    own, (from_above, from_below) = sum_over_all(send, keep, (from_above, from_below))
    grad = input_grad(x, cot, d_exp_a, d_exp_b, from_above, from_below, gain, w_in, order)
    own, grad = lax.optimization_barrier((own, grad))
    other = lax.ppermute(own, "co", SWAP)
    in_sum, out_sum, att_sum, kernel_sum = unpack(
        own, other, me, hidden, width, factor
    )
    return grad, in_sum, kernel_sum, att_sum, out_sum


def solution(mesh):
    fine = Mesh(mesh.devices.reshape(2, 2, 4, 2, 4), ("zl", "co", "x", "zh", "y"))
    big = P(("zl", "co"), ("x", "zh", "y"), None, None)
    return jax.shard_map(
        local,
        mesh=fine,
        in_specs=(big, big, P(), P(), P(), P(), P()),
        out_specs=(big, P(), P(), P(), P()),
        check_vma=False,
    )
```

```python
import functools
import math

import jax
import jax.numpy as jnp
import numpy as np
from jax import lax
from jax.experimental import pallas as pl
from jax.experimental.pallas import tpu as pltpu
from jax.sharding import Mesh, PartitionSpec as P

EPS = 1e-06
BF = jnp.bfloat16
F32 = jnp.float32
LANES = 128
STEP = 16
SMALL = 48
VMEM = 56 * 1024 * 1024


def params(vmem=VMEM):
    return pltpu.CompilerParams(dimension_semantics=("arbitrary",), vmem_limit_bytes=vmem)


def layer_norm(x):
    xf = x.astype(F32)
    centered = xf - jnp.mean(xf, -1, keepdims=True)
    rstd = lax.rsqrt(jnp.mean(centered * centered, -1, keepdims=True) + EPS)
    return centered * rstd, rstd


def place_matrix(cols):
    place = np.arange(cols)[:, None]
    column = np.arange(cols)[None]
    return jnp.asarray(column == place % STEP * (cols // STEP) + place // STEP, BF)


def reorder(order, rows):
    return jnp.dot(order, rows, preferred_element_type=F32)


def neighbours(tile, first):
    zero = jnp.zeros((1, tile.shape[1]), F32)
    parts = [zero, tile[: STEP - 1]] if first else [tile[1:], zero]
    return jnp.concatenate(parts, 0)


def chunked(v):
    return [v[:, k * LANES : (k + 1) * LANES] for k in range(v.shape[1] // LANES)]


def tiled(v):
    return v.reshape(-1, STEP, LANES)


def flat(v):
    return v.reshape(-1, LANES)


def expand_row(x, gain_ref, w_ref, order, normed_t_ref, expanded_ref, r=0):
    cols = x.shape[0]
    xhat, _ = layer_norm(reorder(order, x))
    normed = (xhat * gain_ref[...]).astype(BF)
    normed_t_ref[:, r * cols : (r + 1) * cols] = normed.T
    for k, e in enumerate(chunked(jnp.dot(normed, w_ref[...], preferred_element_type=F32))):
        expanded_ref[k, r, 1 : 1 + cols // STEP] = tiled(e.astype(BF))
        expanded_ref[k, r, 0] = neighbours(e[cols - STEP :], True).astype(BF)
        expanded_ref[k, r, 1 + cols // STEP] = neighbours(e[:STEP], False).astype(BF)


def halo_kernel(above_ref, below_ref, gain_ref, w_ref, order_ref, normed_t_ref, expanded_ref):
    x = jnp.where(pl.program_id(0) == 0, above_ref[0].astype(F32), below_ref[0].astype(F32))
    expand_row(x.astype(BF), gain_ref, w_ref, order_ref[...], normed_t_ref, expanded_ref)


def enter_kernel(
    x_ref, gain_ref, w_ref, order_ref, cot_ref, wo_ref, normed_t_ref, expanded_ref, cot_t_ref, d_ref
):
    order = order_ref[...]
    placed = reorder(order, cot_ref[0]).astype(BF)
    cot_t_ref[...] = placed.T
    d_att = lax.dot_general(
        placed, wo_ref[...], (((1,), (1,)), ((), ())), preferred_element_type=F32
    )
    for k, d in enumerate(chunked(d_att)):
        d_ref[k, 0] = tiled(d.astype(BF))
    expand_row(x_ref[0], gain_ref, w_ref, order, normed_t_ref, expanded_ref)


def enter_specs(rows, cols, width, hidden):
    groups, tiles = hidden // LANES, cols // STEP
    specs = [
        pl.BlockSpec((width, cols), lambda r: (0, r)),
        pl.BlockSpec((groups, 1, tiles + 2, STEP, LANES), lambda r: (0, r, 0, 0, 0)),
    ]
    shapes = [
        jax.ShapeDtypeStruct((width, rows * cols), BF),
        jax.ShapeDtypeStruct((groups, rows, tiles + 2, STEP, LANES), BF),
    ]
    return specs, shapes


def whole(a):
    return pl.BlockSpec(a.shape, lambda r: (0,) * a.ndim)


def enter(x, gain, w_in, order, cot, w_out):
    rows, cols, width = x.shape
    chunks = width // LANES
    specs, shapes = enter_specs(rows, cols, width, w_in.shape[1])
    row = pl.BlockSpec((1, cols, width), lambda r: (r, 0, 0))
    return pl.pallas_call(
        enter_kernel,
        grid=(rows,),
        in_specs=[row, whole(gain), whole(w_in), whole(order), row, whole(w_out)],
        out_specs=specs
        + [specs[0], pl.BlockSpec((chunks, 1, cols // STEP, STEP, LANES), lambda r: (0, r, 0, 0, 0))],
        out_shape=shapes
        + [shapes[0], jax.ShapeDtypeStruct((chunks, rows, cols // STEP, STEP, LANES), BF)],
        compiler_params=params(),
        cost_estimate=pl.CostEstimate(
            flops=2 * rows * cols * width * width * 8,
            bytes_accessed=rows * cols * width * 12,
            transcendentals=0,
        ),
        name="enter",
    )(x, gain, w_in, order, cot, w_out)


def enter_halo(above, below, gain, w_in, order):
    _, cols, width = above.shape
    specs, shapes = enter_specs(2, cols, width, w_in.shape[1])
    row = pl.BlockSpec((1, cols, width), lambda r: (0, 0, 0))
    return pl.pallas_call(
        halo_kernel,
        grid=(2,),
        in_specs=[row, row, whole(gain), whole(w_in), whole(order)],
        out_specs=specs,
        out_shape=shapes,
        compiler_params=params(),
        name="enter_halo",
    )(above, below, gain, w_in, order)


def row_tile(own_ref, halo_ref, r, t):
    rows = own_ref.shape[1]
    if r == 0:
        return halo_ref[0, 0, t]
    if r == rows + 1:
        return halo_ref[0, 1, t]
    return own_ref[0, r - 1, t]


def halves(v):
    return v[: STEP // 2] + v[STEP // 2 :]


def added(total, term):
    return term if total is None else total + term


def own_row(middle_ref, edge_ref, r):
    last = middle_ref.shape[1] + 1
    return edge_ref.at[0, r // last] if r in (0, last) else middle_ref.at[0, r - 1]


def conv_kernel(out_rows, ea_ref, eb_ref, *refs):
    *halo, ka_ref, kb_ref, d_ref, ca_ref, cb_ref, sum_ref = refs
    _, rows, tiles, _, _ = d_ref.shape
    taps_a = [ka_ref[n].astype(F32) for n in range(9)]
    taps_b = [kb_ref[n].astype(F32) for n in range(9)]
    in_rows = sorted({r + i for r in out_rows for i in (-1, 0, 1)})

    def convolve(own_ref, halo_ref, taps, t):
        total = {}
        for r in in_rows:
            for j in range(3):
                if 0 <= r < rows:
                    v = own_ref[0, r, t + j].astype(F32)
                else:
                    v = halo_ref[0, int(r > 0), t + j].astype(F32)
                for i in range(3):
                    o = r + 1 - i
                    if o in out_rows:
                        total[o] = added(total.get(o), v * taps[3 * i + j])
        return total

    def body(t, sums):
        a = convolve(ea_ref, halo[0] if halo else None, taps_a, t)
        b = convolve(eb_ref, halo[1] if halo else None, taps_b, t)
        total = [None, None]
        for n, r in enumerate(out_rows):
            ca_ref[0, n, t] = a[r].astype(BF)
            cb_ref[0, n, t] = b[r].astype(BF)
            g = a[r] * b[r]
            total[0] = added(total[0], g)
            total[1] = added(total[1], g * d_ref[0, r, t].astype(F32))
        return sums[0] + halves(total[0]), sums[1] + halves(total[1])

    zero = jnp.zeros((STEP // 2, LANES), F32)
    pooled, weighted = lax.fori_loop(0, tiles, body, (zero, zero), unroll=2)
    sum_ref[0:8, :] = pooled
    sum_ref[8:16, :] = weighted


def chunk_spec(shape, offset=0):
    block = (1,) + tuple(shape[1:])
    return pl.BlockSpec(block, lambda k: (k + offset,) + (0,) * (len(shape) - 1))


def half_specs(a):
    return [chunk_spec(a.shape), chunk_spec(a.shape, a.shape[0] // 2)]


def tap_specs(taps, chunks):
    block = taps.shape[:2] + (LANES,)
    return [
        pl.BlockSpec(block, lambda k: (0, 0, k)),
        pl.BlockSpec(block, lambda k: (0, 0, k + chunks)),
    ]


def convolution(out_rows, expanded, halo, taps, d_att):
    chunks, _, tiles, _, _ = d_att.shape
    shape = jax.ShapeDtypeStruct((chunks, len(out_rows), tiles, STEP, LANES), BF)
    part = chunk_spec(shape.shape)
    arrays = [expanded] * 2 + ([] if halo is None else [halo] * 2)
    return pl.pallas_call(
        functools.partial(conv_kernel, out_rows),
        grid=(chunks,),
        in_specs=half_specs(expanded)
        + ([] if halo is None else half_specs(halo))
        + tap_specs(taps, chunks)
        + [chunk_spec(d_att.shape)],
        out_specs=[part, part, pl.BlockSpec((16, LANES), lambda k: (0, k))],
        out_shape=[shape, shape, jax.ShapeDtypeStruct((16, chunks * LANES), F32)],
        compiler_params=params(),
        cost_estimate=pl.CostEstimate(
            flops=d_att.size * 600, bytes_accessed=d_att.size * 14, transcendentals=0
        ),
        name="convolution",
    )(*arrays, taps, taps, d_att)


def outer_kernel(cot_t_ref, ma_ref, mb_ref, sa_ref, sb_ref, out_ref):
    cols = ma_ref.shape[2] * STEP
    total = None
    for r in range(ma_ref.shape[1] + 2):
        left = cot_t_ref[:, r * cols : (r + 1) * cols]
        a, b = own_row(ma_ref, sa_ref, r)[...], own_row(mb_ref, sb_ref, r)[...]
        gated = flat((a.astype(F32) * b.astype(F32)).astype(BF))
        total = added(total, jnp.dot(left, gated, preferred_element_type=F32))
    out_ref[0] = total


def outer(cot_t, middle, edge):
    arrays = (*middle, *edge)
    chunks = middle[0].shape[0]
    shape = (chunks, cot_t.shape[0], LANES)
    return pl.pallas_call(
        outer_kernel,
        grid=(chunks,),
        in_specs=[whole(cot_t)] + [chunk_spec(a.shape) for a in arrays],
        out_specs=chunk_spec(shape),
        out_shape=jax.ShapeDtypeStruct(shape, F32),
        compiler_params=params(),
        cost_estimate=pl.CostEstimate(
            flops=4 * cot_t.size * chunks * LANES,
            bytes_accessed=cot_t.size * 8,
            transcendentals=0,
        ),
        name="outer",
    )(cot_t, *arrays)


def gradient_kernel(
    me_ref, ea_ref, eb_ref, ha_ref, hb_ref, ka_ref, kb_ref, ma_ref, mb_ref, ra_ref, rb_ref, d_ref, scale_ref,
    back_ref, out_ref, vec_ref, nt_ref, nh_ref, xa_ref, xb_ref, send_ref, keep_ref, da, db, nt, nh, sems,
):
    _, rows, tiles, _, _ = d_ref.shape
    cols = tiles * STEP
    scale = jnp.broadcast_to(scale_ref[...], (STEP, LANES))
    back = jnp.broadcast_to(back_ref[...], (STEP, LANES))
    copies = [
        pltpu.make_async_copy(nt_ref, nt, sems.at[0]),
        pltpu.make_async_copy(nh_ref, nh, sems.at[1]),
    ]

    @pl.when(pl.program_id(0) == 0)
    def _():
        for copy in copies:
            copy.start()

    def products(own_ref, halo_ref, own, t, sums):
        part = [None] * 9
        for r in range(rows + 2):
            for j in range(3):
                v = row_tile(own_ref, halo_ref, r, t + j).astype(F32)
                for i in range(3):
                    if 0 <= r - i < rows:
                        part[3 * i + j] = added(part[3 * i + j], v * own[r - i])
        return tuple(s + halves(p) for s, p in zip(sums, part))

    def first(own_ref, halo_ref, middle_ref, edge_ref, d, t, sums):
        own = []
        for r in range(rows):
            dg = d_ref[0, r, t].astype(F32) * scale + back
            own.append(dg * own_row(middle_ref, edge_ref, r)[t].astype(F32))
            d[r, t + 1] = own[r].astype(BF)
        return products(own_ref, halo_ref, own, t, sums)

    nought = (jnp.zeros((STEP // 2, LANES), F32),) * 9
    sums = [
        lax.fori_loop(0, tiles, functools.partial(first, *refs), nought, unroll=2)
        for refs in (
            (ea_ref, ha_ref, mb_ref, rb_ref, da),
            (eb_ref, hb_ref, ma_ref, ra_ref, db),
        )
    ]
    for d in (da, db):
        for r in range(rows):
            d[r, 0] = neighbours(d[r, tiles].astype(F32), True).astype(BF)
            d[r, tiles + 1] = neighbours(d[r, 1].astype(F32), False).astype(BF)

    taps_a = [ka_ref[n].astype(F32) for n in range(9)]
    taps_b = [kb_ref[n].astype(F32) for n in range(9)]

    def spread(d, taps, x_ref, t):
        total = [None] * (rows + 2)
        for r in range(rows):
            for j in range(3):
                v = d[r, t + 2 - j].astype(F32)
                for i in range(3):
                    total[r + i] = added(total[r + i], v * taps[3 * i + j])
        for r in range(rows + 2):
            x_ref[0, r, t] = total[r].astype(BF)

    for d, taps, x_ref in ((da, taps_a, xa_ref), (db, taps_b, xb_ref)):

        def second(t, carry, d=d, taps=taps, x_ref=x_ref):
            spread(d, taps, x_ref, t)
            return carry

        lax.fori_loop(0, tiles, second, 0, unroll=1)

    @pl.when(pl.program_id(0) == 0)
    def _():
        for copy in copies:
            copy.wait()

    total = None
    for r in range(rows + 2):
        if r == 0:
            left = nh[:, 0:cols]
        elif r == rows + 1:
            left = nh[:, cols : 2 * cols]
        else:
            left = nt[:, (r - 1) * cols : r * cols]
        right = jnp.concatenate([flat(xa_ref[0, r]), flat(xb_ref[0, r])], -1)
        total = added(total, jnp.dot(left, right, preferred_element_type=F32))
    width = total.shape[0]
    blank = jnp.zeros((7, LANES), F32)
    rows_of = lambda part: [jnp.sum(p, 0, keepdims=True) for p in part]
    small = jnp.concatenate([vec_ref[0], *rows_of(sums[0]), blank, *rows_of(sums[1]), blank], 0)

    def write(ref):
        ref[0, 0:width] = total[:, :LANES].astype(BF)
        ref[0, width : 2 * width] = total[:, LANES:].astype(BF)
        ref[0, 2 * width : 3 * width] = (out_ref[0] * scale_ref[...]).astype(BF)
        ref[0, 3 * width : 3 * width + SMALL] = small.astype(BF)
        ref[0, 3 * width + SMALL :] = jnp.zeros((width // 2 - SMALL, LANES), BF)

    early = pl.program_id(0) < pl.num_programs(0) // 2
    pl.when(early)(lambda: write(send_ref))
    pl.when(jnp.logical_not(early))(lambda: write(keep_ref))


def gradients(
    me, expanded, halo, taps, middle, edge, d_att, scale, back, out_term, vectors, normed_t, halo_t
):
    chunks, rows, tiles, _, _ = d_att.shape
    width = chunks * LANES
    half = chunks // 2
    chunk = lambda s, me: (s + half * (1 - me[0])) % chunks

    def by_chunk(a, offset=0):
        block = (1,) + tuple(a.shape[1:])
        return pl.BlockSpec(block, lambda s, me: (chunk(s, me) + offset,) + (0,) * (len(block) - 1))

    def by_half(a):
        return [by_chunk(a), by_chunk(a, chunks)]

    def lanes(a, offset=0):
        block = a.shape[:-1] + (LANES,)
        return pl.BlockSpec(
            block, lambda s, me: (0,) * (len(block) - 1) + (chunk(s, me) + offset,)
        )

    spread = jax.ShapeDtypeStruct((chunks, rows + 2, tiles, STEP, LANES), BF)
    part = jax.ShapeDtypeStruct((half, 7 * width // 2, LANES), BF)
    block = (1,) + part.shape[1:]
    return pl.pallas_call(
        gradient_kernel,
        grid_spec=pltpu.PrefetchScalarGridSpec(
            num_scalar_prefetch=1,
            grid=(chunks,),
            in_specs=by_half(expanded)
            + by_half(halo)
            + [lanes(taps), lanes(taps, chunks)]
            + [by_chunk(a) for a in (*middle, *edge, d_att)]
            + [lanes(scale), lanes(back), by_chunk(out_term), by_chunk(vectors)]
            + [pl.BlockSpec(memory_space=pl.ANY)] * 2,
            out_specs=[
                by_chunk(spread),
                by_chunk(spread),
                pl.BlockSpec(block, lambda s, me: (jnp.minimum(s, half - 1), 0, 0)),
                pl.BlockSpec(block, lambda s, me: (jnp.maximum(s - half, 0), 0, 0)),
            ],
            scratch_shapes=[pltpu.VMEM((rows, tiles + 2, STEP, LANES), BF)] * 2
            + [pltpu.VMEM(normed_t.shape, BF), pltpu.VMEM(halo_t.shape, BF)]
            + [pltpu.SemaphoreType.DMA((2,))],
        ),
        out_shape=[spread, spread, part, part],
        compiler_params=params(),
        cost_estimate=pl.CostEstimate(
            flops=d_att.size * 3000, bytes_accessed=d_att.size * 20, transcendentals=0
        ),
        name="gradients",
    )(
        me.reshape(1), expanded, expanded, halo, halo, taps, taps, *middle, *edge, d_att, scale, back,
        out_term, vectors, normed_t, halo_t,
    )


def back_project(xa_ref, xb_ref, w_ref):
    chunks = [flat(ref[k, 0]) for ref in (xa_ref, xb_ref) for k in range(ref.shape[0])]
    return lax.dot_general(
        jnp.concatenate(chunks, -1),
        w_ref[...],
        (((1,), (1,)), ((), ())),
        preferred_element_type=F32,
    )


def edge_kernel(
    ca_ref, cb_ref, d_ref, scale_ref, back_ref, taps_ref, w_ref, above_ref, below_ref
):
    side = pl.program_id(0)
    chunks = d_ref.shape[0]
    spread = [None] * (2 * chunks)
    for k in range(chunks):
        dg = d_ref[k, 0].astype(F32) * scale_ref[k] + back_ref[k]
        for n, ref in ((k, cb_ref), (chunks + k, ca_ref)):
            d = dg * ref[k, 0].astype(F32)
            before = neighbours(d[-1], True)[None]
            behind = neighbours(d[0], False)[None]
            windows = (
                jnp.concatenate([d[1:], behind], 0),
                d,
                jnp.concatenate([before, d[:-1]], 0),
            )
            total = None
            for j in range(3):
                tap = taps_ref[6 * side + j, :, n * LANES : (n + 1) * LANES].astype(F32)
                total = added(total, windows[j] * tap[None])
            spread[n] = flat(total.astype(BF))
    row = lax.dot_general(
        jnp.concatenate(spread, -1),
        w_ref[...],
        (((1,), (1,)), ((), ())),
        preferred_element_type=F32,
    ).astype(BF)

    @pl.when(side == 0)
    def _():
        above_ref[...] = row

    @pl.when(side == 1)
    def _():
        below_ref[...] = row


def edge_rows(edge, d_att, scale, back, taps, w_in):
    chunks, rows, tiles, _, _ = d_att.shape
    block = (chunks, 1, tiles, STEP, LANES)
    spec = pl.BlockSpec(block, lambda r: (0, r, 0, 0, 0))
    d_spec = pl.BlockSpec(block, lambda r: (0, r * (rows - 1), 0, 0, 0))
    out = jax.ShapeDtypeStruct((tiles * STEP, w_in.shape[0]), BF)
    return pl.pallas_call(
        edge_kernel,
        grid=(2,),
        in_specs=[spec, spec, d_spec] + [whole(a) for a in (scale, back, taps, w_in)],
        out_specs=[whole(out)] * 2,
        out_shape=[out] * 2,
        compiler_params=params(),
        name="edge_rows",
    )(*edge, d_att, scale, back, taps, w_in)


def input_kernel(
    x_ref, cot_ref, xa_ref, xb_ref, above_ref, below_ref, gain_ref, w_ref, order_ref, out_ref
):
    row = pl.program_id(0)
    last = pl.num_programs(0) - 1
    d_norm = back_project(xa_ref, xb_ref, w_ref)
    d_norm = d_norm + jnp.where(row == 0, 1.0, 0.0) * above_ref[...].astype(F32)
    d_norm = d_norm + jnp.where(row == last, 1.0, 0.0) * below_ref[...].astype(F32)
    d_norm = lax.dot_general(
        order_ref[...], d_norm.astype(BF), (((0,), (0,)), ((), ())), preferred_element_type=F32
    )
    xhat, rstd = layer_norm(x_ref[0])
    dxhat = d_norm * gain_ref[...]
    grad = cot_ref[0].astype(F32) + rstd * (
        dxhat - jnp.mean(dxhat, -1, keepdims=True) - xhat * jnp.mean(dxhat * xhat, -1, keepdims=True)
    )
    out_ref[0, 0] = grad.astype(BF)


def input_grad(x, cot, xa, xb, above, below, gain, w_in, order):
    rows, cols, width = x.shape
    chunks = xa.shape[0]
    spec = pl.BlockSpec((1, cols, width), lambda r: (r, 0, 0))
    inner = pl.BlockSpec(
        (chunks, 1, cols // STEP, STEP, LANES), lambda r: (0, r + 1, 0, 0, 0)
    )
    return pl.pallas_call(
        input_kernel,
        grid=(rows,),
        in_specs=[spec, spec, inner, inner]
        + [whole(a) for a in (above, below, gain, w_in, order)],
        out_specs=pl.BlockSpec((1, 1, cols, width), lambda r: (0, r, 0, 0)),
        out_shape=jax.ShapeDtypeStruct((1, rows, cols, width), BF),
        compiler_params=params(),
        cost_estimate=pl.CostEstimate(
            flops=2 * rows * cols * width * width * 6,
            bytes_accessed=rows * cols * width * 10,
            transcendentals=0,
        ),
        name="input_grad",
    )(x, cot, xa, xb, above, below, gain, w_in, order)


def unpack_kernel(factor, me_ref, own_ref, other_ref, in_ref, out_ref, att_ref, taps_ref):
    step = pl.program_id(0)
    first = me_ref[0] == 0
    half = own_ref.shape[0]
    chunks = 2 * half
    width = chunks * LANES

    def rows(k, start, count):
        own = own_ref[k % half, pl.ds(start, count)].astype(F32)
        other = other_ref[k % half, pl.ds(start, count)].astype(F32)
        return jnp.where(first, own, other) if k < half else jnp.where(first, other, own)

    start = pl.multiple_of(step * LANES, LANES)
    for k in range(chunks):
        here = slice(k * LANES, (k + 1) * LANES)
        in_ref[:, here] = rows(k, start, LANES) * factor
        in_ref[:, width + k * LANES : width + (k + 1) * LANES] = (
            rows(k, start + width, LANES) * factor
        )
        out_ref[here, pl.ds(start, LANES)] = rows(k, start + 2 * width, LANES).T * factor

    @pl.when(step == 0)
    def _():
        small = [rows(k, 3 * width, SMALL) for k in range(chunks)]
        for k in range(chunks):
            here = slice(k * LANES, (k + 1) * LANES)
            taps_ref[:, here] = small[k][16:25] * factor
            taps_ref[:, width + k * LANES : width + (k + 1) * LANES] = small[k][32:41] * factor
            for m in range(chunks):
                block = lax.dot_general(
                    small[k][0:8].astype(BF),
                    small[m][8:16].astype(BF),
                    (((0,), (0,)), ((), ())),
                    preferred_element_type=F32,
                )
                att_ref[here, m * LANES : (m + 1) * LANES] = block * factor


def unpack(own, other, me, hidden, width, factor):
    full = jax.ShapeDtypeStruct((width, width), F32)
    return pl.pallas_call(
        functools.partial(unpack_kernel, factor),
        grid=(width // LANES,),
        in_specs=[pl.BlockSpec(memory_space=pltpu.SMEM), whole(own), whole(other)],
        out_specs=[
            pl.BlockSpec((LANES, hidden), lambda s: (s, 0)),
            whole(full),
            whole(full),
            pl.BlockSpec((9, hidden), lambda s: (0, 0)),
        ],
        out_shape=[
            jax.ShapeDtypeStruct((width, hidden), F32),
            full,
            full,
            jax.ShapeDtypeStruct((9, hidden), F32),
        ],
        compiler_params=params(vmem=16 * 1024 * 1024),
        name="unpack",
    )(me.reshape(1), own, other)


def space_neighbours(down, up):
    count = lax.axis_size("x") * lax.axis_size("zh") * lax.axis_size("y")
    forward = [(i, i + 1) for i in range(count - 1)]
    backward = [(t, s) for s, t in forward]
    axes = ("x", "zh", "y")
    return lax.ppermute(down, axes, forward), lax.ppermute(up, axes, backward)


SPACE = ("x", "zh", "y")
CHIPS = ("zl", "x", "zh", "y")
SWAP = [(0, 1), (1, 0)]


def sum_over_space(v):
    n = lax.axis_size(SPACE)
    copies = lax.optimization_barrier(jnp.broadcast_to(v[None], (n,) + v.shape))
    return jnp.sum(lax.all_to_all(copies, SPACE, 0, 0, tiled=True), 0)


def sum_over_all(send, keep, later):
    n = lax.axis_size(CHIPS)
    other = lax.ppermute(send, "co", SWAP)
    own = (keep.astype(F32) + other.astype(F32)).astype(BF)
    own = lax.optimization_barrier(own.reshape(n, -1, LANES))
    parts = lax.all_to_all(own, CHIPS, 0, 0, tiled=True)
    part = jnp.sum(parts.astype(F32), 0).astype(BF)
    part, later = lax.optimization_barrier((part, later))
    copies = lax.optimization_barrier(jnp.broadcast_to(part[None], parts.shape))
    own = lax.all_to_all(copies, CHIPS, 0, 0, tiled=True)
    return own.reshape(keep.shape), later


def local(frames, cotangent, gain, w_in, kernel, w_att, w_out):
    x = frames[0]
    cot = cotangent[0]
    rows, cols, width = x.shape
    hidden = w_in.shape[1]
    space = lax.axis_size("x") * lax.axis_size("zh") * lax.axis_size("y")
    place = (lax.axis_index("x") * lax.axis_size("zh") + lax.axis_index("zh")) * lax.axis_size(
        "y"
    ) + lax.axis_index("y")
    frame_count = lax.axis_size("zl") * lax.axis_size("co")
    frame = lax.axis_index("zl") * lax.axis_size("co") + lax.axis_index("co")
    pixels = rows * space * cols
    factor = 1.0 / math.sqrt(frame_count * pixels)
    taps = jnp.broadcast_to(kernel[:, None], (9, STEP, hidden))
    gain = gain[None]
    order = place_matrix(cols)

    above, below = space_neighbours(x[-1:], x[:1])
    normed_t, expanded, cot_t, d_att = enter(x, gain, w_in, order, cot, w_out)
    *middle, middle_sums = convolution(tuple(range(1, rows - 1)), expanded, None, taps, d_att)
    halo_t, halo = enter_halo(above, below, gain, w_in, order)
    *edge, edge_sums = convolution((0, rows - 1), expanded, halo, taps, d_att)
    sums = jnp.sum((middle_sums + edge_sums).reshape(2, 8, width), 1)
    sums = sum_over_space(sums.reshape(8, LANES)).reshape(-1)
    out_term = outer(cot_t, middle, edge)
    sums, out_term = lax.optimization_barrier((sums, out_term))
    pooled = sums[:width] / pixels
    d_scale = sums[width:]
    scale = jnp.dot(pooled, w_att, precision=lax.Precision.HIGHEST)
    back = jnp.dot(d_scale, w_att.T, precision=lax.Precision.HIGHEST) / pixels
    to_above, to_below = edge_rows(
        edge, d_att, scale.reshape(-1, 1, LANES), back.reshape(-1, 1, LANES), taps, w_in
    )
    from_above, from_below = space_neighbours(to_below, to_above)
    mine = (jnp.arange(8)[None, :, None] == frame) & (place == 0)
    vectors = jnp.concatenate(
        [jnp.where(mine, v.reshape(-1, 1, LANES), 0.0) for v in (pooled, d_scale)], 1
    )
    me = lax.axis_index("co")
    d_exp_a, d_exp_b, send, keep = gradients(
        me, expanded, halo, taps, middle, edge, d_att, scale[None], back[None], out_term, vectors,
        normed_t, halo_t,
    )
    send, from_above, from_below = lax.optimization_barrier((send, from_above, from_below))
    own, (from_above, from_below) = sum_over_all(send, keep, (from_above, from_below))
    grad = input_grad(x, cot, d_exp_a, d_exp_b, from_above, from_below, gain, w_in, order)
    own, grad = lax.optimization_barrier((own, grad))
    other = lax.ppermute(own, "co", SWAP)
    in_sum, out_sum, att_sum, kernel_sum = unpack(
        own, other, me, hidden, width, factor
    )
    return grad, in_sum, kernel_sum, att_sum, out_sum


def solution(mesh):
    fine = Mesh(mesh.devices.reshape(2, 2, 4, 2, 4), ("zl", "co", "x", "zh", "y"))
    big = P(("zl", "co"), ("x", "zh", "y"), None, None)
    return jax.shard_map(
        local,
        mesh=fine,
        in_specs=(big, big, P(), P(), P(), P(), P()),
        out_specs=(big, P(), P(), P(), P()),
        check_vma=False,
    )
```

```python
import functools
import math

import jax
import jax.numpy as jnp
import numpy as np
from jax import lax
from jax.experimental import pallas as pl
from jax.experimental.pallas import tpu as pltpu
from jax.sharding import Mesh, PartitionSpec as P

EPS = 1e-06
BF = jnp.bfloat16
F32 = jnp.float32
LANES = 128
STEP = 16
SMALL = 48
VMEM = 56 * 1024 * 1024


def params(vmem=VMEM):
    return pltpu.CompilerParams(dimension_semantics=("arbitrary",), vmem_limit_bytes=vmem)


def layer_norm(x):
    xf = x.astype(F32)
    centered = xf - jnp.mean(xf, -1, keepdims=True)
    rstd = lax.rsqrt(jnp.mean(centered * centered, -1, keepdims=True) + EPS)
    return centered * rstd, rstd


def place_matrix(cols):
    place = np.arange(cols)[:, None]
    column = np.arange(cols)[None]
    return jnp.asarray(column == place % STEP * (cols // STEP) + place // STEP, BF)


def reorder(order, rows):
    return jnp.dot(order, rows, preferred_element_type=F32)


def neighbours(tile, first):
    zero = jnp.zeros((1, tile.shape[1]), F32)
    parts = [zero, tile[: STEP - 1]] if first else [tile[1:], zero]
    return jnp.concatenate(parts, 0)


def chunked(v):
    return [v[:, k * LANES : (k + 1) * LANES] for k in range(v.shape[1] // LANES)]


def tiled(v):
    return v.reshape(-1, STEP, LANES)


def flat(v):
    return v.reshape(-1, LANES)


def expand_row(x, gain_ref, w_ref, order, normed_t_ref, expanded_ref, r=0):
    cols = x.shape[0]
    xhat, _ = layer_norm(reorder(order, x))
    normed = (xhat * gain_ref[...]).astype(BF)
    normed_t_ref[:, r * cols : (r + 1) * cols] = normed.T
    for k, e in enumerate(chunked(jnp.dot(normed, w_ref[...], preferred_element_type=F32))):
        expanded_ref[k, r, 1 : 1 + cols // STEP] = tiled(e.astype(BF))
        expanded_ref[k, r, 0] = neighbours(e[cols - STEP :], True).astype(BF)
        expanded_ref[k, r, 1 + cols // STEP] = neighbours(e[:STEP], False).astype(BF)


def halo_kernel(
    odd_ref, first_ref, second_ref, gain_ref, w_ref, order_ref, normed_t_ref, expanded_ref
):
    early = (pl.program_id(0) == 0) == (odd_ref[0] == 1)
    x = jnp.where(early, first_ref[0].astype(F32), second_ref[0].astype(F32))
    expand_row(x.astype(BF), gain_ref, w_ref, order_ref[...], normed_t_ref, expanded_ref)


def enter_kernel(
    x_ref, gain_ref, w_ref, order_ref, cot_ref, wo_ref, normed_t_ref, expanded_ref, cot_t_ref, d_ref
):
    order = order_ref[...]
    placed = reorder(order, cot_ref[0]).astype(BF)
    cot_t_ref[...] = placed.T
    d_att = lax.dot_general(
        placed, wo_ref[...], (((1,), (1,)), ((), ())), preferred_element_type=F32
    )
    for k, d in enumerate(chunked(d_att)):
        d_ref[k, 0] = tiled(d.astype(BF))
    expand_row(x_ref[0], gain_ref, w_ref, order, normed_t_ref, expanded_ref)


def enter_specs(rows, cols, width, hidden):
    groups, tiles = hidden // LANES, cols // STEP
    specs = [
        pl.BlockSpec((width, cols), lambda r: (0, r)),
        pl.BlockSpec((groups, 1, tiles + 2, STEP, LANES), lambda r: (0, r, 0, 0, 0)),
    ]
    shapes = [
        jax.ShapeDtypeStruct((width, rows * cols), BF),
        jax.ShapeDtypeStruct((groups, rows, tiles + 2, STEP, LANES), BF),
    ]
    return specs, shapes


def whole(a):
    return pl.BlockSpec(a.shape, lambda r: (0,) * a.ndim)


def enter(x, gain, w_in, order, cot, w_out):
    rows, cols, width = x.shape
    chunks = width // LANES
    specs, shapes = enter_specs(rows, cols, width, w_in.shape[1])
    row = pl.BlockSpec((1, cols, width), lambda r: (r, 0, 0))
    return pl.pallas_call(
        enter_kernel,
        grid=(rows,),
        in_specs=[row, whole(gain), whole(w_in), whole(order), row, whole(w_out)],
        out_specs=specs
        + [specs[0], pl.BlockSpec((chunks, 1, cols // STEP, STEP, LANES), lambda r: (0, r, 0, 0, 0))],
        out_shape=shapes
        + [shapes[0], jax.ShapeDtypeStruct((chunks, rows, cols // STEP, STEP, LANES), BF)],
        compiler_params=params(),
        cost_estimate=pl.CostEstimate(
            flops=2 * rows * cols * width * width * 8,
            bytes_accessed=rows * cols * width * 12,
            transcendentals=0,
        ),
        name="enter",
    )(x, gain, w_in, order, cot, w_out)


def enter_halo(odd, first, second, gain, w_in, order):
    _, cols, width = first.shape
    specs, shapes = enter_specs(2, cols, width, w_in.shape[1])
    row = pl.BlockSpec((1, cols, width), lambda r: (0, 0, 0))
    return pl.pallas_call(
        halo_kernel,
        grid=(2,),
        in_specs=[pl.BlockSpec(memory_space=pltpu.SMEM), row, row]
        + [whole(a) for a in (gain, w_in, order)],
        out_specs=specs,
        out_shape=shapes,
        compiler_params=params(),
        name="enter_halo",
    )(odd.reshape(1), first, second, gain, w_in, order)


def row_tile(own_ref, halo_ref, r, t):
    rows = own_ref.shape[1]
    if r == 0:
        return halo_ref[0, 0, t]
    if r == rows + 1:
        return halo_ref[0, 1, t]
    return own_ref[0, r - 1, t]


def halves(v):
    return v[: STEP // 2] + v[STEP // 2 :]


def added(total, term):
    return term if total is None else total + term


def conv_kernel(
    ea_ref, eb_ref, ha_ref, hb_ref, ka_ref, kb_ref, d_ref, ca_ref, cb_ref, sum_ref
):
    _, rows, tiles, _, _ = d_ref.shape
    taps_a = [ka_ref[n].astype(F32) for n in range(9)]
    taps_b = [kb_ref[n].astype(F32) for n in range(9)]

    def convolve(own_ref, halo_ref, taps, t):
        total = [None] * rows
        for r in range(rows + 2):
            for j in range(3):
                v = row_tile(own_ref, halo_ref, r, t + j).astype(F32)
                for i in range(3):
                    if 0 <= r - i < rows:
                        total[r - i] = added(total[r - i], v * taps[3 * i + j])
        return total

    def body(t, sums):
        a = convolve(ea_ref, ha_ref, taps_a, t)
        b = convolve(eb_ref, hb_ref, taps_b, t)
        total = [None, None]
        for r in range(rows):
            here = (0, r, t)
            ca_ref[here] = a[r].astype(BF)
            cb_ref[here] = b[r].astype(BF)
            g = a[r] * b[r]
            total[0] = added(total[0], g)
            total[1] = added(total[1], g * d_ref[here].astype(F32))
        return sums[0] + halves(total[0]), sums[1] + halves(total[1])

    zero = jnp.zeros((STEP // 2, LANES), F32)
    pooled, weighted = lax.fori_loop(0, tiles, body, (zero, zero), unroll=1)
    sum_ref[0:8, :] = pooled
    sum_ref[8:16, :] = weighted


def chunk_spec(shape, offset=0):
    block = (1,) + tuple(shape[1:])
    return pl.BlockSpec(block, lambda k: (k + offset,) + (0,) * (len(shape) - 1))


def half_specs(a):
    return [chunk_spec(a.shape), chunk_spec(a.shape, a.shape[0] // 2)]


def tap_specs(taps, chunks):
    block = taps.shape[:2] + (LANES,)
    return [
        pl.BlockSpec(block, lambda k: (0, 0, k)),
        pl.BlockSpec(block, lambda k: (0, 0, k + chunks)),
    ]


def convolution(expanded, halo, taps, d_att):
    chunks = d_att.shape[0]
    part = chunk_spec(d_att.shape)
    shape = jax.ShapeDtypeStruct(d_att.shape, BF)
    return pl.pallas_call(
        conv_kernel,
        grid=(chunks,),
        in_specs=half_specs(expanded) + half_specs(halo) + tap_specs(taps, chunks) + [part],
        out_specs=[part, part, pl.BlockSpec((16, LANES), lambda k: (0, k))],
        out_shape=[shape, shape, jax.ShapeDtypeStruct((16, chunks * LANES), F32)],
        compiler_params=params(),
        cost_estimate=pl.CostEstimate(
            flops=d_att.size * 400, bytes_accessed=d_att.size * 14, transcendentals=0
        ),
        name="convolution",
    )(expanded, expanded, halo, halo, taps, taps, d_att)


def outer_kernel(cot_t_ref, ca_ref, cb_ref, out_ref):
    cols = ca_ref.shape[2] * STEP
    total = None
    for r in range(ca_ref.shape[1]):
        left = cot_t_ref[:, r * cols : (r + 1) * cols]
        gated = flat((ca_ref[0, r].astype(F32) * cb_ref[0, r].astype(F32)).astype(BF))
        total = added(total, jnp.dot(left, gated, preferred_element_type=F32))
    out_ref[0] = total


def outer(cot_t, conv_a, conv_b):
    chunks = conv_a.shape[0]
    shape = (chunks, cot_t.shape[0], LANES)
    return pl.pallas_call(
        outer_kernel,
        grid=(chunks,),
        in_specs=[whole(cot_t), chunk_spec(conv_a.shape), chunk_spec(conv_b.shape)],
        out_specs=chunk_spec(shape),
        out_shape=jax.ShapeDtypeStruct(shape, F32),
        compiler_params=params(),
        cost_estimate=pl.CostEstimate(
            flops=2 * cot_t.shape[0] * conv_a.size * 2,
            bytes_accessed=conv_a.size * 4,
            transcendentals=0,
        ),
        name="outer",
    )(cot_t, conv_a, conv_b)


def gradient_kernel(
    me_ref, ea_ref, eb_ref, ha_ref, hb_ref, ka_ref, kb_ref, ca_ref, cb_ref, d_ref, scale_ref, back_ref,
    out_ref, vec_ref, nt_ref, nh_ref, xa_ref, xb_ref, send_ref, keep_ref, da, db, nt, nh, sems,
):
    _, rows, tiles, _, _ = d_ref.shape
    cols = tiles * STEP
    scale = jnp.broadcast_to(scale_ref[...], (STEP, LANES))
    back = jnp.broadcast_to(back_ref[...], (STEP, LANES))
    copies = [
        pltpu.make_async_copy(nt_ref, nt, sems.at[0]),
        pltpu.make_async_copy(nh_ref, nh, sems.at[1]),
    ]

    @pl.when(pl.program_id(0) == 0)
    def _():
        for copy in copies:
            copy.start()

    def products(own_ref, halo_ref, own, t, sums):
        part = [None] * 9
        for r in range(rows + 2):
            for j in range(3):
                v = row_tile(own_ref, halo_ref, r, t + j).astype(F32)
                for i in range(3):
                    if 0 <= r - i < rows:
                        part[3 * i + j] = added(part[3 * i + j], v * own[r - i])
        return tuple(s + halves(p) for s, p in zip(sums, part))

    def first(own_ref, halo_ref, other_ref, d, t, sums):
        own = []
        for r in range(rows):
            dg = d_ref[0, r, t].astype(F32) * scale + back
            own.append(dg * other_ref[0, r, t].astype(F32))
            d[r, t + 1] = own[r].astype(BF)
        return products(own_ref, halo_ref, own, t, sums)

    nought = (jnp.zeros((STEP // 2, LANES), F32),) * 9
    sums = [
        lax.fori_loop(0, tiles, functools.partial(first, *refs), nought, unroll=2)
        for refs in ((ea_ref, ha_ref, cb_ref, da), (eb_ref, hb_ref, ca_ref, db))
    ]
    for d in (da, db):
        for r in range(rows):
            d[r, 0] = neighbours(d[r, tiles].astype(F32), True).astype(BF)
            d[r, tiles + 1] = neighbours(d[r, 1].astype(F32), False).astype(BF)

    taps_a = [ka_ref[n].astype(F32) for n in range(9)]
    taps_b = [kb_ref[n].astype(F32) for n in range(9)]

    def spread(d, taps, x_ref, t):
        total = [None] * (rows + 2)
        for r in range(rows):
            for j in range(3):
                v = d[r, t + 2 - j].astype(F32)
                for i in range(3):
                    total[r + i] = added(total[r + i], v * taps[3 * i + j])
        for r in range(rows + 2):
            x_ref[0, r, t] = total[r].astype(BF)

    for d, taps, x_ref in ((da, taps_a, xa_ref), (db, taps_b, xb_ref)):

        def second(t, carry, d=d, taps=taps, x_ref=x_ref):
            spread(d, taps, x_ref, t)
            return carry

        lax.fori_loop(0, tiles, second, 0, unroll=1)

    @pl.when(pl.program_id(0) == 0)
    def _():
        for copy in copies:
            copy.wait()

    total = None
    for r in range(rows + 2):
        if r == 0:
            left = nh[:, 0:cols]
        elif r == rows + 1:
            left = nh[:, cols : 2 * cols]
        else:
            left = nt[:, (r - 1) * cols : r * cols]
        right = jnp.concatenate([flat(xa_ref[0, r]), flat(xb_ref[0, r])], -1)
        total = added(total, jnp.dot(left, right, preferred_element_type=F32))
    width = total.shape[0]
    blank = jnp.zeros((7, LANES), F32)
    rows_of = lambda part: [jnp.sum(p, 0, keepdims=True) for p in part]
    small = jnp.concatenate([vec_ref[0], *rows_of(sums[0]), blank, *rows_of(sums[1]), blank], 0)

    def write(ref):
        ref[0, 0:width] = total[:, :LANES].astype(BF)
        ref[0, width : 2 * width] = total[:, LANES:].astype(BF)
        ref[0, 2 * width : 3 * width] = (out_ref[0] * scale_ref[...]).astype(BF)
        ref[0, 3 * width : 3 * width + SMALL] = small.astype(BF)
        ref[0, 3 * width + SMALL :] = jnp.zeros((width // 2 - SMALL, LANES), BF)

    early = pl.program_id(0) < pl.num_programs(0) // 2
    pl.when(early)(lambda: write(send_ref))
    pl.when(jnp.logical_not(early))(lambda: write(keep_ref))


def gradients(
    me, expanded, halo, taps, conv_a, conv_b, d_att, scale, back, out_term, vectors, normed_t, halo_t
):
    chunks, rows, tiles, _, _ = d_att.shape
    width = chunks * LANES
    half = chunks // 2
    chunk = lambda s, me: (s + half * (1 - me[0])) % chunks

    def by_chunk(a, offset=0):
        block = (1,) + tuple(a.shape[1:])
        return pl.BlockSpec(block, lambda s, me: (chunk(s, me) + offset,) + (0,) * (len(block) - 1))

    def by_half(a):
        return [by_chunk(a), by_chunk(a, chunks)]

    def lanes(a, offset=0):
        block = a.shape[:-1] + (LANES,)
        return pl.BlockSpec(
            block, lambda s, me: (0,) * (len(block) - 1) + (chunk(s, me) + offset,)
        )

    spread = jax.ShapeDtypeStruct((chunks, rows + 2, tiles, STEP, LANES), BF)
    part = jax.ShapeDtypeStruct((half, 7 * width // 2, LANES), BF)
    block = (1,) + part.shape[1:]
    return pl.pallas_call(
        gradient_kernel,
        grid_spec=pltpu.PrefetchScalarGridSpec(
            num_scalar_prefetch=1,
            grid=(chunks,),
            in_specs=by_half(expanded)
            + by_half(halo)
            + [lanes(taps), lanes(taps, chunks)]
            + [by_chunk(a) for a in (conv_a, conv_b, d_att)]
            + [lanes(scale), lanes(back), by_chunk(out_term), by_chunk(vectors)]
            + [pl.BlockSpec(memory_space=pl.ANY)] * 2,
            out_specs=[
                by_chunk(spread),
                by_chunk(spread),
                pl.BlockSpec(block, lambda s, me: (jnp.minimum(s, half - 1), 0, 0)),
                pl.BlockSpec(block, lambda s, me: (jnp.maximum(s - half, 0), 0, 0)),
            ],
            scratch_shapes=[pltpu.VMEM((rows, tiles + 2, STEP, LANES), BF)] * 2
            + [pltpu.VMEM(normed_t.shape, BF), pltpu.VMEM(halo_t.shape, BF)]
            + [pltpu.SemaphoreType.DMA((2,))],
        ),
        out_shape=[spread, spread, part, part],
        compiler_params=params(),
        cost_estimate=pl.CostEstimate(
            flops=d_att.size * 3000, bytes_accessed=d_att.size * 20, transcendentals=0
        ),
        name="gradients",
    )(
        me.reshape(1), expanded, expanded, halo, halo, taps, taps, conv_a, conv_b, d_att, scale, back,
        out_term, vectors, normed_t, halo_t,
    )


def back_project(xa_ref, xb_ref, w_ref):
    chunks = [flat(ref[k, 0]) for ref in (xa_ref, xb_ref) for k in range(ref.shape[0])]
    return lax.dot_general(
        jnp.concatenate(chunks, -1),
        w_ref[...],
        (((1,), (1,)), ((), ())),
        preferred_element_type=F32,
    )


def edge_kernel(
    odd_ref, ca_ref, cb_ref, d_ref, scale_ref, back_ref, taps_ref, w_ref, first_ref, second_ref
):
    side = (pl.program_id(0) + 1 - odd_ref[0]) % 2
    chunks = d_ref.shape[0]
    spread = [None] * (2 * chunks)
    for k in range(chunks):
        dg = d_ref[k, 0].astype(F32) * scale_ref[k] + back_ref[k]
        for n, ref in ((k, cb_ref), (chunks + k, ca_ref)):
            d = dg * ref[k, 0].astype(F32)
            before = neighbours(d[-1], True)[None]
            behind = neighbours(d[0], False)[None]
            windows = (
                jnp.concatenate([d[1:], behind], 0),
                d,
                jnp.concatenate([before, d[:-1]], 0),
            )
            total = None
            for j in range(3):
                tap = taps_ref[6 * side + j, :, n * LANES : (n + 1) * LANES].astype(F32)
                total = added(total, windows[j] * tap[None])
            spread[n] = flat(total.astype(BF))
    row = lax.dot_general(
        jnp.concatenate(spread, -1),
        w_ref[...],
        (((1,), (1,)), ((), ())),
        preferred_element_type=F32,
    ).astype(BF)

    @pl.when(pl.program_id(0) == 0)
    def _():
        first_ref[...] = row

    @pl.when(pl.program_id(0) == 1)
    def _():
        second_ref[...] = row


def edge_rows(odd, conv_a, conv_b, d_att, scale, back, taps, w_in):
    chunks, rows, tiles, _, _ = d_att.shape
    side = lambda e, odd: (e + 1 - odd[0]) % 2
    spec = pl.BlockSpec(
        (chunks, 1, tiles, STEP, LANES), lambda e, odd: (0, side(e, odd) * (rows - 1), 0, 0, 0)
    )
    out = jax.ShapeDtypeStruct((tiles * STEP, w_in.shape[0]), BF)
    full = lambda a: pl.BlockSpec(a.shape, lambda e, odd: (0,) * a.ndim)
    return pl.pallas_call(
        edge_kernel,
        grid_spec=pltpu.PrefetchScalarGridSpec(
            num_scalar_prefetch=1,
            grid=(2,),
            in_specs=[spec, spec, spec] + [full(a) for a in (scale, back, taps, w_in)],
            out_specs=[full(out)] * 2,
        ),
        out_shape=[out] * 2,
        compiler_params=params(),
        name="edge_rows",
    )(odd.reshape(1), conv_a, conv_b, d_att, scale, back, taps, w_in)


def input_kernel(
    odd_ref, x_ref, cot_ref, xa_ref, xb_ref, first_ref, second_ref, gain_ref, w_ref, order_ref, out_ref
):
    row = pl.program_id(0)
    last = pl.num_programs(0) - 1
    d_norm = back_project(xa_ref, xb_ref, w_ref)
    odd = odd_ref[0] == 1
    above, below = row == 0, row == last
    early = (above & odd) | (below & jnp.logical_not(odd))
    late = (above & jnp.logical_not(odd)) | (below & odd)
    d_norm = d_norm + jnp.where(early, 1.0, 0.0) * first_ref[...].astype(F32)
    d_norm = d_norm + jnp.where(late, 1.0, 0.0) * second_ref[...].astype(F32)
    d_norm = lax.dot_general(
        order_ref[...], d_norm.astype(BF), (((0,), (0,)), ((), ())), preferred_element_type=F32
    )
    xhat, rstd = layer_norm(x_ref[0])
    dxhat = d_norm * gain_ref[...]
    grad = cot_ref[0].astype(F32) + rstd * (
        dxhat - jnp.mean(dxhat, -1, keepdims=True) - xhat * jnp.mean(dxhat * xhat, -1, keepdims=True)
    )
    out_ref[0, 0] = grad.astype(BF)


def input_grad(odd, x, cot, xa, xb, first, second, gain, w_in, order):
    rows, cols, width = x.shape
    chunks = xa.shape[0]
    spec = pl.BlockSpec((1, cols, width), lambda r: (r, 0, 0))
    inner = pl.BlockSpec(
        (chunks, 1, cols // STEP, STEP, LANES), lambda r: (0, r + 1, 0, 0, 0)
    )
    return pl.pallas_call(
        input_kernel,
        grid=(rows,),
        in_specs=[pl.BlockSpec(memory_space=pltpu.SMEM), spec, spec, inner, inner]
        + [whole(a) for a in (first, second, gain, w_in, order)],
        out_specs=pl.BlockSpec((1, 1, cols, width), lambda r: (0, r, 0, 0)),
        out_shape=jax.ShapeDtypeStruct((1, rows, cols, width), BF),
        compiler_params=params(),
        cost_estimate=pl.CostEstimate(
            flops=2 * rows * cols * width * width * 6,
            bytes_accessed=rows * cols * width * 10,
            transcendentals=0,
        ),
        name="input_grad",
    )(odd.reshape(1), x, cot, xa, xb, first, second, gain, w_in, order)


def unpack_kernel(factor, me_ref, own_ref, other_ref, in_ref, out_ref, att_ref, taps_ref):
    step = pl.program_id(0)
    first = me_ref[0] == 0
    half = own_ref.shape[0]
    chunks = 2 * half
    width = chunks * LANES

    def rows(k, start, count):
        own = own_ref[k % half, pl.ds(start, count)].astype(F32)
        other = other_ref[k % half, pl.ds(start, count)].astype(F32)
        return jnp.where(first, own, other) if k < half else jnp.where(first, other, own)

    start = pl.multiple_of(step * LANES, LANES)
    for k in range(chunks):
        here = slice(k * LANES, (k + 1) * LANES)
        in_ref[:, here] = rows(k, start, LANES) * factor
        in_ref[:, width + k * LANES : width + (k + 1) * LANES] = (
            rows(k, start + width, LANES) * factor
        )
        out_ref[here, pl.ds(start, LANES)] = rows(k, start + 2 * width, LANES).T * factor

    @pl.when(step == 0)
    def _():
        small = [rows(k, 3 * width, SMALL) for k in range(chunks)]
        for k in range(chunks):
            here = slice(k * LANES, (k + 1) * LANES)
            taps_ref[:, here] = small[k][16:25] * factor
            taps_ref[:, width + k * LANES : width + (k + 1) * LANES] = small[k][32:41] * factor
            for m in range(chunks):
                block = lax.dot_general(
                    small[k][0:8].astype(BF),
                    small[m][8:16].astype(BF),
                    (((0,), (0,)), ((), ())),
                    preferred_element_type=F32,
                )
                att_ref[here, m * LANES : (m + 1) * LANES] = block * factor


def unpack(own, other, me, hidden, width, factor):
    full = jax.ShapeDtypeStruct((width, width), F32)
    return pl.pallas_call(
        functools.partial(unpack_kernel, factor),
        grid=(width // LANES,),
        in_specs=[pl.BlockSpec(memory_space=pltpu.SMEM), whole(own), whole(other)],
        out_specs=[
            pl.BlockSpec((LANES, hidden), lambda s: (s, 0)),
            whole(full),
            whole(full),
            pl.BlockSpec((9, hidden), lambda s: (0, 0)),
        ],
        out_shape=[
            jax.ShapeDtypeStruct((width, hidden), F32),
            full,
            full,
            jax.ShapeDtypeStruct((9, hidden), F32),
        ],
        compiler_params=params(vmem=16 * 1024 * 1024),
        name="unpack",
    )(me.reshape(1), own, other)


def exchange_pairs(first, second):
    count = lax.axis_size(SPACE)
    inner = [(i, i ^ 1) for i in range(count)]
    outer_pairs = [(i, i + 1) for i in range(1, count - 1, 2)]
    crossing = outer_pairs + [(t, s) for s, t in outer_pairs]
    return lax.ppermute(first, SPACE, inner), lax.ppermute(second, SPACE, crossing)


SPACE = ("x", "zh", "y")
CHIPS = ("zl", "x", "zh", "y")
SWAP = [(0, 1), (1, 0)]


def sum_over_space(v):
    n = lax.axis_size(SPACE)
    copies = lax.optimization_barrier(jnp.broadcast_to(v[None], (n,) + v.shape))
    return jnp.sum(lax.all_to_all(copies, SPACE, 0, 0, tiled=True), 0)


def sum_over_all(send, keep, later):
    n = lax.axis_size(CHIPS)
    other = lax.ppermute(send, "co", SWAP)
    own = (keep.astype(F32) + other.astype(F32)).astype(BF)
    own = lax.optimization_barrier(own.reshape(n, -1, LANES))
    parts = lax.all_to_all(own, CHIPS, 0, 0, tiled=True)
    part = jnp.sum(parts.astype(F32), 0).astype(BF)
    part, later = lax.optimization_barrier((part, later))
    copies = lax.optimization_barrier(jnp.broadcast_to(part[None], parts.shape))
    own = lax.all_to_all(copies, CHIPS, 0, 0, tiled=True)
    return own.reshape(keep.shape), later


def local(frames, cotangent, gain, w_in, kernel, w_att, w_out):
    x = frames[0]
    cot = cotangent[0]
    rows, cols, width = x.shape
    hidden = w_in.shape[1]
    space = lax.axis_size("x") * lax.axis_size("zh") * lax.axis_size("y")
    place = (lax.axis_index("x") * lax.axis_size("zh") + lax.axis_index("zh")) * lax.axis_size(
        "y"
    ) + lax.axis_index("y")
    frame_count = lax.axis_size("zl") * lax.axis_size("co")
    frame = lax.axis_index("zl") * lax.axis_size("co") + lax.axis_index("co")
    pixels = rows * space * cols
    factor = 1.0 / math.sqrt(frame_count * pixels)
    taps = jnp.broadcast_to(kernel[:, None], (9, STEP, hidden))
    gain = gain[None]
    order = place_matrix(cols)

    odd = place % 2
    edge_row = lambda r: lax.dynamic_slice_in_dim(x, r, 1, 0)
    first, second = exchange_pairs(
        edge_row((1 - odd) * (rows - 1)), edge_row(odd * (rows - 1))
    )
    normed_t, expanded, cot_t, d_att = enter(x, gain, w_in, order, cot, w_out)
    halo_t, halo = enter_halo(odd, first, second, gain, w_in, order)
    conv_a, conv_b, sums = convolution(expanded, halo, taps, d_att)
    sums = jnp.sum(sums.reshape(2, 8, width), 1)
    sums = sum_over_space(sums.reshape(8, LANES)).reshape(-1)
    out_term = outer(cot_t, conv_a, conv_b)
    sums, out_term = lax.optimization_barrier((sums, out_term))
    pooled = sums[:width] / pixels
    d_scale = sums[width:]
    scale = jnp.dot(pooled, w_att, precision=lax.Precision.HIGHEST)
    back = jnp.dot(d_scale, w_att.T, precision=lax.Precision.HIGHEST) / pixels
    first, second = edge_rows(
        odd, conv_a, conv_b, d_att, scale.reshape(-1, 1, LANES), back.reshape(-1, 1, LANES), taps, w_in
    )
    first, second = exchange_pairs(first, second)
    mine = (jnp.arange(8)[None, :, None] == frame) & (place == 0)
    vectors = jnp.concatenate(
        [jnp.where(mine, v.reshape(-1, 1, LANES), 0.0) for v in (pooled, d_scale)], 1
    )
    me = lax.axis_index("co")
    d_exp_a, d_exp_b, send, keep = gradients(
        me, expanded, halo, taps, conv_a, conv_b, d_att, scale[None], back[None], out_term, vectors,
        normed_t, halo_t,
    )
    send, first, second = lax.optimization_barrier((send, first, second))
    own, (first, second) = sum_over_all(send, keep, (first, second))
    grad = input_grad(odd, x, cot, d_exp_a, d_exp_b, first, second, gain, w_in, order)
    own, grad = lax.optimization_barrier((own, grad))
    other = lax.ppermute(own, "co", SWAP)
    in_sum, out_sum, att_sum, kernel_sum = unpack(
        own, other, me, hidden, width, factor
    )
    return grad, in_sum, kernel_sum, att_sum, out_sum


def solution(mesh):
    fine = Mesh(mesh.devices.reshape(2, 2, 4, 2, 4), ("zl", "co", "x", "zh", "y"))
    big = P(("zl", "co"), ("x", "zh", "y"), None, None)
    return jax.shard_map(
        local,
        mesh=fine,
        in_specs=(big, big, P(), P(), P(), P(), P()),
        out_specs=(big, P(), P(), P(), P()),
        check_vma=False,
    )
```

```python
import functools
import math

import jax
import jax.numpy as jnp
import numpy as np
from jax import lax
from jax.experimental import pallas as pl
from jax.experimental.pallas import tpu as pltpu
from jax.sharding import Mesh, PartitionSpec as P

EPS = 1e-06
BF = jnp.bfloat16
F32 = jnp.float32
LANES = 128
STEP = 16
SMALL = 48
VMEM = 56 * 1024 * 1024


def params(vmem=VMEM):
    return pltpu.CompilerParams(dimension_semantics=("arbitrary",), vmem_limit_bytes=vmem)


def layer_norm(x):
    xf = x.astype(F32)
    centered = xf - jnp.mean(xf, -1, keepdims=True)
    rstd = lax.rsqrt(jnp.mean(centered * centered, -1, keepdims=True) + EPS)
    return centered * rstd, rstd


def place_matrix(cols):
    place = np.arange(cols)[:, None]
    column = np.arange(cols)[None]
    return jnp.asarray(column == place % STEP * (cols // STEP) + place // STEP, BF)


def reorder(order, rows):
    return jnp.dot(order, rows, preferred_element_type=F32)


def neighbours(tile, first):
    zero = jnp.zeros((1, tile.shape[1]), F32)
    parts = [zero, tile[: STEP - 1]] if first else [tile[1:], zero]
    return jnp.concatenate(parts, 0)


def chunked(v):
    return [v[:, k * LANES : (k + 1) * LANES] for k in range(v.shape[1] // LANES)]


def tiled(v):
    return v.reshape(-1, STEP, LANES)


def flat(v):
    return v.reshape(-1, LANES)


def expand_row(x, gain_ref, w_ref, order, normed_t_ref, expanded_ref, r=0):
    cols = x.shape[0]
    xhat, _ = layer_norm(reorder(order, x))
    normed = (xhat * gain_ref[...]).astype(BF)
    normed_t_ref[:, r * cols : (r + 1) * cols] = normed.T
    for k, e in enumerate(chunked(jnp.dot(normed, w_ref[...], preferred_element_type=F32))):
        expanded_ref[k, r, 1 : 1 + cols // STEP] = tiled(e.astype(BF))
        expanded_ref[k, r, 0] = neighbours(e[cols - STEP :], True).astype(BF)
        expanded_ref[k, r, 1 + cols // STEP] = neighbours(e[:STEP], False).astype(BF)


def halo_kernel(
    odd_ref, first_ref, second_ref, gain_ref, w_ref, order_ref, normed_t_ref, expanded_ref
):
    early = (pl.program_id(0) == 0) == (odd_ref[0] == 1)
    x = jnp.where(early, first_ref[0].astype(F32), second_ref[0].astype(F32))
    expand_row(x.astype(BF), gain_ref, w_ref, order_ref[...], normed_t_ref, expanded_ref)


def enter_kernel(
    x_ref, gain_ref, w_ref, order_ref, cot_ref, wo_ref, normed_t_ref, expanded_ref, cot_t_ref, d_ref
):
    order = order_ref[...]
    placed = reorder(order, cot_ref[0]).astype(BF)
    cot_t_ref[...] = placed.T
    d_att = lax.dot_general(
        placed, wo_ref[...], (((1,), (1,)), ((), ())), preferred_element_type=F32
    )
    for k, d in enumerate(chunked(d_att)):
        d_ref[k, 0] = tiled(d.astype(BF))
    expand_row(x_ref[0], gain_ref, w_ref, order, normed_t_ref, expanded_ref)


def enter_specs(rows, cols, width, hidden):
    groups, tiles = hidden // LANES, cols // STEP
    specs = [
        pl.BlockSpec((width, cols), lambda r: (0, r)),
        pl.BlockSpec((groups, 1, tiles + 2, STEP, LANES), lambda r: (0, r, 0, 0, 0)),
    ]
    shapes = [
        jax.ShapeDtypeStruct((width, rows * cols), BF),
        jax.ShapeDtypeStruct((groups, rows, tiles + 2, STEP, LANES), BF),
    ]
    return specs, shapes


def whole(a):
    return pl.BlockSpec(a.shape, lambda r: (0,) * a.ndim)


def enter(x, gain, w_in, order, cot, w_out):
    rows, cols, width = x.shape
    chunks = width // LANES
    specs, shapes = enter_specs(rows, cols, width, w_in.shape[1])
    row = pl.BlockSpec((1, cols, width), lambda r: (r, 0, 0))
    return pl.pallas_call(
        enter_kernel,
        grid=(rows,),
        in_specs=[row, whole(gain), whole(w_in), whole(order), row, whole(w_out)],
        out_specs=specs
        + [specs[0], pl.BlockSpec((chunks, 1, cols // STEP, STEP, LANES), lambda r: (0, r, 0, 0, 0))],
        out_shape=shapes
        + [shapes[0], jax.ShapeDtypeStruct((chunks, rows, cols // STEP, STEP, LANES), BF)],
        compiler_params=params(),
        cost_estimate=pl.CostEstimate(
            flops=2 * rows * cols * width * width * 8,
            bytes_accessed=rows * cols * width * 12,
            transcendentals=0,
        ),
        name="enter",
    )(x, gain, w_in, order, cot, w_out)


def enter_halo(odd, first, second, gain, w_in, order):
    _, cols, width = first.shape
    specs, shapes = enter_specs(2, cols, width, w_in.shape[1])
    row = pl.BlockSpec((1, cols, width), lambda r: (0, 0, 0))
    return pl.pallas_call(
        halo_kernel,
        grid=(2,),
        in_specs=[pl.BlockSpec(memory_space=pltpu.SMEM), row, row]
        + [whole(a) for a in (gain, w_in, order)],
        out_specs=specs,
        out_shape=shapes,
        compiler_params=params(),
        name="enter_halo",
    )(odd.reshape(1), first, second, gain, w_in, order)


def row_tile(own_ref, halo_ref, r, t):
    rows = own_ref.shape[1]
    if r == 0:
        return halo_ref[0, 0, t]
    if r == rows + 1:
        return halo_ref[0, 1, t]
    return own_ref[0, r - 1, t]


def halves(v):
    return v[: STEP // 2] + v[STEP // 2 :]


def spread_taps(taps_ref):
    return [taps_ref[n].astype(F32) for n in range(9)]


def added(total, term):
    return term if total is None else total + term


def conv_kernel(
    ea_ref, eb_ref, ha_ref, hb_ref, ka_ref, kb_ref, d_ref, ca_ref, cb_ref, sum_ref
):
    _, rows, tiles, _, _ = d_ref.shape
    taps_a, taps_b = spread_taps(ka_ref), spread_taps(kb_ref)

    def convolve(own_ref, halo_ref, taps, t):
        total = [None] * rows
        for r in range(rows + 2):
            for j in range(3):
                v = row_tile(own_ref, halo_ref, r, t + j).astype(F32)
                for i in range(3):
                    if 0 <= r - i < rows:
                        total[r - i] = added(total[r - i], v * taps[3 * i + j])
        return total

    def body(t, sums):
        a = convolve(ea_ref, ha_ref, taps_a, t)
        b = convolve(eb_ref, hb_ref, taps_b, t)
        total = [None, None]
        for r in range(rows):
            here = (0, r, t)
            ca_ref[here] = a[r].astype(BF)
            cb_ref[here] = b[r].astype(BF)
            g = a[r] * b[r]
            total[0] = added(total[0], g)
            total[1] = added(total[1], g * d_ref[here].astype(F32))
        return sums[0] + halves(total[0]), sums[1] + halves(total[1])

    zero = jnp.zeros((STEP // 2, LANES), F32)
    pooled, weighted = lax.fori_loop(0, tiles, body, (zero, zero), unroll=1)
    chunk, chunks = pl.program_id(0), pl.num_programs(0)
    sum_ref[pl.ds(chunk, 1), :] = jnp.sum(pooled, 0, keepdims=True)
    sum_ref[pl.ds(chunks + chunk, 1), :] = jnp.sum(weighted, 0, keepdims=True)


def chunk_spec(shape, offset=0):
    block = (1,) + tuple(shape[1:])
    return pl.BlockSpec(block, lambda k: (k + offset,) + (0,) * (len(shape) - 1))


def half_specs(a):
    return [chunk_spec(a.shape), chunk_spec(a.shape, a.shape[0] // 2)]


def tap_specs(taps, chunks):
    block = taps.shape[:2] + (LANES,)
    return [
        pl.BlockSpec(block, lambda k: (0, 0, k)),
        pl.BlockSpec(block, lambda k: (0, 0, k + chunks)),
    ]


def convolution(expanded, halo, taps, d_att):
    chunks = d_att.shape[0]
    part = chunk_spec(d_att.shape)
    shape = jax.ShapeDtypeStruct(d_att.shape, BF)
    return pl.pallas_call(
        conv_kernel,
        grid=(chunks,),
        in_specs=half_specs(expanded) + half_specs(halo) + tap_specs(taps, chunks) + [part],
        out_specs=[part, part, pl.BlockSpec((2 * chunks, LANES), lambda k: (0, 0))],
        out_shape=[shape, shape, jax.ShapeDtypeStruct((2 * chunks, LANES), F32)],
        compiler_params=params(),
        cost_estimate=pl.CostEstimate(
            flops=d_att.size * 400, bytes_accessed=d_att.size * 14, transcendentals=0
        ),
        name="convolution",
    )(expanded, expanded, halo, halo, taps, taps, d_att)


def outer_kernel(cot_t_ref, ca_ref, cb_ref, out_ref):
    cols = ca_ref.shape[2] * STEP
    total = None
    for r in range(ca_ref.shape[1]):
        left = cot_t_ref[:, r * cols : (r + 1) * cols]
        gated = flat((ca_ref[0, r].astype(F32) * cb_ref[0, r].astype(F32)).astype(BF))
        total = added(total, jnp.dot(left, gated, preferred_element_type=F32))
    out_ref[0] = total


def outer(cot_t, conv_a, conv_b):
    chunks = conv_a.shape[0]
    shape = (chunks, cot_t.shape[0], LANES)
    return pl.pallas_call(
        outer_kernel,
        grid=(chunks,),
        in_specs=[whole(cot_t), chunk_spec(conv_a.shape), chunk_spec(conv_b.shape)],
        out_specs=chunk_spec(shape),
        out_shape=jax.ShapeDtypeStruct(shape, F32),
        compiler_params=params(),
        cost_estimate=pl.CostEstimate(
            flops=2 * cot_t.shape[0] * conv_a.size * 2,
            bytes_accessed=conv_a.size * 4,
            transcendentals=0,
        ),
        name="outer",
    )(cot_t, conv_a, conv_b)


def gradient_kernel(
    me_ref, ea_ref, eb_ref, ha_ref, hb_ref, ka_ref, kb_ref, ca_ref, cb_ref, d_ref, scale_ref, back_ref,
    out_ref, vec_ref, nt_ref, nh_ref, xa_ref, xb_ref, send_ref, keep_ref, da, db, nt, nh, sems,
):
    _, rows, tiles, _, _ = d_ref.shape
    cols = tiles * STEP
    scale = jnp.broadcast_to(scale_ref[...], (STEP, LANES))
    back = jnp.broadcast_to(back_ref[...], (STEP, LANES))
    copies = [
        pltpu.make_async_copy(nt_ref, nt, sems.at[0]),
        pltpu.make_async_copy(nh_ref, nh, sems.at[1]),
    ]

    @pl.when(pl.program_id(0) == 0)
    def _():
        for copy in copies:
            copy.start()

    def products(own_ref, halo_ref, own, t, sums):
        part = [None] * 9
        for r in range(rows + 2):
            for j in range(3):
                v = row_tile(own_ref, halo_ref, r, t + j).astype(F32)
                for i in range(3):
                    if 0 <= r - i < rows:
                        part[3 * i + j] = added(part[3 * i + j], v * own[r - i])
        return tuple(s + halves(p) for s, p in zip(sums, part))

    def first(own_ref, halo_ref, other_ref, d, t, sums):
        own = []
        for r in range(rows):
            dg = d_ref[0, r, t].astype(F32) * scale + back
            own.append(dg * other_ref[0, r, t].astype(F32))
            d[r, t + 1] = own[r].astype(BF)
        return products(own_ref, halo_ref, own, t, sums)

    nought = (jnp.zeros((STEP // 2, LANES), F32),) * 9
    sums = [
        lax.fori_loop(0, tiles, functools.partial(first, *refs), nought, unroll=2)
        for refs in ((ea_ref, ha_ref, cb_ref, da), (eb_ref, hb_ref, ca_ref, db))
    ]
    for d in (da, db):
        for r in range(rows):
            d[r, 0] = neighbours(d[r, tiles].astype(F32), True).astype(BF)
            d[r, tiles + 1] = neighbours(d[r, 1].astype(F32), False).astype(BF)

    taps_a, taps_b = spread_taps(ka_ref), spread_taps(kb_ref)

    def spread(d, taps, x_ref, t):
        total = [None] * (rows + 2)
        for r in range(rows):
            for j in range(3):
                v = d[r, t + 2 - j].astype(F32)
                for i in range(3):
                    total[r + i] = added(total[r + i], v * taps[3 * i + j])
        for r in range(rows + 2):
            x_ref[0, r, t] = total[r].astype(BF)

    for d, taps, x_ref in ((da, taps_a, xa_ref), (db, taps_b, xb_ref)):

        def second(t, carry, d=d, taps=taps, x_ref=x_ref):
            spread(d, taps, x_ref, t)
            return carry

        lax.fori_loop(0, tiles, second, 0, unroll=1)

    @pl.when(pl.program_id(0) == 0)
    def _():
        for copy in copies:
            copy.wait()

    total = None
    for r in range(rows + 2):
        if r == 0:
            left = nh[:, 0:cols]
        elif r == rows + 1:
            left = nh[:, cols : 2 * cols]
        else:
            left = nt[:, (r - 1) * cols : r * cols]
        right = jnp.concatenate([flat(xa_ref[0, r]), flat(xb_ref[0, r])], -1)
        total = added(total, jnp.dot(left, right, preferred_element_type=F32))
    width = total.shape[0]
    blank = jnp.zeros((7, LANES), F32)
    rows_of = lambda part: [jnp.sum(p, 0, keepdims=True) for p in part]
    small = jnp.concatenate([vec_ref[0], *rows_of(sums[0]), blank, *rows_of(sums[1]), blank], 0)

    def write(ref):
        ref[0, 0:width] = total[:, :LANES].astype(BF)
        ref[0, width : 2 * width] = total[:, LANES:].astype(BF)
        ref[0, 2 * width : 3 * width] = (out_ref[0] * scale_ref[...]).astype(BF)
        ref[0, 3 * width : 3 * width + SMALL] = small.astype(BF)
        ref[0, 3 * width + SMALL :] = jnp.zeros((width // 2 - SMALL, LANES), BF)

    early = pl.program_id(0) < pl.num_programs(0) // 2
    pl.when(early)(lambda: write(send_ref))
    pl.when(jnp.logical_not(early))(lambda: write(keep_ref))


def gradients(
    me, expanded, halo, taps, conv_a, conv_b, d_att, scale, back, out_term, vectors, normed_t, halo_t
):
    chunks, rows, tiles, _, _ = d_att.shape
    width = chunks * LANES
    half = chunks // 2
    chunk = lambda s, me: (s + half * (1 - me[0])) % chunks

    def by_chunk(a, offset=0):
        block = (1,) + tuple(a.shape[1:])
        return pl.BlockSpec(block, lambda s, me: (chunk(s, me) + offset,) + (0,) * (len(block) - 1))

    def by_half(a):
        return [by_chunk(a), by_chunk(a, chunks)]

    def lanes(a, offset=0):
        block = a.shape[:-1] + (LANES,)
        return pl.BlockSpec(
            block, lambda s, me: (0,) * (len(block) - 1) + (chunk(s, me) + offset,)
        )

    spread = jax.ShapeDtypeStruct((chunks, rows + 2, tiles, STEP, LANES), BF)
    part = jax.ShapeDtypeStruct((half, 7 * width // 2, LANES), BF)
    block = (1,) + part.shape[1:]
    return pl.pallas_call(
        gradient_kernel,
        grid_spec=pltpu.PrefetchScalarGridSpec(
            num_scalar_prefetch=1,
            grid=(chunks,),
            in_specs=by_half(expanded)
            + by_half(halo)
            + [lanes(taps), lanes(taps, chunks)]
            + [by_chunk(a) for a in (conv_a, conv_b, d_att)]
            + [lanes(scale), lanes(back), by_chunk(out_term), by_chunk(vectors)]
            + [pl.BlockSpec(memory_space=pl.ANY)] * 2,
            out_specs=[
                by_chunk(spread),
                by_chunk(spread),
                pl.BlockSpec(block, lambda s, me: (jnp.minimum(s, half - 1), 0, 0)),
                pl.BlockSpec(block, lambda s, me: (jnp.maximum(s - half, 0), 0, 0)),
            ],
            scratch_shapes=[pltpu.VMEM((rows, tiles + 2, STEP, LANES), BF)] * 2
            + [pltpu.VMEM(normed_t.shape, BF), pltpu.VMEM(halo_t.shape, BF)]
            + [pltpu.SemaphoreType.DMA((2,))],
        ),
        out_shape=[spread, spread, part, part],
        compiler_params=params(),
        cost_estimate=pl.CostEstimate(
            flops=d_att.size * 3000, bytes_accessed=d_att.size * 20, transcendentals=0
        ),
        name="gradients",
    )(
        me.reshape(1), expanded, expanded, halo, halo, taps, taps, conv_a, conv_b, d_att, scale, back,
        out_term, vectors, normed_t, halo_t,
    )


def back_project(xa_ref, xb_ref, w_ref):
    chunks = [flat(ref[k, 0]) for ref in (xa_ref, xb_ref) for k in range(ref.shape[0])]
    return lax.dot_general(
        jnp.concatenate(chunks, -1),
        w_ref[...],
        (((1,), (1,)), ((), ())),
        preferred_element_type=F32,
    )


def edge_kernel(
    pixels, at_ref, ca_ref, cb_ref, d_ref, sums_ref, att_ref, taps_ref, w_ref,
    first_ref, second_ref, scale_ref, back_ref, vec_ref,
):
    side = (pl.program_id(0) + 1 - at_ref[0]) % 2

    @pl.when(pl.program_id(0) == 0)
    def _():
        sums = jnp.sum(sums_ref[...], 0)
        half = sums.shape[0] // 2
        line = lambda rows: jnp.concatenate([rows[k : k + 1] for k in range(half)], -1)
        eight = lambda row: jnp.broadcast_to(row, (8, row.shape[1]))
        exact = dict(precision=lax.Precision.HIGHEST, preferred_element_type=F32)
        pooled = sums[:half] / pixels
        scale_ref[...] = jnp.dot(eight(line(pooled)), att_ref[...], **exact)[:1]
        back = lax.dot_general(
            eight(line(sums[half:])), att_ref[...], (((1,), (1,)), ((), ())), **exact
        )
        back_ref[...] = back[:1] / pixels
        row = lax.broadcasted_iota(jnp.int32, (8, LANES), 0)
        mine = row == jnp.where(at_ref[2] == 0, at_ref[1], 8)
        for k in range(half):
            for n, v in enumerate((pooled[k : k + 1], sums[half + k : half + k + 1])):
                rows = jnp.where(mine, jnp.broadcast_to(v, (8, LANES)), 0.0)
                vec_ref[k, 8 * n : 8 * n + 8] = rows

    scale, back = scale_ref[...], back_ref[...]
    every = taps_ref[...].astype(F32)
    taps = jnp.where(side == 0, every[0:3], every[6:9])
    chunks = d_ref.shape[0]
    spread = [None] * (2 * chunks)
    for k in range(chunks):
        here = slice(k * LANES, (k + 1) * LANES)
        dg = d_ref[k, 0].astype(F32) * scale[:, here] + back[:, here]
        for n, ref in ((k, cb_ref), (chunks + k, ca_ref)):
            d = dg * ref[k, 0].astype(F32)
            before = neighbours(d[-1], True)[None]
            behind = neighbours(d[0], False)[None]
            windows = (
                jnp.concatenate([d[1:], behind], 0),
                d,
                jnp.concatenate([before, d[:-1]], 0),
            )
            total = None
            for j in range(3):
                tap = taps[j : j + 1, n * LANES : (n + 1) * LANES]
                total = added(total, windows[j] * tap[None])
            spread[n] = flat(total.astype(BF))
    row = lax.dot_general(
        jnp.concatenate(spread, -1),
        w_ref[...],
        (((1,), (1,)), ((), ())),
        preferred_element_type=F32,
    ).astype(BF)

    @pl.when(pl.program_id(0) == 0)
    def _():
        first_ref[...] = row

    @pl.when(pl.program_id(0) == 1)
    def _():
        second_ref[...] = row


def edge_rows(at, conv_a, conv_b, d_att, sums, w_att, taps, w_in, pixels):
    chunks, rows, tiles, _, _ = d_att.shape
    side = lambda e, at: (e + 1 - at[0]) % 2
    spec = pl.BlockSpec(
        (chunks, 1, tiles, STEP, LANES), lambda e, at: (0, side(e, at) * (rows - 1), 0, 0, 0)
    )
    out = jax.ShapeDtypeStruct((tiles * STEP, w_in.shape[0]), BF)
    line = jax.ShapeDtypeStruct((1, chunks * LANES), F32)
    outs = [out, out, line, line, jax.ShapeDtypeStruct((chunks, 16, LANES), F32)]
    full = lambda a: pl.BlockSpec(a.shape, lambda e, at: (0,) * a.ndim)
    return pl.pallas_call(
        functools.partial(edge_kernel, pixels),
        grid_spec=pltpu.PrefetchScalarGridSpec(
            num_scalar_prefetch=1,
            grid=(2,),
            in_specs=[spec, spec, spec] + [full(a) for a in (sums, w_att, taps, w_in)],
            out_specs=[full(a) for a in outs],
        ),
        out_shape=outs,
        compiler_params=params(),
        name="edge_rows",
    )(at, conv_a, conv_b, d_att, sums, w_att, taps, w_in)


def input_kernel(
    odd_ref, x_ref, cot_ref, xa_ref, xb_ref, first_ref, second_ref, gain_ref, w_ref, order_ref, out_ref
):
    row = pl.program_id(0)
    last = pl.num_programs(0) - 1
    d_norm = back_project(xa_ref, xb_ref, w_ref)
    odd = odd_ref[0] == 1
    above, below = row == 0, row == last
    early = (above & odd) | (below & jnp.logical_not(odd))
    late = (above & jnp.logical_not(odd)) | (below & odd)
    d_norm = d_norm + jnp.where(early, 1.0, 0.0) * first_ref[...].astype(F32)
    d_norm = d_norm + jnp.where(late, 1.0, 0.0) * second_ref[...].astype(F32)
    d_norm = lax.dot_general(
        order_ref[...], d_norm.astype(BF), (((0,), (0,)), ((), ())), preferred_element_type=F32
    )
    xhat, rstd = layer_norm(x_ref[0])
    dxhat = d_norm * gain_ref[...]
    grad = cot_ref[0].astype(F32) + rstd * (
        dxhat - jnp.mean(dxhat, -1, keepdims=True) - xhat * jnp.mean(dxhat * xhat, -1, keepdims=True)
    )
    out_ref[0, 0] = grad.astype(BF)


def input_grad(odd, x, cot, xa, xb, first, second, gain, w_in, order):
    rows, cols, width = x.shape
    chunks = xa.shape[0]
    spec = pl.BlockSpec((1, cols, width), lambda r: (r, 0, 0))
    inner = pl.BlockSpec(
        (chunks, 1, cols // STEP, STEP, LANES), lambda r: (0, r + 1, 0, 0, 0)
    )
    return pl.pallas_call(
        input_kernel,
        grid=(rows,),
        in_specs=[pl.BlockSpec(memory_space=pltpu.SMEM), spec, spec, inner, inner]
        + [whole(a) for a in (first, second, gain, w_in, order)],
        out_specs=pl.BlockSpec((1, 1, cols, width), lambda r: (0, r, 0, 0)),
        out_shape=jax.ShapeDtypeStruct((1, rows, cols, width), BF),
        compiler_params=params(),
        cost_estimate=pl.CostEstimate(
            flops=2 * rows * cols * width * width * 6,
            bytes_accessed=rows * cols * width * 10,
            transcendentals=0,
        ),
        name="input_grad",
    )(odd.reshape(1), x, cot, xa, xb, first, second, gain, w_in, order)


def unpack_kernel(factor, me_ref, own_ref, other_ref, in_ref, out_ref, att_ref, taps_ref):
    step = pl.program_id(0)
    first = me_ref[0] == 0
    half = own_ref.shape[0]
    chunks = 2 * half
    width = chunks * LANES

    def rows(k, start, count):
        own = own_ref[k % half, pl.ds(start, count)].astype(F32)
        other = other_ref[k % half, pl.ds(start, count)].astype(F32)
        return jnp.where(first, own, other) if k < half else jnp.where(first, other, own)

    start = pl.multiple_of(step * LANES, LANES)
    for k in range(chunks):
        here = slice(k * LANES, (k + 1) * LANES)
        in_ref[:, here] = rows(k, start, LANES) * factor
        in_ref[:, width + k * LANES : width + (k + 1) * LANES] = (
            rows(k, start + width, LANES) * factor
        )
        out_ref[here, pl.ds(start, LANES)] = rows(k, start + 2 * width, LANES).T * factor

    @pl.when(step == 0)
    def _():
        small = [rows(k, 3 * width, SMALL) for k in range(chunks)]
        for k in range(chunks):
            here = slice(k * LANES, (k + 1) * LANES)
            taps_ref[:, here] = small[k][16:25] * factor
            taps_ref[:, width + k * LANES : width + (k + 1) * LANES] = small[k][32:41] * factor
            for m in range(chunks):
                block = lax.dot_general(
                    small[k][0:8].astype(BF),
                    small[m][8:16].astype(BF),
                    (((0,), (0,)), ((), ())),
                    preferred_element_type=F32,
                )
                att_ref[here, m * LANES : (m + 1) * LANES] = block * factor


def unpack(own, other, me, hidden, width, factor):
    full = jax.ShapeDtypeStruct((width, width), F32)
    return pl.pallas_call(
        functools.partial(unpack_kernel, factor),
        grid=(width // LANES,),
        in_specs=[pl.BlockSpec(memory_space=pltpu.SMEM), whole(own), whole(other)],
        out_specs=[
            pl.BlockSpec((LANES, hidden), lambda s: (s, 0)),
            whole(full),
            whole(full),
            pl.BlockSpec((9, hidden), lambda s: (0, 0)),
        ],
        out_shape=[
            jax.ShapeDtypeStruct((width, hidden), F32),
            full,
            full,
            jax.ShapeDtypeStruct((9, hidden), F32),
        ],
        compiler_params=params(vmem=16 * 1024 * 1024),
        name="unpack",
    )(me.reshape(1), own, other)


def exchange_pairs(first, second):
    count = lax.axis_size(SPACE)
    inner = [(i, i ^ 1) for i in range(count)]
    outer_pairs = [(i, i + 1) for i in range(1, count - 1, 2)]
    crossing = outer_pairs + [(t, s) for s, t in outer_pairs]
    return lax.ppermute(first, SPACE, inner), lax.ppermute(second, SPACE, crossing)


SPACE = ("x", "zh", "y")
CHIPS = ("zl", "x", "zh", "y")
SWAP = [(0, 1), (1, 0)]


def from_space(v):
    n = lax.axis_size(SPACE)
    copies = lax.optimization_barrier(jnp.broadcast_to(v[None], (n,) + v.shape))
    return lax.all_to_all(copies, SPACE, 0, 0, tiled=True)


def sum_over_all(send, keep, later):
    n = lax.axis_size(CHIPS)
    other = lax.ppermute(send, "co", SWAP)
    own = (keep.astype(F32) + other.astype(F32)).astype(BF)
    own = lax.optimization_barrier(own.reshape(n, -1, LANES))
    parts = lax.all_to_all(own, CHIPS, 0, 0, tiled=True)
    part = jnp.sum(parts.astype(F32), 0).astype(BF)
    part, later = lax.optimization_barrier((part, later))
    copies = lax.optimization_barrier(jnp.broadcast_to(part[None], parts.shape))
    own = lax.all_to_all(copies, CHIPS, 0, 0, tiled=True)
    return own.reshape(keep.shape), later


def local(frames, cotangent, gain, w_in, kernel, w_att, w_out):
    x = frames[0]
    cot = cotangent[0]
    rows, cols, width = x.shape
    hidden = w_in.shape[1]
    space = lax.axis_size("x") * lax.axis_size("zh") * lax.axis_size("y")
    place = (lax.axis_index("x") * lax.axis_size("zh") + lax.axis_index("zh")) * lax.axis_size(
        "y"
    ) + lax.axis_index("y")
    frame_count = lax.axis_size("zl") * lax.axis_size("co")
    frame = lax.axis_index("zl") * lax.axis_size("co") + lax.axis_index("co")
    pixels = rows * space * cols
    factor = 1.0 / math.sqrt(frame_count * pixels)
    gain = gain[None]
    order = place_matrix(cols)

    odd = place % 2
    edge_row = lambda r: lax.dynamic_slice_in_dim(x, r, 1, 0)
    first, second = exchange_pairs(
        edge_row((1 - odd) * (rows - 1)), edge_row(odd * (rows - 1))
    )
    normed_t, expanded, cot_t, d_att = enter(x, gain, w_in, order, cot, w_out)
    taps = jnp.broadcast_to(kernel[:, None], (9, STEP, hidden))
    first, second, taps = lax.optimization_barrier((first, second, taps))
    halo_t, halo = enter_halo(odd, first, second, gain, w_in, order)
    conv_a, conv_b, sums = convolution(expanded, halo, taps, d_att)
    sums = from_space(sums)
    out_term = outer(cot_t, conv_a, conv_b)
    sums, out_term = lax.optimization_barrier((sums, out_term))
    first, second, scale, back, vectors = edge_rows(
        jnp.stack([odd, frame, place]), conv_a, conv_b, d_att, sums, w_att, kernel, w_in, pixels
    )
    first, second = exchange_pairs(first, second)
    me = lax.axis_index("co")
    d_exp_a, d_exp_b, send, keep = gradients(
        me, expanded, halo, taps, conv_a, conv_b, d_att, scale, back, out_term, vectors,
        normed_t, halo_t,
    )
    send, first, second = lax.optimization_barrier((send, first, second))
    own, (first, second) = sum_over_all(send, keep, (first, second))
    grad = input_grad(odd, x, cot, d_exp_a, d_exp_b, first, second, gain, w_in, order)
    own, grad = lax.optimization_barrier((own, grad))
    other = lax.ppermute(own, "co", SWAP)
    in_sum, out_sum, att_sum, kernel_sum = unpack(
        own, other, me, hidden, width, factor
    )
    return grad, in_sum, kernel_sum, att_sum, out_sum


def solution(mesh):
    fine = Mesh(mesh.devices.reshape(2, 2, 4, 2, 4), ("zl", "co", "x", "zh", "y"))
    big = P(("zl", "co"), ("x", "zh", "y"), None, None)
    return jax.shard_map(
        local,
        mesh=fine,
        in_specs=(big, big, P(), P(), P(), P(), P()),
        out_specs=(big, P(), P(), P(), P()),
        check_vma=False,
    )
```

```python
import functools
import math

import jax
import jax.numpy as jnp
import numpy as np
from jax import lax
from jax.experimental import pallas as pl
from jax.experimental.pallas import tpu as pltpu
from jax.sharding import Mesh, PartitionSpec as P

EPS = 1e-06
BF = jnp.bfloat16
F32 = jnp.float32
LANES = 128
STEP = 16
SMALL = 48
VMEM = 56 * 1024 * 1024


def params(vmem=VMEM):
    return pltpu.CompilerParams(dimension_semantics=("arbitrary",), vmem_limit_bytes=vmem)


def layer_norm(x):
    xf = x.astype(F32)
    centered = xf - jnp.mean(xf, -1, keepdims=True)
    rstd = lax.rsqrt(jnp.mean(centered * centered, -1, keepdims=True) + EPS)
    return centered * rstd, rstd


def place_matrix(cols):
    place = np.arange(cols)[:, None]
    column = np.arange(cols)[None]
    return jnp.asarray(column == place % STEP * (cols // STEP) + place // STEP, BF)


def reorder(order, rows):
    return jnp.dot(order, rows, preferred_element_type=F32)


def neighbours(tile, first):
    zero = jnp.zeros((1, tile.shape[1]), F32)
    parts = [zero, tile[: STEP - 1]] if first else [tile[1:], zero]
    return jnp.concatenate(parts, 0)


def chunked(v):
    return [v[:, k * LANES : (k + 1) * LANES] for k in range(v.shape[1] // LANES)]


def tiled(v):
    return v.reshape(-1, STEP, LANES)


def flat(v):
    return v.reshape(-1, LANES)


def expand_row(x, gain_ref, w_ref, order, normed_t_ref, expanded_ref, r=0):
    cols = x.shape[0]
    xhat, _ = layer_norm(reorder(order, x))
    normed = (xhat * gain_ref[...]).astype(BF)
    normed_t_ref[:, r * cols : (r + 1) * cols] = normed.T
    for k, e in enumerate(chunked(jnp.dot(normed, w_ref[...], preferred_element_type=F32))):
        expanded_ref[k, r, 1 : 1 + cols // STEP] = tiled(e.astype(BF))
        expanded_ref[k, r, 0] = neighbours(e[cols - STEP :], True).astype(BF)
        expanded_ref[k, r, 1 + cols // STEP] = neighbours(e[:STEP], False).astype(BF)


def halo_kernel(
    odd_ref, first_ref, second_ref, gain_ref, w_ref, order_ref, normed_t_ref, expanded_ref
):
    early = (pl.program_id(0) == 0) == (odd_ref[0] == 1)
    x = jnp.where(early, first_ref[0].astype(F32), second_ref[0].astype(F32))
    expand_row(x.astype(BF), gain_ref, w_ref, order_ref[...], normed_t_ref, expanded_ref)


def enter_kernel(
    x_ref, gain_ref, w_ref, order_ref, cot_ref, wo_ref, normed_t_ref, expanded_ref, cot_t_ref, d_ref
):
    order = order_ref[...]
    placed = reorder(order, cot_ref[0]).astype(BF)
    cot_t_ref[...] = placed.T
    d_att = lax.dot_general(
        placed, wo_ref[...], (((1,), (1,)), ((), ())), preferred_element_type=F32
    )
    for k, d in enumerate(chunked(d_att)):
        d_ref[k, 0] = tiled(d.astype(BF))
    expand_row(x_ref[0], gain_ref, w_ref, order, normed_t_ref, expanded_ref)


def enter_specs(rows, cols, width, hidden):
    groups, tiles = hidden // LANES, cols // STEP
    specs = [
        pl.BlockSpec((width, cols), lambda r: (0, r)),
        pl.BlockSpec((groups, 1, tiles + 2, STEP, LANES), lambda r: (0, r, 0, 0, 0)),
    ]
    shapes = [
        jax.ShapeDtypeStruct((width, rows * cols), BF),
        jax.ShapeDtypeStruct((groups, rows, tiles + 2, STEP, LANES), BF),
    ]
    return specs, shapes


def whole(a):
    return pl.BlockSpec(a.shape, lambda r: (0,) * a.ndim)


def enter(x, gain, w_in, order, cot, w_out):
    rows, cols, width = x.shape
    chunks = width // LANES
    specs, shapes = enter_specs(rows, cols, width, w_in.shape[1])
    row = pl.BlockSpec((1, cols, width), lambda r: (r, 0, 0))
    return pl.pallas_call(
        enter_kernel,
        grid=(rows,),
        in_specs=[row, whole(gain), whole(w_in), whole(order), row, whole(w_out)],
        out_specs=specs
        + [specs[0], pl.BlockSpec((chunks, 1, cols // STEP, STEP, LANES), lambda r: (0, r, 0, 0, 0))],
        out_shape=shapes
        + [shapes[0], jax.ShapeDtypeStruct((chunks, rows, cols // STEP, STEP, LANES), BF)],
        compiler_params=params(),
        cost_estimate=pl.CostEstimate(
            flops=2 * rows * cols * width * width * 8,
            bytes_accessed=rows * cols * width * 12,
            transcendentals=0,
        ),
        name="enter",
    )(x, gain, w_in, order, cot, w_out)


def enter_halo(odd, first, second, gain, w_in, order):
    _, cols, width = first.shape
    specs, shapes = enter_specs(2, cols, width, w_in.shape[1])
    row = pl.BlockSpec((1, cols, width), lambda r: (0, 0, 0))
    return pl.pallas_call(
        halo_kernel,
        grid=(2,),
        in_specs=[pl.BlockSpec(memory_space=pltpu.SMEM), row, row]
        + [whole(a) for a in (gain, w_in, order)],
        out_specs=specs,
        out_shape=shapes,
        compiler_params=params(),
        name="enter_halo",
    )(odd.reshape(1), first, second, gain, w_in, order)


def row_tile(own_ref, halo_ref, r, t):
    rows = own_ref.shape[1]
    if r == 0:
        return halo_ref[0, 0, t]
    if r == rows + 1:
        return halo_ref[0, 1, t]
    return own_ref[0, r - 1, t]


def halves(v):
    return v[: STEP // 2] + v[STEP // 2 :]


def spread_taps(taps_ref):
    return [taps_ref[n].astype(F32) for n in range(9)]


def added(total, term):
    return term if total is None else total + term


def conv_kernel(
    ea_ref, eb_ref, ha_ref, hb_ref, ka_ref, kb_ref, d_ref, ca_ref, cb_ref, sum_ref
):
    _, rows, tiles, _, _ = d_ref.shape
    taps_a, taps_b = spread_taps(ka_ref), spread_taps(kb_ref)

    def convolve(own_ref, halo_ref, taps, t):
        total = [None] * rows
        for r in range(rows + 2):
            for j in range(3):
                v = row_tile(own_ref, halo_ref, r, t + j).astype(F32)
                for i in range(3):
                    if 0 <= r - i < rows:
                        total[r - i] = added(total[r - i], v * taps[3 * i + j])
        return total

    def body(t, sums):
        a = convolve(ea_ref, ha_ref, taps_a, t)
        b = convolve(eb_ref, hb_ref, taps_b, t)
        total = [None, None]
        for r in range(rows):
            here = (0, r, t)
            ca_ref[here] = a[r].astype(BF)
            cb_ref[here] = b[r].astype(BF)
            g = a[r] * b[r]
            total[0] = added(total[0], g)
            total[1] = added(total[1], g * d_ref[here].astype(F32))
        return sums[0] + halves(total[0]), sums[1] + halves(total[1])

    zero = jnp.zeros((STEP // 2, LANES), F32)
    pooled, weighted = lax.fori_loop(0, tiles, body, (zero, zero), unroll=4)
    chunk, chunks = pl.program_id(0), pl.num_programs(0)
    sum_ref[pl.ds(chunk, 1), :] = jnp.sum(pooled, 0, keepdims=True)
    sum_ref[pl.ds(chunks + chunk, 1), :] = jnp.sum(weighted, 0, keepdims=True)


def chunk_spec(shape, offset=0):
    block = (1,) + tuple(shape[1:])
    return pl.BlockSpec(block, lambda k: (k + offset,) + (0,) * (len(shape) - 1))


def half_specs(a):
    return [chunk_spec(a.shape), chunk_spec(a.shape, a.shape[0] // 2)]


def tap_specs(taps, chunks):
    block = taps.shape[:2] + (LANES,)
    return [
        pl.BlockSpec(block, lambda k: (0, 0, k)),
        pl.BlockSpec(block, lambda k: (0, 0, k + chunks)),
    ]


def convolution(expanded, halo, taps, d_att):
    chunks = d_att.shape[0]
    part = chunk_spec(d_att.shape)
    shape = jax.ShapeDtypeStruct(d_att.shape, BF)
    return pl.pallas_call(
        conv_kernel,
        grid=(chunks,),
        in_specs=half_specs(expanded) + half_specs(halo) + tap_specs(taps, chunks) + [part],
        out_specs=[part, part, pl.BlockSpec((2 * chunks, LANES), lambda k: (0, 0))],
        out_shape=[shape, shape, jax.ShapeDtypeStruct((2 * chunks, LANES), F32)],
        compiler_params=params(),
        cost_estimate=pl.CostEstimate(
            flops=d_att.size * 400, bytes_accessed=d_att.size * 14, transcendentals=0
        ),
        name="convolution",
    )(expanded, expanded, halo, halo, taps, taps, d_att)


def outer_kernel(cot_t_ref, ca_ref, cb_ref, out_ref):
    cols = ca_ref.shape[2] * STEP
    total = None
    for r in range(ca_ref.shape[1]):
        left = cot_t_ref[:, r * cols : (r + 1) * cols]
        gated = flat((ca_ref[0, r].astype(F32) * cb_ref[0, r].astype(F32)).astype(BF))
        total = added(total, jnp.dot(left, gated, preferred_element_type=F32))
    out_ref[0] = total


def outer(cot_t, conv_a, conv_b):
    chunks = conv_a.shape[0]
    shape = (chunks, cot_t.shape[0], LANES)
    return pl.pallas_call(
        outer_kernel,
        grid=(chunks,),
        in_specs=[whole(cot_t), chunk_spec(conv_a.shape), chunk_spec(conv_b.shape)],
        out_specs=chunk_spec(shape),
        out_shape=jax.ShapeDtypeStruct(shape, F32),
        compiler_params=params(),
        cost_estimate=pl.CostEstimate(
            flops=2 * cot_t.shape[0] * conv_a.size * 2,
            bytes_accessed=conv_a.size * 4,
            transcendentals=0,
        ),
        name="outer",
    )(cot_t, conv_a, conv_b)


def gradient_kernel(
    me_ref, ea_ref, eb_ref, ha_ref, hb_ref, ka_ref, kb_ref, ca_ref, cb_ref, d_ref, scale_ref, back_ref,
    out_ref, vec_ref, nt_ref, nh_ref, xa_ref, xb_ref, send_ref, keep_ref, da, db, nt, nh, sems,
):
    _, rows, tiles, _, _ = d_ref.shape
    cols = tiles * STEP
    scale = jnp.broadcast_to(scale_ref[...], (STEP, LANES))
    back = jnp.broadcast_to(back_ref[...], (STEP, LANES))
    copies = [
        pltpu.make_async_copy(nt_ref, nt, sems.at[0]),
        pltpu.make_async_copy(nh_ref, nh, sems.at[1]),
    ]

    @pl.when(pl.program_id(0) == 0)
    def _():
        for copy in copies:
            copy.start()

    def products(own_ref, halo_ref, own, t, sums):
        part = [None] * 9
        for r in range(rows + 2):
            for j in range(3):
                v = row_tile(own_ref, halo_ref, r, t + j).astype(F32)
                for i in range(3):
                    if 0 <= r - i < rows:
                        part[3 * i + j] = added(part[3 * i + j], v * own[r - i])
        return tuple(s + halves(p) for s, p in zip(sums, part))

    def first(own_ref, halo_ref, other_ref, d, t, sums):
        own = []
        for r in range(rows):
            dg = d_ref[0, r, t].astype(F32) * scale + back
            own.append(dg * other_ref[0, r, t].astype(F32))
            d[r, t + 1] = own[r].astype(BF)
        return products(own_ref, halo_ref, own, t, sums)

    nought = (jnp.zeros((STEP // 2, LANES), F32),) * 9
    sums = [
        lax.fori_loop(0, tiles, functools.partial(first, *refs), nought, unroll=4)
        for refs in ((ea_ref, ha_ref, cb_ref, da), (eb_ref, hb_ref, ca_ref, db))
    ]
    for d in (da, db):
        for r in range(rows):
            d[r, 0] = neighbours(d[r, tiles].astype(F32), True).astype(BF)
            d[r, tiles + 1] = neighbours(d[r, 1].astype(F32), False).astype(BF)

    taps_a, taps_b = spread_taps(ka_ref), spread_taps(kb_ref)

    def spread(d, taps, x_ref, t):
        total = [None] * (rows + 2)
        for r in range(rows):
            for j in range(3):
                v = d[r, t + 2 - j].astype(F32)
                for i in range(3):
                    total[r + i] = added(total[r + i], v * taps[3 * i + j])
        for r in range(rows + 2):
            x_ref[0, r, t] = total[r].astype(BF)

    for d, taps, x_ref in ((da, taps_a, xa_ref), (db, taps_b, xb_ref)):

        def second(t, carry, d=d, taps=taps, x_ref=x_ref):
            spread(d, taps, x_ref, t)
            return carry

        lax.fori_loop(0, tiles, second, 0, unroll=4)

    @pl.when(pl.program_id(0) == 0)
    def _():
        for copy in copies:
            copy.wait()

    total = None
    for r in range(rows + 2):
        if r == 0:
            left = nh[:, 0:cols]
        elif r == rows + 1:
            left = nh[:, cols : 2 * cols]
        else:
            left = nt[:, (r - 1) * cols : r * cols]
        right = jnp.concatenate([flat(xa_ref[0, r]), flat(xb_ref[0, r])], -1)
        total = added(total, jnp.dot(left, right, preferred_element_type=F32))
    width = total.shape[0]
    blank = jnp.zeros((7, LANES), F32)
    rows_of = lambda part: [jnp.sum(p, 0, keepdims=True) for p in part]
    small = jnp.concatenate([vec_ref[0], *rows_of(sums[0]), blank, *rows_of(sums[1]), blank], 0)

    def write(ref):
        ref[0, 0:width] = total[:, :LANES].astype(BF)
        ref[0, width : 2 * width] = total[:, LANES:].astype(BF)
        ref[0, 2 * width : 3 * width] = (out_ref[0] * scale_ref[...]).astype(BF)
        ref[0, 3 * width : 3 * width + SMALL] = small.astype(BF)
        ref[0, 3 * width + SMALL :] = jnp.zeros((width // 2 - SMALL, LANES), BF)

    early = pl.program_id(0) < pl.num_programs(0) // 2
    pl.when(early)(lambda: write(send_ref))
    pl.when(jnp.logical_not(early))(lambda: write(keep_ref))


def gradients(
    me, expanded, halo, taps, conv_a, conv_b, d_att, scale, back, out_term, vectors, normed_t, halo_t
):
    chunks, rows, tiles, _, _ = d_att.shape
    width = chunks * LANES
    half = chunks // 2
    chunk = lambda s, me: (s + half * (1 - me[0])) % chunks

    def by_chunk(a, offset=0):
        block = (1,) + tuple(a.shape[1:])
        return pl.BlockSpec(block, lambda s, me: (chunk(s, me) + offset,) + (0,) * (len(block) - 1))

    def by_half(a):
        return [by_chunk(a), by_chunk(a, chunks)]

    def lanes(a, offset=0):
        block = a.shape[:-1] + (LANES,)
        return pl.BlockSpec(
            block, lambda s, me: (0,) * (len(block) - 1) + (chunk(s, me) + offset,)
        )

    spread = jax.ShapeDtypeStruct((chunks, rows + 2, tiles, STEP, LANES), BF)
    part = jax.ShapeDtypeStruct((half, 7 * width // 2, LANES), BF)
    block = (1,) + part.shape[1:]
    return pl.pallas_call(
        gradient_kernel,
        grid_spec=pltpu.PrefetchScalarGridSpec(
            num_scalar_prefetch=1,
            grid=(chunks,),
            in_specs=by_half(expanded)
            + by_half(halo)
            + [lanes(taps), lanes(taps, chunks)]
            + [by_chunk(a) for a in (conv_a, conv_b, d_att)]
            + [lanes(scale), lanes(back), by_chunk(out_term), by_chunk(vectors)]
            + [pl.BlockSpec(memory_space=pl.ANY)] * 2,
            out_specs=[
                by_chunk(spread),
                by_chunk(spread),
                pl.BlockSpec(block, lambda s, me: (jnp.minimum(s, half - 1), 0, 0)),
                pl.BlockSpec(block, lambda s, me: (jnp.maximum(s - half, 0), 0, 0)),
            ],
            scratch_shapes=[pltpu.VMEM((rows, tiles + 2, STEP, LANES), BF)] * 2
            + [pltpu.VMEM(normed_t.shape, BF), pltpu.VMEM(halo_t.shape, BF)]
            + [pltpu.SemaphoreType.DMA((2,))],
        ),
        out_shape=[spread, spread, part, part],
        compiler_params=params(),
        cost_estimate=pl.CostEstimate(
            flops=d_att.size * 3000, bytes_accessed=d_att.size * 20, transcendentals=0
        ),
        name="gradients",
    )(
        me.reshape(1), expanded, expanded, halo, halo, taps, taps, conv_a, conv_b, d_att, scale, back,
        out_term, vectors, normed_t, halo_t,
    )


def back_project(xa_ref, xb_ref, w_ref):
    chunks = [flat(ref[k, 0]) for ref in (xa_ref, xb_ref) for k in range(ref.shape[0])]
    return lax.dot_general(
        jnp.concatenate(chunks, -1),
        w_ref[...],
        (((1,), (1,)), ((), ())),
        preferred_element_type=F32,
    )


def edge_kernel(
    pixels, at_ref, ca_ref, cb_ref, d_ref, sums_ref, att_ref, taps_ref, w_ref,
    first_ref, second_ref, scale_ref, back_ref, vec_ref,
):
    side = (pl.program_id(0) + 1 - at_ref[0]) % 2

    @pl.when(pl.program_id(0) == 0)
    def _():
        sums = jnp.sum(sums_ref[...], 0)
        half = sums.shape[0] // 2
        line = lambda rows: jnp.concatenate([rows[k : k + 1] for k in range(half)], -1)
        eight = lambda row: jnp.broadcast_to(row, (8, row.shape[1]))
        exact = dict(precision=lax.Precision.HIGHEST, preferred_element_type=F32)
        pooled = sums[:half] / pixels
        scale_ref[...] = jnp.dot(eight(line(pooled)), att_ref[...], **exact)[:1]
        back = lax.dot_general(
            eight(line(sums[half:])), att_ref[...], (((1,), (1,)), ((), ())), **exact
        )
        back_ref[...] = back[:1] / pixels
        row = lax.broadcasted_iota(jnp.int32, (8, LANES), 0)
        mine = row == jnp.where(at_ref[2] == 0, at_ref[1], 8)
        for k in range(half):
            for n, v in enumerate((pooled[k : k + 1], sums[half + k : half + k + 1])):
                rows = jnp.where(mine, jnp.broadcast_to(v, (8, LANES)), 0.0)
                vec_ref[k, 8 * n : 8 * n + 8] = rows

    scale, back = scale_ref[...], back_ref[...]
    every = taps_ref[...].astype(F32)
    taps = jnp.where(side == 0, every[0:3], every[6:9])
    chunks = d_ref.shape[0]
    spread = [None] * (2 * chunks)
    for k in range(chunks):
        here = slice(k * LANES, (k + 1) * LANES)
        dg = d_ref[k, 0].astype(F32) * scale[:, here] + back[:, here]
        for n, ref in ((k, cb_ref), (chunks + k, ca_ref)):
            d = dg * ref[k, 0].astype(F32)
            before = neighbours(d[-1], True)[None]
            behind = neighbours(d[0], False)[None]
            windows = (
                jnp.concatenate([d[1:], behind], 0),
                d,
                jnp.concatenate([before, d[:-1]], 0),
            )
            total = None
            for j in range(3):
                tap = taps[j : j + 1, n * LANES : (n + 1) * LANES]
                total = added(total, windows[j] * tap[None])
            spread[n] = flat(total.astype(BF))
    row = lax.dot_general(
        jnp.concatenate(spread, -1),
        w_ref[...],
        (((1,), (1,)), ((), ())),
        preferred_element_type=F32,
    ).astype(BF)

    @pl.when(pl.program_id(0) == 0)
    def _():
        first_ref[...] = row

    @pl.when(pl.program_id(0) == 1)
    def _():
        second_ref[...] = row


def edge_rows(at, conv_a, conv_b, d_att, sums, w_att, taps, w_in, pixels):
    chunks, rows, tiles, _, _ = d_att.shape
    side = lambda e, at: (e + 1 - at[0]) % 2
    spec = pl.BlockSpec(
        (chunks, 1, tiles, STEP, LANES), lambda e, at: (0, side(e, at) * (rows - 1), 0, 0, 0)
    )
    out = jax.ShapeDtypeStruct((tiles * STEP, w_in.shape[0]), BF)
    line = jax.ShapeDtypeStruct((1, chunks * LANES), F32)
    outs = [out, out, line, line, jax.ShapeDtypeStruct((chunks, 16, LANES), F32)]
    full = lambda a: pl.BlockSpec(a.shape, lambda e, at: (0,) * a.ndim)
    return pl.pallas_call(
        functools.partial(edge_kernel, pixels),
        grid_spec=pltpu.PrefetchScalarGridSpec(
            num_scalar_prefetch=1,
            grid=(2,),
            in_specs=[spec, spec, spec] + [full(a) for a in (sums, w_att, taps, w_in)],
            out_specs=[full(a) for a in outs],
        ),
        out_shape=outs,
        compiler_params=params(),
        name="edge_rows",
    )(at, conv_a, conv_b, d_att, sums, w_att, taps, w_in)


def input_kernel(
    odd_ref, x_ref, cot_ref, xa_ref, xb_ref, first_ref, second_ref, gain_ref, w_ref, order_ref, out_ref
):
    row = pl.program_id(0)
    last = pl.num_programs(0) - 1
    d_norm = back_project(xa_ref, xb_ref, w_ref)
    odd = odd_ref[0] == 1
    above, below = row == 0, row == last
    early = (above & odd) | (below & jnp.logical_not(odd))
    late = (above & jnp.logical_not(odd)) | (below & odd)
    d_norm = d_norm + jnp.where(early, 1.0, 0.0) * first_ref[...].astype(F32)
    d_norm = d_norm + jnp.where(late, 1.0, 0.0) * second_ref[...].astype(F32)
    d_norm = lax.dot_general(
        order_ref[...], d_norm.astype(BF), (((0,), (0,)), ((), ())), preferred_element_type=F32
    )
    xhat, rstd = layer_norm(x_ref[0])
    dxhat = d_norm * gain_ref[...]
    grad = cot_ref[0].astype(F32) + rstd * (
        dxhat - jnp.mean(dxhat, -1, keepdims=True) - xhat * jnp.mean(dxhat * xhat, -1, keepdims=True)
    )
    out_ref[0, 0] = grad.astype(BF)


def input_grad(odd, x, cot, xa, xb, first, second, gain, w_in, order):
    rows, cols, width = x.shape
    chunks = xa.shape[0]
    spec = pl.BlockSpec((1, cols, width), lambda r: (r, 0, 0))
    inner = pl.BlockSpec(
        (chunks, 1, cols // STEP, STEP, LANES), lambda r: (0, r + 1, 0, 0, 0)
    )
    return pl.pallas_call(
        input_kernel,
        grid=(rows,),
        in_specs=[pl.BlockSpec(memory_space=pltpu.SMEM), spec, spec, inner, inner]
        + [whole(a) for a in (first, second, gain, w_in, order)],
        out_specs=pl.BlockSpec((1, 1, cols, width), lambda r: (0, r, 0, 0)),
        out_shape=jax.ShapeDtypeStruct((1, rows, cols, width), BF),
        compiler_params=params(),
        cost_estimate=pl.CostEstimate(
            flops=2 * rows * cols * width * width * 6,
            bytes_accessed=rows * cols * width * 10,
            transcendentals=0,
        ),
        name="input_grad",
    )(odd.reshape(1), x, cot, xa, xb, first, second, gain, w_in, order)


def unpack_kernel(factor, me_ref, own_ref, other_ref, in_ref, out_ref, att_ref, taps_ref):
    step = pl.program_id(0)
    first = me_ref[0] == 0
    half = own_ref.shape[0]
    chunks = 2 * half
    width = chunks * LANES

    def rows(k, start, count):
        own = own_ref[k % half, pl.ds(start, count)].astype(F32)
        other = other_ref[k % half, pl.ds(start, count)].astype(F32)
        return jnp.where(first, own, other) if k < half else jnp.where(first, other, own)

    start = pl.multiple_of(step * LANES, LANES)
    for k in range(chunks):
        here = slice(k * LANES, (k + 1) * LANES)
        in_ref[:, here] = rows(k, start, LANES) * factor
        in_ref[:, width + k * LANES : width + (k + 1) * LANES] = (
            rows(k, start + width, LANES) * factor
        )
        out_ref[here, pl.ds(start, LANES)] = rows(k, start + 2 * width, LANES).T * factor

    @pl.when(step == 0)
    def _():
        small = [rows(k, 3 * width, SMALL) for k in range(chunks)]
        for k in range(chunks):
            here = slice(k * LANES, (k + 1) * LANES)
            taps_ref[:, here] = small[k][16:25] * factor
            taps_ref[:, width + k * LANES : width + (k + 1) * LANES] = small[k][32:41] * factor
            for m in range(chunks):
                block = lax.dot_general(
                    small[k][0:8].astype(BF),
                    small[m][8:16].astype(BF),
                    (((0,), (0,)), ((), ())),
                    preferred_element_type=F32,
                )
                att_ref[here, m * LANES : (m + 1) * LANES] = block * factor


def unpack(own, other, me, hidden, width, factor):
    full = jax.ShapeDtypeStruct((width, width), F32)
    return pl.pallas_call(
        functools.partial(unpack_kernel, factor),
        grid=(width // LANES,),
        in_specs=[pl.BlockSpec(memory_space=pltpu.SMEM), whole(own), whole(other)],
        out_specs=[
            pl.BlockSpec((LANES, hidden), lambda s: (s, 0)),
            whole(full),
            whole(full),
            pl.BlockSpec((9, hidden), lambda s: (0, 0)),
        ],
        out_shape=[
            jax.ShapeDtypeStruct((width, hidden), F32),
            full,
            full,
            jax.ShapeDtypeStruct((9, hidden), F32),
        ],
        compiler_params=params(vmem=16 * 1024 * 1024),
        name="unpack",
    )(me.reshape(1), own, other)


def exchange_pairs(first, second):
    count = lax.axis_size(SPACE)
    inner = [(i, i ^ 1) for i in range(count)]
    outer_pairs = [(i, i + 1) for i in range(1, count - 1, 2)]
    crossing = outer_pairs + [(t, s) for s, t in outer_pairs]
    return lax.ppermute(first, SPACE, inner), lax.ppermute(second, SPACE, crossing)


SPACE = ("x", "zh", "y")
CHIPS = ("zl", "x", "zh", "y")
SWAP = [(0, 1), (1, 0)]


def from_space(v):
    n = lax.axis_size(SPACE)
    copies = lax.optimization_barrier(jnp.broadcast_to(v[None], (n,) + v.shape))
    return lax.all_to_all(copies, SPACE, 0, 0, tiled=True)


def sum_over_all(send, keep, later):
    n = lax.axis_size(CHIPS)
    other = lax.ppermute(send, "co", SWAP)
    own = (keep.astype(F32) + other.astype(F32)).astype(BF)
    own = lax.optimization_barrier(own.reshape(n, -1, LANES))
    parts = lax.all_to_all(own, CHIPS, 0, 0, tiled=True)
    part = jnp.sum(parts.astype(F32), 0).astype(BF)
    part, later = lax.optimization_barrier((part, later))
    copies = lax.optimization_barrier(jnp.broadcast_to(part[None], parts.shape))
    own = lax.all_to_all(copies, CHIPS, 0, 0, tiled=True)
    return own.reshape(keep.shape), later


def local(frames, cotangent, gain, w_in, kernel, w_att, w_out):
    x = frames[0]
    cot = cotangent[0]
    rows, cols, width = x.shape
    hidden = w_in.shape[1]
    space = lax.axis_size("x") * lax.axis_size("zh") * lax.axis_size("y")
    place = (lax.axis_index("x") * lax.axis_size("zh") + lax.axis_index("zh")) * lax.axis_size(
        "y"
    ) + lax.axis_index("y")
    frame_count = lax.axis_size("zl") * lax.axis_size("co")
    frame = lax.axis_index("zl") * lax.axis_size("co") + lax.axis_index("co")
    pixels = rows * space * cols
    factor = 1.0 / math.sqrt(frame_count * pixels)
    gain = gain[None]
    order = place_matrix(cols)

    odd = place % 2
    edge_row = lambda r: lax.dynamic_slice_in_dim(x, r, 1, 0)
    first, second = exchange_pairs(
        edge_row((1 - odd) * (rows - 1)), edge_row(odd * (rows - 1))
    )
    taps = jnp.broadcast_to(kernel[:, None], (9, STEP, hidden))
    gain, taps = lax.optimization_barrier((gain, taps))
    normed_t, expanded, cot_t, d_att = enter(x, gain, w_in, order, cot, w_out)
    halo_t, halo = enter_halo(odd, first, second, gain, w_in, order)
    conv_a, conv_b, sums = convolution(expanded, halo, taps, d_att)
    sums = from_space(sums)
    out_term = outer(cot_t, conv_a, conv_b)
    sums, out_term = lax.optimization_barrier((sums, out_term))
    first, second, scale, back, vectors = edge_rows(
        jnp.stack([odd, frame, place]), conv_a, conv_b, d_att, sums, w_att, kernel, w_in, pixels
    )
    first, second = exchange_pairs(first, second)
    me = lax.axis_index("co")
    d_exp_a, d_exp_b, send, keep = gradients(
        me, expanded, halo, taps, conv_a, conv_b, d_att, scale, back, out_term, vectors,
        normed_t, halo_t,
    )
    send, first, second = lax.optimization_barrier((send, first, second))
    own, (first, second) = sum_over_all(send, keep, (first, second))
    grad = input_grad(odd, x, cot, d_exp_a, d_exp_b, first, second, gain, w_in, order)
    own, grad = lax.optimization_barrier((own, grad))
    other = lax.ppermute(own, "co", SWAP)
    in_sum, out_sum, att_sum, kernel_sum = unpack(
        own, other, me, hidden, width, factor
    )
    return grad, in_sum, kernel_sum, att_sum, out_sum


def solution(mesh):
    fine = Mesh(mesh.devices.reshape(2, 2, 4, 2, 4), ("zl", "co", "x", "zh", "y"))
    big = P(("zl", "co"), ("x", "zh", "y"), None, None)
    return jax.shard_map(
        local,
        mesh=fine,
        in_specs=(big, big, P(), P(), P(), P(), P()),
        out_specs=(big, P(), P(), P(), P()),
        check_vma=False,
    )
```

```python
import functools
import math

import jax
import jax.numpy as jnp
import numpy as np
from jax import lax
from jax.experimental import pallas as pl
from jax.experimental.pallas import tpu as pltpu
from jax.sharding import Mesh, PartitionSpec as P

EPS = 1e-06
BF = jnp.bfloat16
F32 = jnp.float32
LANES = 128
STEP = 16
SMALL = 48
VMEM = 56 * 1024 * 1024


def params(vmem=VMEM):
    return pltpu.CompilerParams(dimension_semantics=("arbitrary",), vmem_limit_bytes=vmem)


def layer_norm(x):
    xf = x.astype(F32)
    centered = xf - jnp.mean(xf, -1, keepdims=True)
    rstd = lax.rsqrt(jnp.mean(centered * centered, -1, keepdims=True) + EPS)
    return centered * rstd, rstd


def place_matrix(cols):
    place = np.arange(cols)[:, None]
    column = np.arange(cols)[None]
    return jnp.asarray(column == place % STEP * (cols // STEP) + place // STEP, BF)


def reorder(order, rows):
    return jnp.dot(order, rows, preferred_element_type=F32)


def neighbours(tile, first):
    zero = jnp.zeros((1, tile.shape[1]), F32)
    parts = [zero, tile[: STEP - 1]] if first else [tile[1:], zero]
    return jnp.concatenate(parts, 0)


def chunked(v):
    return [v[:, k * LANES : (k + 1) * LANES] for k in range(v.shape[1] // LANES)]


def tiled(v):
    return v.reshape(-1, STEP, LANES)


def flat(v):
    return v.reshape(-1, LANES)


def expand_row(x, gain_ref, w_ref, order, normed_t_ref, expanded_ref, r=0):
    cols = x.shape[0]
    xhat, _ = layer_norm(reorder(order, x))
    normed = (xhat * gain_ref[...]).astype(BF)
    normed_t_ref[:, r * cols : (r + 1) * cols] = normed.T
    for k, e in enumerate(chunked(jnp.dot(normed, w_ref[...], preferred_element_type=F32))):
        expanded_ref[k, r, 1 : 1 + cols // STEP] = tiled(e.astype(BF))
        expanded_ref[k, r, 0] = neighbours(e[cols - STEP :], True).astype(BF)
        expanded_ref[k, r, 1 + cols // STEP] = neighbours(e[:STEP], False).astype(BF)


def halo_kernel(
    odd_ref, first_ref, second_ref, gain_ref, w_ref, order_ref, normed_t_ref, expanded_ref
):
    early = (pl.program_id(0) == 0) == (odd_ref[0] == 1)
    x = jnp.where(early, first_ref[0].astype(F32), second_ref[0].astype(F32))
    expand_row(x.astype(BF), gain_ref, w_ref, order_ref[...], normed_t_ref, expanded_ref)


def enter_kernel(
    x_ref, gain_ref, w_ref, order_ref, cot_ref, wo_ref, normed_t_ref, expanded_ref, cot_t_ref, d_ref
):
    order = order_ref[...]
    placed = reorder(order, cot_ref[0]).astype(BF)
    cot_t_ref[...] = placed.T
    d_att = lax.dot_general(
        placed, wo_ref[...], (((1,), (1,)), ((), ())), preferred_element_type=F32
    )
    for k, d in enumerate(chunked(d_att)):
        d_ref[k, 0] = tiled(d.astype(BF))
    expand_row(x_ref[0], gain_ref, w_ref, order, normed_t_ref, expanded_ref)


def enter_specs(rows, cols, width, hidden):
    groups, tiles = hidden // LANES, cols // STEP
    specs = [
        pl.BlockSpec((width, cols), lambda r: (0, r)),
        pl.BlockSpec((groups, 1, tiles + 2, STEP, LANES), lambda r: (0, r, 0, 0, 0)),
    ]
    shapes = [
        jax.ShapeDtypeStruct((width, rows * cols), BF),
        jax.ShapeDtypeStruct((groups, rows, tiles + 2, STEP, LANES), BF),
    ]
    return specs, shapes


def whole(a):
    return pl.BlockSpec(a.shape, lambda r: (0,) * a.ndim)


def enter(x, gain, w_in, order, cot, w_out):
    rows, cols, width = x.shape
    chunks = width // LANES
    specs, shapes = enter_specs(rows, cols, width, w_in.shape[1])
    row = pl.BlockSpec((1, cols, width), lambda r: (r, 0, 0))
    return pl.pallas_call(
        enter_kernel,
        grid=(rows,),
        in_specs=[row, whole(gain), whole(w_in), whole(order), row, whole(w_out)],
        out_specs=specs
        + [specs[0], pl.BlockSpec((chunks, 1, cols // STEP, STEP, LANES), lambda r: (0, r, 0, 0, 0))],
        out_shape=shapes
        + [shapes[0], jax.ShapeDtypeStruct((chunks, rows, cols // STEP, STEP, LANES), BF)],
        compiler_params=params(),
        cost_estimate=pl.CostEstimate(
            flops=2 * rows * cols * width * width * 8,
            bytes_accessed=rows * cols * width * 12,
            transcendentals=0,
        ),
        name="enter",
    )(x, gain, w_in, order, cot, w_out)


def enter_halo(odd, first, second, gain, w_in, order):
    _, cols, width = first.shape
    specs, shapes = enter_specs(2, cols, width, w_in.shape[1])
    row = pl.BlockSpec((1, cols, width), lambda r: (0, 0, 0))
    return pl.pallas_call(
        halo_kernel,
        grid=(2,),
        in_specs=[pl.BlockSpec(memory_space=pltpu.SMEM), row, row]
        + [whole(a) for a in (gain, w_in, order)],
        out_specs=specs,
        out_shape=shapes,
        compiler_params=params(vmem=24 * 1024 * 1024),
        name="enter_halo",
    )(odd.reshape(1), first, second, gain, w_in, order)


def row_tile(own_ref, halo_ref, r, t):
    rows = own_ref.shape[1]
    if r == 0:
        return halo_ref[0, 0, t]
    if r == rows + 1:
        return halo_ref[0, 1, t]
    return own_ref[0, r - 1, t]


def halves(v):
    return v[: STEP // 2] + v[STEP // 2 :]


def spread_taps(taps_ref):
    return [taps_ref[n].astype(F32) for n in range(9)]


def added(total, term):
    return term if total is None else total + term


def conv_kernel(
    ea_ref, eb_ref, ha_ref, hb_ref, ka_ref, kb_ref, d_ref, ca_ref, cb_ref, sum_ref
):
    _, rows, tiles, _, _ = d_ref.shape
    taps_a, taps_b = spread_taps(ka_ref), spread_taps(kb_ref)

    def convolve(own_ref, halo_ref, taps, t):
        total = [None] * rows
        for r in range(rows + 2):
            for j in range(3):
                v = row_tile(own_ref, halo_ref, r, t + j).astype(F32)
                for i in range(3):
                    if 0 <= r - i < rows:
                        total[r - i] = added(total[r - i], v * taps[3 * i + j])
        return total

    def body(t, sums):
        a = convolve(ea_ref, ha_ref, taps_a, t)
        b = convolve(eb_ref, hb_ref, taps_b, t)
        total = [None, None]
        for r in range(rows):
            here = (0, r, t)
            ca_ref[here] = a[r].astype(BF)
            cb_ref[here] = b[r].astype(BF)
            g = a[r] * b[r]
            total[0] = added(total[0], g)
            total[1] = added(total[1], g * d_ref[here].astype(F32))
        return sums[0] + halves(total[0]), sums[1] + halves(total[1])

    zero = jnp.zeros((STEP // 2, LANES), F32)
    pooled, weighted = lax.fori_loop(0, tiles, body, (zero, zero), unroll=4)
    chunk, chunks = pl.program_id(0), pl.num_programs(0)
    sum_ref[pl.ds(chunk, 1), :] = jnp.sum(pooled, 0, keepdims=True)
    sum_ref[pl.ds(chunks + chunk, 1), :] = jnp.sum(weighted, 0, keepdims=True)


def chunk_spec(shape, offset=0):
    block = (1,) + tuple(shape[1:])
    return pl.BlockSpec(block, lambda k: (k + offset,) + (0,) * (len(shape) - 1))


def half_specs(a):
    return [chunk_spec(a.shape), chunk_spec(a.shape, a.shape[0] // 2)]


def tap_specs(taps, chunks):
    block = taps.shape[:2] + (LANES,)
    return [
        pl.BlockSpec(block, lambda k: (0, 0, k)),
        pl.BlockSpec(block, lambda k: (0, 0, k + chunks)),
    ]


def convolution(expanded, halo, taps, d_att):
    chunks = d_att.shape[0]
    part = chunk_spec(d_att.shape)
    shape = jax.ShapeDtypeStruct(d_att.shape, BF)
    return pl.pallas_call(
        conv_kernel,
        grid=(chunks,),
        in_specs=half_specs(expanded) + half_specs(halo) + tap_specs(taps, chunks) + [part],
        out_specs=[part, part, pl.BlockSpec((2 * chunks, LANES), lambda k: (0, 0))],
        out_shape=[shape, shape, jax.ShapeDtypeStruct((2 * chunks, LANES), F32)],
        compiler_params=params(),
        cost_estimate=pl.CostEstimate(
            flops=d_att.size * 400, bytes_accessed=d_att.size * 14, transcendentals=0
        ),
        name="convolution",
    )(expanded, expanded, halo, halo, taps, taps, d_att)


def outer_kernel(cot_t_ref, ca_ref, cb_ref, out_ref):
    cols = ca_ref.shape[2] * STEP
    total = None
    for r in range(ca_ref.shape[1]):
        left = cot_t_ref[:, r * cols : (r + 1) * cols]
        gated = flat((ca_ref[0, r].astype(F32) * cb_ref[0, r].astype(F32)).astype(BF))
        total = added(total, jnp.dot(left, gated, preferred_element_type=F32))
    out_ref[0] = total


def outer(cot_t, conv_a, conv_b):
    chunks = conv_a.shape[0]
    shape = (chunks, cot_t.shape[0], LANES)
    return pl.pallas_call(
        outer_kernel,
        grid=(chunks,),
        in_specs=[whole(cot_t), chunk_spec(conv_a.shape), chunk_spec(conv_b.shape)],
        out_specs=chunk_spec(shape),
        out_shape=jax.ShapeDtypeStruct(shape, F32),
        compiler_params=params(),
        cost_estimate=pl.CostEstimate(
            flops=2 * cot_t.shape[0] * conv_a.size * 2,
            bytes_accessed=conv_a.size * 4,
            transcendentals=0,
        ),
        name="outer",
    )(cot_t, conv_a, conv_b)


def gradient_kernel(
    me_ref, ea_ref, eb_ref, ha_ref, hb_ref, ka_ref, kb_ref, ca_ref, cb_ref, d_ref, scale_ref, back_ref,
    out_ref, vec_ref, nt_ref, nh_ref, xa_ref, xb_ref, send_ref, keep_ref, da, db, nt, nh, sems,
):
    _, rows, tiles, _, _ = d_ref.shape
    cols = tiles * STEP
    scale = jnp.broadcast_to(scale_ref[...], (STEP, LANES))
    back = jnp.broadcast_to(back_ref[...], (STEP, LANES))
    copies = [
        pltpu.make_async_copy(nt_ref, nt, sems.at[0]),
        pltpu.make_async_copy(nh_ref, nh, sems.at[1]),
    ]

    @pl.when(pl.program_id(0) == 0)
    def _():
        for copy in copies:
            copy.start()

    def products(own_ref, halo_ref, own, t, sums):
        part = [None] * 9
        for r in range(rows + 2):
            for j in range(3):
                v = row_tile(own_ref, halo_ref, r, t + j).astype(F32)
                for i in range(3):
                    if 0 <= r - i < rows:
                        part[3 * i + j] = added(part[3 * i + j], v * own[r - i])
        return tuple(s + halves(p) for s, p in zip(sums, part))

    def first(own_ref, halo_ref, other_ref, d, t, sums):
        own = []
        for r in range(rows):
            dg = d_ref[0, r, t].astype(F32) * scale + back
            own.append(dg * other_ref[0, r, t].astype(F32))
            d[r, t + 1] = own[r].astype(BF)
        return products(own_ref, halo_ref, own, t, sums)

    nought = (jnp.zeros((STEP // 2, LANES), F32),) * 9
    sums = [
        lax.fori_loop(0, tiles, functools.partial(first, *refs), nought, unroll=4)
        for refs in ((ea_ref, ha_ref, cb_ref, da), (eb_ref, hb_ref, ca_ref, db))
    ]
    for d in (da, db):
        for r in range(rows):
            d[r, 0] = neighbours(d[r, tiles].astype(F32), True).astype(BF)
            d[r, tiles + 1] = neighbours(d[r, 1].astype(F32), False).astype(BF)

    taps_a, taps_b = spread_taps(ka_ref), spread_taps(kb_ref)

    def spread(d, taps, x_ref, t):
        total = [None] * (rows + 2)
        for r in range(rows):
            for j in range(3):
                v = d[r, t + 2 - j].astype(F32)
                for i in range(3):
                    total[r + i] = added(total[r + i], v * taps[3 * i + j])
        for r in range(rows + 2):
            x_ref[0, r, t] = total[r].astype(BF)

    for d, taps, x_ref in ((da, taps_a, xa_ref), (db, taps_b, xb_ref)):

        def second(t, carry, d=d, taps=taps, x_ref=x_ref):
            spread(d, taps, x_ref, t)
            return carry

        lax.fori_loop(0, tiles, second, 0, unroll=4)

    @pl.when(pl.program_id(0) == 0)
    def _():
        for copy in copies:
            copy.wait()

    total = None
    for r in range(rows + 2):
        if r == 0:
            left = nh[:, 0:cols]
        elif r == rows + 1:
            left = nh[:, cols : 2 * cols]
        else:
            left = nt[:, (r - 1) * cols : r * cols]
        right = jnp.concatenate([flat(xa_ref[0, r]), flat(xb_ref[0, r])], -1)
        total = added(total, jnp.dot(left, right, preferred_element_type=F32))
    width = total.shape[0]
    blank = jnp.zeros((7, LANES), F32)
    rows_of = lambda part: [jnp.sum(p, 0, keepdims=True) for p in part]
    small = jnp.concatenate([vec_ref[0], *rows_of(sums[0]), blank, *rows_of(sums[1]), blank], 0)

    def write(ref):
        ref[0, 0:width] = total[:, :LANES].astype(BF)
        ref[0, width : 2 * width] = total[:, LANES:].astype(BF)
        ref[0, 2 * width : 3 * width] = (out_ref[0] * scale_ref[...]).astype(BF)
        ref[0, 3 * width : 3 * width + SMALL] = small.astype(BF)
        ref[0, 3 * width + SMALL :] = jnp.zeros((width // 2 - SMALL, LANES), BF)

    early = pl.program_id(0) < pl.num_programs(0) // 2
    pl.when(early)(lambda: write(send_ref))
    pl.when(jnp.logical_not(early))(lambda: write(keep_ref))


def gradients(
    me, expanded, halo, taps, conv_a, conv_b, d_att, scale, back, out_term, vectors, normed_t, halo_t
):
    chunks, rows, tiles, _, _ = d_att.shape
    width = chunks * LANES
    half = chunks // 2
    chunk = lambda s, me: (s + half * (1 - me[0])) % chunks

    def by_chunk(a, offset=0):
        block = (1,) + tuple(a.shape[1:])
        return pl.BlockSpec(block, lambda s, me: (chunk(s, me) + offset,) + (0,) * (len(block) - 1))

    def by_half(a):
        return [by_chunk(a), by_chunk(a, chunks)]

    def lanes(a, offset=0):
        block = a.shape[:-1] + (LANES,)
        return pl.BlockSpec(
            block, lambda s, me: (0,) * (len(block) - 1) + (chunk(s, me) + offset,)
        )

    spread = jax.ShapeDtypeStruct((chunks, rows + 2, tiles, STEP, LANES), BF)
    part = jax.ShapeDtypeStruct((half, 7 * width // 2, LANES), BF)
    block = (1,) + part.shape[1:]
    return pl.pallas_call(
        gradient_kernel,
        grid_spec=pltpu.PrefetchScalarGridSpec(
            num_scalar_prefetch=1,
            grid=(chunks,),
            in_specs=by_half(expanded)
            + by_half(halo)
            + [lanes(taps), lanes(taps, chunks)]
            + [by_chunk(a) for a in (conv_a, conv_b, d_att)]
            + [lanes(scale), lanes(back), by_chunk(out_term), by_chunk(vectors)]
            + [pl.BlockSpec(memory_space=pl.ANY)] * 2,
            out_specs=[
                by_chunk(spread),
                by_chunk(spread),
                pl.BlockSpec(block, lambda s, me: (jnp.minimum(s, half - 1), 0, 0)),
                pl.BlockSpec(block, lambda s, me: (jnp.maximum(s - half, 0), 0, 0)),
            ],
            scratch_shapes=[pltpu.VMEM((rows, tiles + 2, STEP, LANES), BF)] * 2
            + [pltpu.VMEM(normed_t.shape, BF), pltpu.VMEM(halo_t.shape, BF)]
            + [pltpu.SemaphoreType.DMA((2,))],
        ),
        out_shape=[spread, spread, part, part],
        compiler_params=params(),
        cost_estimate=pl.CostEstimate(
            flops=d_att.size * 3000, bytes_accessed=d_att.size * 20, transcendentals=0
        ),
        name="gradients",
    )(
        me.reshape(1), expanded, expanded, halo, halo, taps, taps, conv_a, conv_b, d_att, scale, back,
        out_term, vectors, normed_t, halo_t,
    )


def back_project(xa_ref, xb_ref, w_ref):
    chunks = [flat(ref[k, 0]) for ref in (xa_ref, xb_ref) for k in range(ref.shape[0])]
    return lax.dot_general(
        jnp.concatenate(chunks, -1),
        w_ref[...],
        (((1,), (1,)), ((), ())),
        preferred_element_type=F32,
    )


def edge_kernel(
    pixels, at_ref, ca_ref, cb_ref, d_ref, sums_ref, att_ref, taps_ref, w_ref,
    first_ref, second_ref, scale_ref, back_ref, vec_ref,
):
    side = (pl.program_id(0) + 1 - at_ref[0]) % 2

    @pl.when(pl.program_id(0) == 0)
    def _():
        sums = jnp.sum(sums_ref[...], 0)
        half = sums.shape[0] // 2
        line = lambda rows: jnp.concatenate([rows[k : k + 1] for k in range(half)], -1)
        eight = lambda row: jnp.broadcast_to(row, (8, row.shape[1]))
        exact = dict(precision=lax.Precision.HIGHEST, preferred_element_type=F32)
        pooled = sums[:half] / pixels
        scale_ref[...] = jnp.dot(eight(line(pooled)), att_ref[...], **exact)[:1]
        back = lax.dot_general(
            eight(line(sums[half:])), att_ref[...], (((1,), (1,)), ((), ())), **exact
        )
        back_ref[...] = back[:1] / pixels
        row = lax.broadcasted_iota(jnp.int32, (8, LANES), 0)
        mine = row == jnp.where(at_ref[2] == 0, at_ref[1], 8)
        for k in range(half):
            for n, v in enumerate((pooled[k : k + 1], sums[half + k : half + k + 1])):
                rows = jnp.where(mine, jnp.broadcast_to(v, (8, LANES)), 0.0)
                vec_ref[k, 8 * n : 8 * n + 8] = rows

    scale, back = scale_ref[...], back_ref[...]
    every = taps_ref[...].astype(F32)
    taps = jnp.where(side == 0, every[0:3], every[6:9])
    chunks = d_ref.shape[0]
    spread = [None] * (2 * chunks)
    for k in range(chunks):
        here = slice(k * LANES, (k + 1) * LANES)
        dg = d_ref[k, 0].astype(F32) * scale[:, here] + back[:, here]
        for n, ref in ((k, cb_ref), (chunks + k, ca_ref)):
            d = dg * ref[k, 0].astype(F32)
            before = neighbours(d[-1], True)[None]
            behind = neighbours(d[0], False)[None]
            windows = (
                jnp.concatenate([d[1:], behind], 0),
                d,
                jnp.concatenate([before, d[:-1]], 0),
            )
            total = None
            for j in range(3):
                tap = taps[j : j + 1, n * LANES : (n + 1) * LANES]
                total = added(total, windows[j] * tap[None])
            spread[n] = flat(total.astype(BF))
    row = lax.dot_general(
        jnp.concatenate(spread, -1),
        w_ref[...],
        (((1,), (1,)), ((), ())),
        preferred_element_type=F32,
    ).astype(BF)

    @pl.when(pl.program_id(0) == 0)
    def _():
        first_ref[...] = row

    @pl.when(pl.program_id(0) == 1)
    def _():
        second_ref[...] = row


def edge_rows(at, conv_a, conv_b, d_att, sums, w_att, taps, w_in, pixels):
    chunks, rows, tiles, _, _ = d_att.shape
    side = lambda e, at: (e + 1 - at[0]) % 2
    spec = pl.BlockSpec(
        (chunks, 1, tiles, STEP, LANES), lambda e, at: (0, side(e, at) * (rows - 1), 0, 0, 0)
    )
    out = jax.ShapeDtypeStruct((tiles * STEP, w_in.shape[0]), BF)
    line = jax.ShapeDtypeStruct((1, chunks * LANES), F32)
    outs = [out, out, line, line, jax.ShapeDtypeStruct((chunks, 16, LANES), F32)]
    full = lambda a: pl.BlockSpec(a.shape, lambda e, at: (0,) * a.ndim)
    return pl.pallas_call(
        functools.partial(edge_kernel, pixels),
        grid_spec=pltpu.PrefetchScalarGridSpec(
            num_scalar_prefetch=1,
            grid=(2,),
            in_specs=[spec, spec, spec] + [full(a) for a in (sums, w_att, taps, w_in)],
            out_specs=[full(a) for a in outs],
        ),
        out_shape=outs,
        compiler_params=params(),
        name="edge_rows",
    )(at, conv_a, conv_b, d_att, sums, w_att, taps, w_in)


def input_kernel(
    odd_ref, x_ref, cot_ref, xa_ref, xb_ref, first_ref, second_ref, gain_ref, w_ref, order_ref, out_ref
):
    row = pl.program_id(0)
    last = pl.num_programs(0) - 1
    d_norm = back_project(xa_ref, xb_ref, w_ref)
    odd = odd_ref[0] == 1
    above, below = row == 0, row == last
    early = (above & odd) | (below & jnp.logical_not(odd))
    late = (above & jnp.logical_not(odd)) | (below & odd)
    d_norm = d_norm + jnp.where(early, 1.0, 0.0) * first_ref[...].astype(F32)
    d_norm = d_norm + jnp.where(late, 1.0, 0.0) * second_ref[...].astype(F32)
    d_norm = lax.dot_general(
        order_ref[...], d_norm.astype(BF), (((0,), (0,)), ((), ())), preferred_element_type=F32
    )
    xhat, rstd = layer_norm(x_ref[0])
    dxhat = d_norm * gain_ref[...]
    grad = cot_ref[0].astype(F32) + rstd * (
        dxhat - jnp.mean(dxhat, -1, keepdims=True) - xhat * jnp.mean(dxhat * xhat, -1, keepdims=True)
    )
    out_ref[0, 0] = grad.astype(BF)


def input_grad(odd, x, cot, xa, xb, first, second, gain, w_in, order):
    rows, cols, width = x.shape
    chunks = xa.shape[0]
    spec = pl.BlockSpec((1, cols, width), lambda r: (r, 0, 0))
    inner = pl.BlockSpec(
        (chunks, 1, cols // STEP, STEP, LANES), lambda r: (0, r + 1, 0, 0, 0)
    )
    return pl.pallas_call(
        input_kernel,
        grid=(rows,),
        in_specs=[pl.BlockSpec(memory_space=pltpu.SMEM), spec, spec, inner, inner]
        + [whole(a) for a in (first, second, gain, w_in, order)],
        out_specs=pl.BlockSpec((1, 1, cols, width), lambda r: (0, r, 0, 0)),
        out_shape=jax.ShapeDtypeStruct((1, rows, cols, width), BF),
        compiler_params=params(),
        cost_estimate=pl.CostEstimate(
            flops=2 * rows * cols * width * width * 6,
            bytes_accessed=rows * cols * width * 10,
            transcendentals=0,
        ),
        name="input_grad",
    )(odd.reshape(1), x, cot, xa, xb, first, second, gain, w_in, order)


def unpack_kernel(factor, me_ref, own_ref, other_ref, in_ref, out_ref, att_ref, taps_ref):
    step = pl.program_id(0)
    first = me_ref[0] == 0
    half = own_ref.shape[0]
    chunks = 2 * half
    width = chunks * LANES

    def rows(k, start, count):
        own = own_ref[k % half, pl.ds(start, count)].astype(F32)
        other = other_ref[k % half, pl.ds(start, count)].astype(F32)
        return jnp.where(first, own, other) if k < half else jnp.where(first, other, own)

    start = pl.multiple_of(step * LANES, LANES)
    for k in range(chunks):
        here = slice(k * LANES, (k + 1) * LANES)
        in_ref[:, here] = rows(k, start, LANES) * factor
        in_ref[:, width + k * LANES : width + (k + 1) * LANES] = (
            rows(k, start + width, LANES) * factor
        )
        out_ref[here, pl.ds(start, LANES)] = rows(k, start + 2 * width, LANES).T * factor

    @pl.when(step == 0)
    def _():
        small = [rows(k, 3 * width, SMALL) for k in range(chunks)]
        for k in range(chunks):
            here = slice(k * LANES, (k + 1) * LANES)
            taps_ref[:, here] = small[k][16:25] * factor
            taps_ref[:, width + k * LANES : width + (k + 1) * LANES] = small[k][32:41] * factor
            for m in range(chunks):
                block = lax.dot_general(
                    small[k][0:8].astype(BF),
                    small[m][8:16].astype(BF),
                    (((0,), (0,)), ((), ())),
                    preferred_element_type=F32,
                )
                att_ref[here, m * LANES : (m + 1) * LANES] = block * factor


def unpack(own, other, me, hidden, width, factor):
    full = jax.ShapeDtypeStruct((width, width), F32)
    return pl.pallas_call(
        functools.partial(unpack_kernel, factor),
        grid=(width // LANES,),
        in_specs=[pl.BlockSpec(memory_space=pltpu.SMEM), whole(own), whole(other)],
        out_specs=[
            pl.BlockSpec((LANES, hidden), lambda s: (s, 0)),
            whole(full),
            whole(full),
            pl.BlockSpec((9, hidden), lambda s: (0, 0)),
        ],
        out_shape=[
            jax.ShapeDtypeStruct((width, hidden), F32),
            full,
            full,
            jax.ShapeDtypeStruct((9, hidden), F32),
        ],
        compiler_params=params(vmem=16 * 1024 * 1024),
        name="unpack",
    )(me.reshape(1), own, other)


def exchange_pairs(first, second):
    count = lax.axis_size(SPACE)
    inner = [(i, i ^ 1) for i in range(count)]
    outer_pairs = [(i, i + 1) for i in range(1, count - 1, 2)]
    crossing = outer_pairs + [(t, s) for s, t in outer_pairs]
    return lax.ppermute(first, SPACE, inner), lax.ppermute(second, SPACE, crossing)


SPACE = ("x", "zh", "y")
CHIPS = ("zl", "x", "zh", "y")
SWAP = [(0, 1), (1, 0)]


def from_space(v):
    n = lax.axis_size(SPACE)
    copies = lax.optimization_barrier(jnp.broadcast_to(v[None], (n,) + v.shape))
    return lax.all_to_all(copies, SPACE, 0, 0, tiled=True)


def sum_over_all(send, keep, later):
    n = lax.axis_size(CHIPS)
    other = lax.ppermute(send, "co", SWAP)
    own = (keep.astype(F32) + other.astype(F32)).astype(BF)
    own = lax.optimization_barrier(own.reshape(n, -1, LANES))
    parts = lax.all_to_all(own, CHIPS, 0, 0, tiled=True)
    part = jnp.sum(parts.astype(F32), 0).astype(BF)
    part, later = lax.optimization_barrier((part, later))
    copies = lax.optimization_barrier(jnp.broadcast_to(part[None], parts.shape))
    own = lax.all_to_all(copies, CHIPS, 0, 0, tiled=True)
    return own.reshape(keep.shape), later


def local(frames, cotangent, gain, w_in, kernel, w_att, w_out):
    x = frames[0]
    cot = cotangent[0]
    rows, cols, width = x.shape
    hidden = w_in.shape[1]
    space = lax.axis_size("x") * lax.axis_size("zh") * lax.axis_size("y")
    place = (lax.axis_index("x") * lax.axis_size("zh") + lax.axis_index("zh")) * lax.axis_size(
        "y"
    ) + lax.axis_index("y")
    frame_count = lax.axis_size("zl") * lax.axis_size("co")
    frame = lax.axis_index("zl") * lax.axis_size("co") + lax.axis_index("co")
    pixels = rows * space * cols
    factor = 1.0 / math.sqrt(frame_count * pixels)
    gain = gain[None]
    order = place_matrix(cols)

    odd = place % 2
    edge_row = lambda r: lax.dynamic_slice_in_dim(x, r, 1, 0)
    first, second = exchange_pairs(
        edge_row((1 - odd) * (rows - 1)), edge_row(odd * (rows - 1))
    )
    taps = jnp.broadcast_to(kernel[:, None], (9, STEP, hidden))
    gain, taps = lax.optimization_barrier((gain, taps))
    normed_t, expanded, cot_t, d_att = enter(x, gain, w_in, order, cot, w_out)
    halo_t, halo = enter_halo(odd, first, second, gain, w_in, order)
    conv_a, conv_b, sums = convolution(expanded, halo, taps, d_att)
    sums = from_space(sums)
    out_term = outer(cot_t, conv_a, conv_b)
    sums, out_term = lax.optimization_barrier((sums, out_term))
    first, second, scale, back, vectors = edge_rows(
        jnp.stack([odd, frame, place]), conv_a, conv_b, d_att, sums, w_att, kernel, w_in, pixels
    )
    first, second = exchange_pairs(first, second)
    me = lax.axis_index("co")
    d_exp_a, d_exp_b, send, keep = gradients(
        me, expanded, halo, taps, conv_a, conv_b, d_att, scale, back, out_term, vectors,
        normed_t, halo_t,
    )
    send, first, second = lax.optimization_barrier((send, first, second))
    own, (first, second) = sum_over_all(send, keep, (first, second))
    grad = input_grad(odd, x, cot, d_exp_a, d_exp_b, first, second, gain, w_in, order)
    own, grad = lax.optimization_barrier((own, grad))
    other = lax.ppermute(own, "co", SWAP)
    in_sum, out_sum, att_sum, kernel_sum = unpack(
        own, other, me, hidden, width, factor
    )
    return grad, in_sum, kernel_sum, att_sum, out_sum


def solution(mesh):
    fine = Mesh(mesh.devices.reshape(2, 2, 4, 2, 4), ("zl", "co", "x", "zh", "y"))
    big = P(("zl", "co"), ("x", "zh", "y"), None, None)
    return jax.shard_map(
        local,
        mesh=fine,
        in_specs=(big, big, P(), P(), P(), P(), P()),
        out_specs=(big, P(), P(), P(), P()),
        check_vma=False,
    )
```
